32 devices in a mesh: dp: 8 (over y, x, core), seq: 4 (over z).
Axes of the slice: x: 2, y: 2, z: 4, core: 2. Of those that a mesh axis runs over, the one named last changes fastest.
Arguments:
- patches: bfloat16 [96, 576, 384], P('dp', 'seq'), may hold values from -6 to 6
- first_gain: bfloat16 [384], replicated, may hold values from 0.5 to 1.5
- first_shift: bfloat16 [384], replicated, may hold values from -1.25 to 1.25
- qkv_weight: bfloat16 [384, 1152], replicated, may hold values from -0.3125 to 0.3125
- query_value_bias: bfloat16 [768], replicated, may hold values from -1.75 to 1.75
- out_weight: bfloat16 [384, 384], replicated, may hold values from -2.5 to 2.5
- out_bias: bfloat16 [384], replicated, may hold values from -1.25 to 1.25
- second_gain: bfloat16 [384], replicated, may hold values from 0.5 to 1.5
- second_shift: bfloat16 [384], replicated, may hold values from -1.25 to 1.25
- up_weight: bfloat16 [384, 1536], replicated, may hold values from -0.3125 to 0.3125
- up_bias: bfloat16 [1536], replicated, may hold values from -1.75 to 1.75
- down_weight: bfloat16 [1536, 384], replicated, may hold values from -0.15625 to 0.15625
- down_bias: bfloat16 [384], replicated, may hold values from -1.25 to 1.25
- map_weight: bfloat16 [384, 8], replicated, may hold values from -0.3125 to 0.3125
- map_bias: bfloat16 [8], replicated, may hold values from -3 to 3
- keep_mask: int32 [96, 576], P('dp', 'seq'), may hold values from 0 to 1, as said below
- image_valid: int32 [96], P('dp'), may hold values from 0 to 1, as said below
- token_cotangent: bfloat16 [96, 8, 384], P('dp'), may hold values from -448 to 448
Outputs:
- learned: float32 [96, 8, 384], P('dp')
- penalty: float32 [], replicated
- grad_patches: float32 [96, 576, 384], P('dp', 'seq')
- grad_first_gain: float32 [384], replicated
- grad_first_shift: float32 [384], replicated
- grad_qkv_weight: float32 [384, 1152], replicated
- grad_query_value_bias: float32 [768], replicated
- grad_out_weight: float32 [384, 384], replicated
- grad_out_bias: float32 [384], replicated
- grad_second_gain: float32 [384], replicated
- grad_second_shift: float32 [384], replicated
- grad_up_weight: float32 [384, 1536], replicated
- grad_up_bias: float32 [1536], replicated
- grad_down_weight: float32 [1536, 384], replicated
- grad_down_bias: float32 [384], replicated
- grad_map_weight: float32 [384, 8], replicated
- grad_map_bias: float32 [8], replicated
The draws below stay inside these ranges and needn't reach their ends.
Inputs may be any that keep to these rules, and one draw needn't show every extreme that they name: `keep_mask`: patch 0 of every image is kept. `image_valid`: the last image is valid.
All inputs are finite; a program needn't handle non-finite values.
Results may differ from the reference program's by a relative error of at most 0.0049.
Values may be sent and summed in bfloat16 or wider, within the bound.
No kernel may reach another device: no remote copies, remote signals or barrier semaphores. Data moves between devices by JAX's collectives and lax.ppermute only.
A program may use at most 256 MiB of HBM per device.

```python
import jax
import jax.numpy as jnp
from jax import lax

D = 384
HEADS = 6
HD = 64
FF = 1536
S_TOK = 8
IMAGES = 96
PATCHES = 576


def draw_keep_mask(key, part):
    patch_key = jax.random.fold_in(key, 11)
    image_order = jnp.arange(IMAGES, dtype=jnp.int32)[:, None]
    keep_rates = 300 + 700 * image_order // max(IMAGES - 1, 1)
    positions = jnp.arange(PATCHES, dtype=jnp.int32)[None, :]
    limits = keep_rates * (200 + 800 * positions // (PATCHES - 1)) // 1000
    random_rolls = jax.random.randint(patch_key, (IMAGES, PATCHES), 0, 1000)
    kept_flags = (random_rolls < limits).astype(jnp.int32)
    return jnp.where(positions == 0, 1, kept_flags).astype(jnp.int32)


def draw_image_valid(key, part):
    image_order = jnp.arange(IMAGES, dtype=jnp.int32)
    limits = 300 + 600 * image_order // (IMAGES - 1)
    random_rolls = jax.random.randint(jax.random.fold_in(key, 23), (IMAGES,), 0, 1000)
    valid_flags = (random_rolls < limits).astype(jnp.int32)
    return jnp.where(image_order == IMAGES - 1, 1, valid_flags).astype(jnp.int32)


def shard_levels(own_key, extent, cuts, low, top_value):
    def one(dim, shards_of):
        steps = jax.random.uniform(jax.random.fold_in(jax.random.fold_in(own_key, 6), dim), (shards_of,), jnp.float32, low / len(cuts), top_value / len(cuts))
        return jnp.repeat(jnp.exp(steps), extent[dim] // shards_of).reshape((-1,) + (1,) * (len(extent) - dim - 1))

    gain = one(*cuts[0])
    for cut in cuts[1:]:
        gain = gain * one(*cut)
    return gain


def gaussian(own_key, shape, spread, limit, cuts=(), kind=jnp.bfloat16):
    result = jax.random.normal(own_key, shape, jnp.float32) * spread
    if len(cuts) > 0:
        result = shard_levels(own_key, shape, cuts, -0.22, 0.18) * result
    return jnp.clip(result, min=-limit, max=limit).astype(kind)


def setup_inputs(seed: int = 0) -> dict:
    key_of = jax.random.split(jax.random.key(seed), 19)
    patches = gaussian(key_of[0], (IMAGES, PATCHES, D), 1.0, 6.0, ((0, 8), (1, 4)))
    first_gain = jnp.clip(1.0 + 0.1 * jax.random.normal(key_of[1], (D,), jnp.float32), 0.5, 1.5).astype(jnp.bfloat16)
    first_shift = gaussian(key_of[2], (D,), 0.2, 1.25)
    qkv_weight = gaussian(key_of[3], (D, 3 * D), D ** -0.5, 0.3125)
    query_value_bias = gaussian(key_of[4], (2 * D,), 0.3, 1.75)
    out_weight = gaussian(key_of[5], (D, D), (D // 64) ** -0.5, 2.5)
    out_bias = gaussian(key_of[6], (D,), 0.2, 1.25)
    second_gain = jnp.clip(1.0 + 0.1 * jax.random.normal(key_of[7], (D,), jnp.float32), 0.5, 1.5).astype(jnp.bfloat16)
    second_shift = gaussian(key_of[8], (D,), 0.2, 1.25)
    up_weight = gaussian(key_of[9], (D, FF), D ** -0.5, 0.3125)
    up_bias = gaussian(key_of[10], (FF,), 0.3, 1.75)
    down_weight = gaussian(key_of[11], (FF, D), FF ** -0.5, 0.15625)
    down_bias = gaussian(key_of[12], (D,), 0.2, 1.25)
    map_weight = gaussian(key_of[13], (D, S_TOK), D ** -0.5, 0.3125)
    map_bias = gaussian(key_of[14], (S_TOK,), 0.5, 3.0)
    keep_mask = draw_keep_mask(jax.random.fold_in(key_of[18], 71), 0)
    image_valid = draw_image_valid(jax.random.fold_in(key_of[18], 71), 0)
    token_cotangent = gaussian(key_of[17], (IMAGES, S_TOK, D), (PATCHES / 8), 448.0, ((0, 8),))
    return dict(patches=patches, first_gain=first_gain, first_shift=first_shift, qkv_weight=qkv_weight, query_value_bias=query_value_bias, out_weight=out_weight, out_bias=out_bias, second_gain=second_gain, second_shift=second_shift, up_weight=up_weight, up_bias=up_bias, down_weight=down_weight, down_bias=down_bias, map_weight=map_weight, map_bias=map_bias, keep_mask=keep_mask, image_valid=image_valid, token_cotangent=token_cotangent)


PRECISE = lax.Precision.HIGHEST
EPSILON = 1e-06
MASKED_SCORE = -1e+30

@jax.custom_vjp
def low(v):
    return lax.optimization_barrier(v.astype(jnp.bfloat16)).astype(jnp.float32)

@jax.custom_vjp
def low_back(v):
    return v

def low_keep(v):
    return (low(v), None)

def low_pass(kept, grad):
    return (grad,)

def back_keep(v):
    return (v, None)

def back_low(kept, grad):
    return (low(grad),)
low.defvjp(low_keep, low_pass)
low_back.defvjp(back_keep, back_low)

def layer_norm(values, scale_vec, shift_vec):
    average = lax.optimization_barrier(jnp.mean(values, axis=-1, keepdims=True))
    centred = values - average
    variance = lax.optimization_barrier(jnp.mean(centred * centred, axis=-1, keepdims=True))
    return centred * lax.rsqrt(variance + EPSILON) * scale_vec + shift_vec

def exact_gelu(values):
    return jax.nn.gelu(values, approximate=False)

def group_forward(params, patch_rows, keep_rows, valid_rows):
    first_gain, first_shift, qkv_weight, query_value_bias, out_weight, out_bias, second_gain, second_shift, up_weight, up_bias, down_weight, down_bias, map_weight, map_bias = params
    group_count, length, features = patch_rows.shape
    normed = low(layer_norm(patch_rows, first_gain, first_shift))
    mixed_rows = low_back(jnp.einsum('gpd,de->gpe', normed, qkv_weight, precision=PRECISE))
    queries = low(mixed_rows[..., :features] + query_value_bias[:features])
    keys_low = low(mixed_rows[..., features:2 * features])
    values = low(mixed_rows[..., 2 * features:] + query_value_bias[features:])
    queries = queries.reshape(group_count, length, HEADS, HD)
    keys_low = keys_low.reshape(group_count, length, HEADS, HD)
    values = values.reshape(group_count, length, HEADS, HD)
    product = low_back(jnp.einsum('gqhe,gkhe->ghqk', queries, keys_low, precision=PRECISE))
    scores = product * HD ** (-0.5)
    scores = jnp.where(keep_rows[:, None, None, :] > 0, scores, MASKED_SCORE)
    row_max = lax.optimization_barrier(jnp.max(scores, axis=-1, keepdims=True))
    exponent = jnp.exp(scores - row_max)
    probabilities = exponent / lax.optimization_barrier(jnp.sum(exponent, axis=-1, keepdims=True))
    attended = jnp.einsum('ghqk,gkhe->gqhe', low(probabilities), values, precision=PRECISE)
    attended = low(low_back(attended.reshape(group_count, length, features)))
    branch = low_back(jnp.einsum('gpe,ed->gpd', attended, out_weight, precision=PRECISE)) + out_bias
    middle = patch_rows + branch
    second_normed = low(layer_norm(middle, second_gain, second_shift))
    hidden_pre = low_back(jnp.einsum('gpd,df->gpf', second_normed, up_weight, precision=PRECISE)) + up_bias
    hidden = low(low_back(exact_gelu(hidden_pre)))
    output = middle + low_back(jnp.einsum('gpf,fd->gpd', hidden, down_weight, precision=PRECISE)) + down_bias
    logits = jnp.einsum('gpd,ds->gps', output, map_weight, precision=PRECISE) + map_bias
    token_maps = jax.nn.sigmoid(logits)
    kept_float = keep_rows.astype(jnp.float32)
    weighted = token_maps * kept_float[..., None]
    token_sums = jnp.einsum('gps,gpd->gsd', weighted, output, precision=PRECISE)
    counts = lax.optimization_barrier(jnp.sum(kept_float, axis=1))
    learned = token_sums / counts[:, None, None]
    map_total = lax.optimization_barrier(jnp.sum(token_maps, axis=-1))
    intersection = lax.optimization_barrier(jnp.sum(kept_float * (map_total * map_total - lax.optimization_barrier(jnp.sum(token_maps * token_maps, axis=-1))), axis=1))
    penalty_share = jnp.sum(valid_rows * intersection) / PATCHES
    return (learned, penalty_share)

def reference(patches, first_gain, first_shift, qkv_weight, query_value_bias, out_weight, out_bias, second_gain, second_shift, up_weight, up_bias, down_weight, down_bias, map_weight, map_bias, keep_mask, image_valid, token_cotangent):
    params = tuple((tensor.astype(jnp.float32) for tensor in (first_gain, first_shift, qkv_weight, query_value_bias, out_weight, out_bias, second_gain, second_shift, up_weight, up_bias, down_weight, down_bias, map_weight, map_bias)))
    inputs = patches.astype(jnp.float32)
    valid_float = image_valid.astype(jnp.float32)
    valid_count = jnp.sum(valid_float)
    group_size = 4
    blocked_keep = keep_mask.reshape(IMAGES // group_size, group_size, PATCHES)
    blocked_valid = valid_float.reshape(IMAGES // group_size, group_size)
    checked = jax.checkpoint(group_forward)

    def forward(weights_all, input_rows):
        blocked_rows = input_rows.reshape(IMAGES // group_size, group_size, PATCHES, D)

        def step(carry, pieces):
            learned_part, share = checked(weights_all, pieces[0], pieces[1], pieces[2])
            return (carry + share, learned_part)
        total_share, learned_all = lax.scan(step, jnp.zeros((), jnp.float32), (blocked_rows, blocked_keep, blocked_valid))
        return (learned_all.reshape(IMAGES, S_TOK, D), total_share / valid_count)
    (learned, penalty), back_fn = jax.vjp(forward, params, inputs)
    penalty_weight = jnp.full((), PATCHES, jnp.float32)
    param_grads, grad_patches = back_fn((token_cotangent.astype(jnp.float32), penalty_weight))
    return (learned, penalty, grad_patches) + tuple(param_grads)
```

```python
import jax
import jax.numpy as jnp
from jax import lax
from jax.experimental import pallas as pl
from jax.experimental.pallas import tpu as pltpu
from jax.sharding import PartitionSpec as P

f32, bf = jnp.float32, jnp.bfloat16
EPSILON = 1e-6
MASKED = -1e30
MIB = 1 << 20


def mm(a, b):
    return lax.dot_general(a, b, (((1,), (0,)), ((), ())), preferred_element_type=f32)


def mm_nt(a, b):
    return lax.dot_general(a, b, (((1,), (1,)), ((), ())), preferred_element_type=f32)


def mm_tn(a, b):
    return lax.dot_general(a, b, (((0,), (0,)), ((), ())), preferred_element_type=f32)


def row_mean(x):
    return jnp.sum(x, axis=-1, keepdims=True) * (1.0 / x.shape[-1])


def normalise(x):
    centred = x - row_mean(x)
    r = lax.rsqrt(row_mean(centred * centred) + EPSILON)
    return centred * r, r


def normal_parts(v):
    expo = jnp.exp(v * v * (-0.5))
    t = 1.0 / (1.0 + jnp.abs(v) * (0.3275911 * 0.7071067811865476))
    series = t * (0.127414796 + t * (-0.142248368 + t * (0.7107068705 + t * (-0.7265760135 + t * 0.5307027145))))
    tail = series * expo
    return jnp.where(v >= 0, 1.0 - tail, tail), expo * 0.3989422804014327


def split2(a):
    high = a.astype(bf)
    return high, (a - high.astype(f32)).astype(bf)


def attend_kernel(parts, rows, slot, *refs):
    x_refs, flag_refs = refs[:parts], refs[parts:2 * parts]
    vec_ref, wqkv, wout = refs[2 * parts:2 * parts + 3]
    qa_ref, k_ref, v_ref, caug_ref, att_ref, mid_ref = refs[2 * parts + 3:2 * parts + 9]
    nrm_s, q_s = refs[2 * parts + 9:]
    n, width = nrm_s.shape
    vec = lambda i: vec_ref[i:i + 1, :]
    r8 = lax.broadcasted_iota(jnp.int32, (8, 128), 0)
    l8 = lax.broadcasted_iota(jnp.int32, (8, 128), 1) & 63
    place = ((r8 == 0) & (l8 == 3)) | ((r8 == 1) & (l8 < 3)) | ((r8 == 2) & (l8 == 4))
    place = jnp.where(place, 1.0, 0.0).astype(bf)
    row = lax.broadcasted_iota(jnp.int32, (8, rows), 0)
    for i in range(parts):
        rs = slice(i * rows, (i + 1) * rows)
        xh, _ = normalise(x_refs[i][0:rows, :].astype(f32))
        nrm_s[rs, :] = (xh * vec(0) + vec(1)).astype(bf)
        keep = flag_refs[i][rows:rows + 16, 0:rows].astype(f32)[slot:slot + 1, :]
        marks = jnp.where(row == 0, (1.0 - keep) * MASKED, jnp.where(row == 1, 1.0, jnp.where(row == 2, keep, 0.0)))
        caug_ref[rs, :] = mm_tn(marks.astype(bf), place).astype(bf)
    nrm = nrm_s[...]
    q_s[...] = (mm(nrm, wqkv[:, 0:width]) + vec(2)).astype(bf) * jnp.asarray(0.125, bf)
    k_ref[...] = mm(nrm, wqkv[:, width:2 * width]).astype(bf)
    v_ref[...] = (mm(nrm, wqkv[:, 2 * width:3 * width]) + vec(3)).astype(bf)
    lane = lax.broadcasted_iota(jnp.int32, (n, 128), 1)
    lane64 = lane & 63
    ones = jnp.ones((n, 128), bf)
    for j in range(width // 128):
        sl = slice(128 * j, 128 * j + 128)
        outs = []
        for e in range(2):
            own = (lane < 64) if e == 0 else (lane >= 64)
            kp = jnp.where(own, k_ref[:, sl], caug_ref[...])
            qp = jnp.where(own, q_s[:, sl], jnp.where(lane64 == 3, 1.0, 0.0).astype(bf))
            s = mm_nt(qp, kp)
            m = jnp.max(s, axis=-1, keepdims=True)
            p = jnp.exp(s - m).astype(bf)
            o = mm(p, jnp.concatenate([v_ref[:, sl], ones], axis=1))
            total = o[:, 128:256]
            outs.append(o[:, 0:128] / total)
            logs = -(m + jnp.log(total))
            hi = logs.astype(bf).astype(f32)
            lo = (logs - hi).astype(bf).astype(f32)
            aug = jnp.where(lane64 == 0, hi, jnp.where(lane64 == 1, lo, jnp.where(lane64 == 2, logs - hi - lo, jnp.where(lane64 == 3, 1.0, 0.0))))
            h = 2 * j + e
            qa_ref[:, 128 * h:128 * h + 128] = jnp.where(own, q_s[:, sl], aug.astype(bf))
        att_ref[:, sl] = jnp.where(lane < 64, outs[0], outs[1]).astype(bf)
    pr = mm(att_ref[...], wout[...])
    for i in range(parts):
        rs = slice(i * rows, (i + 1) * rows)
        mid_ref[rs, :] = x_refs[i][0:rows, :].astype(f32) + pr[rs, :] + vec(4)


def attend_call(pieces, flags, slot, rows, vec, wqkv, wout):
    parts, width = len(pieces), wout.shape[0]
    n = parts * rows
    vm = pl.BlockSpec(memory_space=pltpu.VMEM)
    outs = [((n, 2 * width), bf), ((n, width), bf), ((n, width), bf), ((n, 128), bf), ((n, width), bf), ((n, width), f32)]
    return pl.pallas_call(
        lambda *refs: attend_kernel(parts, rows, slot, *refs),
        out_shape=[jax.ShapeDtypeStruct(s, d) for s, d in outs],
        in_specs=[vm] * (2 * parts + 3), out_specs=[vm] * 6,
        scratch_shapes=[pltpu.VMEM((n, width), bf), pltpu.VMEM((n, width), bf)],
        compiler_params=pltpu.CompilerParams(vmem_limit_bytes=VM_A * MIB),
        cost_estimate=pl.CostEstimate(flops=7_000_000_000, bytes_accessed=1_000_000, transcendentals=2_000_000),
        name="attend",
    )(*pieces, *flags, vec, wqkv, wout)


def feed_kernel(slot, own_count, first, *refs):
    mid_ref, att_ref, caug_ref, vec_ref, mb_ref, mapw_ref, cot_ref, valid_ref, count_ref, wout, wup, wdn = refs[:12]
    refs = refs[12:]
    if first:
        acc_in = sm_in = None
    else:
        acc_in, sm_in = refs[:2]
        refs = refs[2:]
    gm_ref, doa_ref, learn_ref, acc, sm = refs[:5]
    sec_s, hid_s, gp_s, g_s = refs[5:]
    n, width = mid_ref.shape
    blocks = hid_s.shape[1] // width
    tokens = mapw_ref.shape[0]
    vec = lambda i: vec_ref[i:i + 1, :]
    place = lax.axis_index("seq") * own_count + slot

    def add(ref, ref_in, rows, value):
        ref[rows, :] = value if first else ref_in[rows, :] + value

    xh, _ = normalise(mid_ref[...])
    sec_s[...] = (xh * vec(5) + vec(6)).astype(bf)
    total = None
    for j in range(blocks):
        js = slice(width * j, width * (j + 1))
        pre = mm(sec_s[...], wup[:, js]) + vec(8 + j)
        upper, density = normal_parts(pre)
        hid_s[:, js] = (pre * upper).astype(bf)
        gp_s[:, js] = upper + pre * density
        t = mm(hid_s[:, js], wdn[js, :])
        total = t if total is None else total + t
    out = mid_ref[...] + total + vec(7)
    ohi, olo = split2(out)
    cm = jnp.concatenate([mapw_ref[...].astype(f32), cot_ref[place].astype(f32)], axis=0).astype(bf)
    lg = mm_nt(cm, ohi) + mm_nt(cm, olo)
    pick = jnp.where(lax.broadcasted_iota(jnp.int32, (8, 128), 1) == 4, 1.0, 0.0).astype(bf)
    keep = mm_nt(pick, caug_ref[...])[0:1, :]
    maps = jax.nn.sigmoid(lg[0:tokens, :] + mb_ref[:, 0:1])
    inverse = 1.0 / jnp.sum(keep, axis=-1, keepdims=True)
    tot = jnp.sum(maps, axis=0, keepdims=True)
    inter = jnp.sum(keep * (tot * tot - jnp.sum(maps * maps, axis=0, keepdims=True)), axis=-1, keepdims=True)
    valid = valid_ref[place].astype(f32)
    gmaps = keep * (lg[tokens:2 * tokens, :] * inverse + (2.0 * valid / count_ref[0:1, 0:1]) * (tot - maps))
    gl = gmaps * maps * (1.0 - maps)
    mk = maps * keep
    mkh, mkl = split2(mk)
    glh, gll = split2(gl)
    st = jnp.concatenate([mkh.astype(f32), mkl.astype(f32), glh.astype(f32), gll.astype(f32)], axis=0).astype(bf)
    r1 = mm(st, ohi) + mm(st, olo)
    learn_ref[...] = (r1[0:tokens, :] + r1[tokens:2 * tokens, :]) * inverse
    add(sm, sm_in, slice(8, 16), r1[2 * tokens:3 * tokens, :] + r1[3 * tokens:, :])
    gah, gal = split2(mk * inverse)
    lhs = jnp.concatenate([glh.astype(f32), gah.astype(f32), gll.astype(f32), gal.astype(f32)], axis=0).astype(bf)
    g = mm_tn(lhs, jnp.concatenate([cm, cm], axis=0))
    g_s[...] = g
    add(sm, sm_in, slice(0, 1), jnp.sum(g, axis=0, keepdims=True))
    glow = g.astype(bf)
    g_t = glow.T
    sec_t = sec_s[...].T
    gsec = None
    for j in range(blocks):
        js = slice(width * j, width * (j + 1))
        gh = mm_nt(glow, wdn[js, :]).astype(bf).astype(f32)
        gpre = gh * gp_s[:, js]
        gpl = gpre.astype(bf)
        add(sm, sm_in, slice(4 + j, 5 + j), jnp.sum(gpre, axis=0, keepdims=True))
        t = mm_nt(gpl, wup[:, js])
        gsec = t if gsec is None else gsec + t
        add(acc, acc_in, js, mm(g_t, hid_s[:, js]))
        add(acc, acc_in, slice(width * (blocks + j), width * (blocks + j + 1)), mm(sec_t, gpl))
    xh, r = normalise(mid_ref[...])
    gg = gsec * vec(5)
    gm = g_s[...] + r * (gg - row_mean(gg) - xh * row_mean(gg * xh))
    gm_ref[...] = gm
    gml = gm.astype(bf)
    add(sm, sm_in, slice(1, 2), jnp.sum(gm, axis=0, keepdims=True))
    add(sm, sm_in, slice(2, 3), jnp.sum(gsec * xh, axis=0, keepdims=True))
    add(sm, sm_in, slice(3, 4), jnp.sum(gsec, axis=0, keepdims=True))
    glb = jnp.sum(gl, axis=-1, keepdims=True)
    lr = lax.broadcasted_iota(jnp.int32, (8, width), 1)
    rr = lax.broadcasted_iota(jnp.int32, (8, width), 0)
    add(sm, sm_in, slice(16, 24), jnp.where(lr == 0, glb, jnp.where((lr == 1) & (rr == 0), valid * inter * (1.0 / n), 0.0)))
    used = width * (2 * blocks + 1)
    add(acc, acc_in, slice(2 * blocks * width, used), mm(att_ref[...].T, gml))
    if first and acc.shape[0] > used:
        acc[used:, :] = jnp.zeros((acc.shape[0] - used, width), f32)
    do = mm_nt(gml, wout[...]).astype(bf).astype(f32)
    lane = lax.broadcasted_iota(jnp.int32, (n, 128), 1)
    lane64 = lane & 63
    for j in range(width // 128):
        sl = slice(128 * j, 128 * j + 128)
        dj = do[:, sl]
        pd = dj * att_ref[:, sl].astype(f32)
        for e in range(2):
            own = (lane < 64) if e == 0 else (lane >= 64)
            dl = -jnp.sum(jnp.where(own, pd, 0.0), axis=-1, keepdims=True)
            hi = dl.astype(bf).astype(f32)
            aug = jnp.where(lane64 == 0, hi, jnp.where(lane64 == 1, dl - hi, 0.0))
            h = 2 * j + e
            doa_ref[:, 128 * h:128 * h + 128] = jnp.where(own, dj, aug).astype(bf)


def feed_call(slot, own_count, packed_rows, mid, att, caug, vec, mb, mapw, cot, valid, count, wout, wup, wdn, acc, sm):
    n, width = mid.shape
    hidden = wup.shape[1]
    first = acc is None
    vm = pl.BlockSpec(memory_space=pltpu.VMEM)
    smem = pl.BlockSpec(memory_space=pltpu.SMEM)
    outs = [((n, width), f32), ((n, 2 * width), bf), ((8, width), f32), ((packed_rows, width), f32), ((24, width), f32)]
    args = (mid, att, caug, vec, mb, mapw, cot, valid, count, wout, wup, wdn)
    extra = () if first else (acc, sm)
    return pl.pallas_call(
        lambda *refs: feed_kernel(slot, own_count, first, *refs),
        out_shape=[jax.ShapeDtypeStruct(s, d) for s, d in outs],
        in_specs=[vm] * 7 + [smem] + [vm] * (4 + len(extra)), out_specs=[vm] * 5,
        input_output_aliases={} if first else {12: 3, 13: 4},
        scratch_shapes=[pltpu.VMEM((n, width), bf), pltpu.VMEM((n, hidden), bf), pltpu.VMEM((n, hidden), f32), pltpu.VMEM((n, width), f32)],
        compiler_params=pltpu.CompilerParams(vmem_limit_bytes=VM_F * MIB),
        cost_estimate=pl.CostEstimate(flops=13_000_000_000, bytes_accessed=1_000_000, transcendentals=2_000_000),
        name="feed",
    )(*args, *extra)


def back_kernel(parts, rows, first, *refs):
    x_refs = refs[:parts]
    qa, k_ref, v_ref, doa, caug, gm, vec_ref, wqkv = refs[parts:parts + 8]
    refs = refs[parts + 8:]
    if first:
        dwq_in = sm_in = None
    else:
        dwq_in, sm_in = refs[:2]
        refs = refs[2:]
    g_refs, (dwq, sm, dm_s) = refs[:parts], refs[parts:]
    n, width = k_ref.shape
    step = n // 3 if n % 48 == 0 else n
    vec = lambda i: vec_ref[i:i + 1, :]

    def add(ref, ref_in, at, value):
        ref[at] = value if first else ref_in[at] + value

    k_t = k_ref[...].T
    lane = lax.broadcasted_iota(jnp.int32, (step, 128), 1)
    ones = jnp.ones((step, 128), bf)
    for j in range(width // 128):
        sl = slice(128 * j, 128 * j + 128)
        dqt = [None, None]
        dvsum = None
        for c in range(n // step):
            cs = slice(c * step, c * step + step)
            dvs, dks = [], []
            for e in range(2):
                h = 2 * j + e
                hs = slice(128 * h, 128 * h + 128)
                own = (lane < 64) if e == 0 else (lane >= 64)
                kp = jnp.where(own, k_ref[cs, sl], caug[cs, :])
                vp = jnp.where(own, v_ref[cs, sl], ones)
                p = jnp.exp(mm_nt(kp, qa[:, hs]))
                ds = (p * mm_nt(vp, doa[:, hs])).astype(bf)
                dvs.append(mm(p.astype(bf), doa[:, hs]))
                dks.append(mm(ds, qa[:, hs]))
                t = mm(k_t[64 * h:64 * h + 64, cs], ds)
                dqt[e] = t if dqt[e] is None else dqt[e] + t
            dm_s[cs, width + 128 * j:width + 128 * j + 128] = jnp.where(lane < 64, dks[0], dks[1]).astype(bf)
            dv = jnp.where(lane < 64, dvs[0], dvs[1])
            dm_s[cs, 2 * width + 128 * j:2 * width + 128 * j + 128] = dv.astype(bf)
            s = jnp.sum(dv, axis=0, keepdims=True)
            dvsum = s if dvsum is None else dvsum + s
        add(sm, sm_in, (slice(3, 4), sl), dvsum)
        dq = jnp.concatenate(dqt, axis=0).T * 0.125
        add(sm, sm_in, (slice(2, 3), sl), jnp.sum(dq, axis=0, keepdims=True))
        dm_s[:, sl] = dq.astype(bf)
    x = jnp.concatenate([ref[0:rows, :] for ref in x_refs], axis=0).astype(f32)
    xh, r = normalise(x)
    nrm_t = (xh * vec(0) + vec(1)).astype(bf).T
    for j in range(3):
        js = slice(width * j, width * (j + 1))
        add(dwq, dwq_in, (js, slice(None)), mm(nrm_t, dm_s[:, js]))
    if first:
        if dwq.shape[0] > 3 * width:
            dwq[3 * width:, :] = jnp.zeros((dwq.shape[0] - 3 * width, width), f32)
        sm[4:8, :] = jnp.zeros((4, width), f32)
    else:
        sm[4:8, :] = sm_in[4:8, :]
    gf = mm_nt(dm_s[...], wqkv[...])
    gg = gf * vec(0)
    gx = gm[...] + r * (gg - row_mean(gg) - xh * row_mean(gg * xh))
    add(sm, sm_in, (slice(0, 1), slice(None)), jnp.sum(gf * xh, axis=0, keepdims=True))
    add(sm, sm_in, (slice(1, 2), slice(None)), jnp.sum(gf, axis=0, keepdims=True))
    for i in range(parts):
        g_refs[i][...] = gx[i * rows:(i + 1) * rows, :].astype(bf)


def back_call(pieces, rows, packed_rows, qa, k, v, doa, caug, gm, vec, wqkv, dwq, sm):
    parts = len(pieces)
    n, width = k.shape
    first = dwq is None
    vm = pl.BlockSpec(memory_space=pltpu.VMEM)
    outs = [((rows, width), bf)] * parts + [((packed_rows, width), f32), ((8, width), f32)]
    extra = () if first else (dwq, sm)
    base = parts + 8
    return pl.pallas_call(
        lambda *refs: back_kernel(parts, rows, first, *refs),
        out_shape=[jax.ShapeDtypeStruct(s, d) for s, d in outs],
        in_specs=[vm] * (base + len(extra)), out_specs=[vm] * (parts + 2),
        input_output_aliases={} if first else {base: parts, base + 1: parts + 1},
        scratch_shapes=[pltpu.VMEM((n, 3 * width), bf)],
        compiler_params=pltpu.CompilerParams(vmem_limit_bytes=VM_B * MIB),
        cost_estimate=pl.CostEstimate(flops=8_000_000_000, bytes_accessed=1_000_000, transcendentals=2_000_000),
        name="back",
    )(*pieces, qa, k, v, doa, caug, gm, vec, wqkv, *extra)


def unpack_kernel(hidden, a0, a1, b0, b1, gdn, gup, gout, gqkv, a_s, b_s):
    side = lax.axis_index("dp") & 1
    half_a, width = a0.shape
    half_b = b0.shape[0]
    a_s[pl.ds(pl.multiple_of(side * half_a, 16), half_a), :] = a0[...]
    a_s[pl.ds(pl.multiple_of((1 - side) * half_a, 16), half_a), :] = a1[...]
    b_s[pl.ds(pl.multiple_of(side * half_b, 16), half_b), :] = b0[...]
    b_s[pl.ds(pl.multiple_of((1 - side) * half_b, 16), half_b), :] = b1[...]
    blocks = hidden // width
    for j in range(blocks):
        js = slice(width * j, width * (j + 1))
        gdn[js, :] = a_s[js, :].T.astype(f32)
        gup[:, js] = a_s[width * (blocks + j):width * (blocks + j + 1), :].astype(f32)
    gout[...] = a_s[2 * blocks * width:(2 * blocks + 1) * width, :].astype(f32)
    for j in range(3):
        js = slice(width * j, width * (j + 1))
        gqkv[:, js] = b_s[js, :].astype(f32)


def unpack_call(hidden, a0, a1, b0, b1):
    width = a0.shape[1]
    vm = pl.BlockSpec(memory_space=pltpu.VMEM)
    outs = [(hidden, width), (width, hidden), (width, width), (width, 3 * width)]
    return pl.pallas_call(
        lambda *refs: unpack_kernel(hidden, *refs),
        out_shape=[jax.ShapeDtypeStruct(s, f32) for s in outs],
        in_specs=[vm] * 4, out_specs=[vm] * 4,
        scratch_shapes=[pltpu.VMEM((2 * a0.shape[0], width), bf), pltpu.VMEM((2 * b0.shape[0], width), bf)],
        compiler_params=pltpu.CompilerParams(vmem_limit_bytes=24 * MIB),
        name="unpack",
    )(a0, a1, b0, b1)


def place_kernel(parts, own, *refs):
    out = refs[parts * own]
    me = lax.axis_index("seq")
    for k in range(parts):
        for i in range(own):
            out[(me ^ k) * own + i] = refs[i * parts + k][...].astype(f32)


def place_call(got):
    own, parts = len(got), len(got[0])
    rows, width = got[0][0].shape
    vm = pl.BlockSpec(memory_space=pltpu.VMEM)
    return pl.pallas_call(
        lambda *refs: place_kernel(parts, own, *refs),
        out_shape=jax.ShapeDtypeStruct((parts * own, rows, width), f32),
        in_specs=[vm] * (parts * own), out_specs=vm,
        compiler_params=pltpu.CompilerParams(vmem_limit_bytes=8 * MIB),
        name="place",
    )(*[g for image in got for g in image])


VM_A, VM_F, VM_B = 24, 32, 24


def xor_permute(x, axis, k):
    return lax.ppermute(x, axis, [(i, i ^ k) for i in range(lax.axis_size(axis))])


def after(x, *others):
    return lax.optimization_barrier((x,) + others)[0]


def tree_sum(parts):
    while len(parts) > 1:
        parts = [parts[i] + parts[i + 1] for i in range(0, len(parts), 2)]
    return parts[0]


def pick(x, index):
    return lax.dynamic_index_in_dim(x, index, 0, keepdims=False)


def halves(small):
    high = lax.reduce_precision(small, 8, 7)
    return jnp.concatenate([high, lax.reduce_precision(small - high, 8, 7)], axis=0).astype(bf)


def whole(pair):
    rows = pair.shape[0] // 2
    return pair[:rows].astype(f32) + pair[rows:].astype(f32)


def scatter_stage(big, small, axis, index, count, shift):
    chunks = big.reshape(count, big.shape[0] // count, big.shape[1])
    rows = chunks.shape[1]
    pair = halves(small)
    kept = [pick(chunks, index).astype(f32)]
    smalls = [whole(pair)]
    for k in range(1, count):
        sent = jnp.concatenate([pick(chunks, index ^ k).astype(bf), pair], axis=0)
        got = xor_permute(sent, axis, k << shift)
        kept.append(got[:rows].astype(f32))
        smalls.append(whole(got[rows:]))
    return tree_sum(kept), tree_sum(smalls)


def gather_stage(part, axis, index, count, shift):
    out = jnp.zeros((count,) + part.shape, part.dtype)
    out = lax.dynamic_update_index_in_dim(out, part, index, 0)
    for k in range(1, count):
        got = xor_permute(part, axis, k << shift)
        out = lax.dynamic_update_index_in_dim(out, got, index ^ k, 0)
    return out


class Reduction:
    def __init__(self):
        self.dp, self.seq = lax.axis_index("dp"), lax.axis_index("seq")
        self.chips, self.depth = lax.axis_size("dp") // 2, lax.axis_size("seq")

    def core(self, big, small):
        return scatter_stage(big, small, "dp", self.dp & 1, 2, 0)

    def plane(self, big, small):
        return scatter_stage(big, small, "dp", self.dp >> 1, self.chips, 1)

    def column(self, big, small):
        return scatter_stage(big, small, "seq", self.seq, self.depth, 0)

    def spread_column(self, part, rider=None):
        part = part.astype(bf)
        rows, width = part.shape
        if rider is not None:
            part = jnp.concatenate([part, rider], axis=0)
        part = gather_stage(part, "seq", self.seq, self.depth, 0)
        return part[:, :rows].reshape(-1, width), part[:, rows:]

    def spread_plane(self, part):
        return gather_stage(part, "dp", self.dp >> 1, self.chips, 1).reshape(-1, part.shape[1])

    def spread_core(self, part):
        return part, xor_permute(part, "dp", 1)


def padded(rows, unit):
    return rows + -rows % unit


def per_device(
    patches, first_gain, first_shift, qkv_weight, query_value_bias, out_weight, out_bias,
    second_gain, second_shift, up_weight, up_bias, down_weight, down_bias, map_weight, map_bias,
    keep_mask, image_valid, token_cotangent,
):
    images, rows, width = patches.shape
    me = lax.axis_index("seq")
    depth, dps = lax.axis_size("seq"), lax.axis_size("dp")
    own = images // depth
    hidden, tokens = up_weight.shape[1], map_weight.shape[1]
    nb = hidden // width
    unit = 8 * dps * depth
    rows_a, rows_b = padded((2 * nb + 1) * width, unit), padded(3 * width, unit)

    blocks = patches.reshape(depth, own, rows, width)
    flags = keep_mask.astype(bf).reshape(depth, own, rows)
    flags = jnp.pad(flags, ((0, 0), (0, 16 - own), (0, width - rows)))
    order = sorted(range(1, depth), key=lambda k: (k == 1, k))
    pieces = []
    hold = None
    for i in range(own):
        got = [None] * depth
        for k in [0] + order:
            b = pick(blocks, me ^ k)[i]
            if i == 0:
                b = jnp.concatenate([b, pick(flags, me ^ k)], axis=0)
            if k > 0:
                if hold is not None:
                    b = after(b, hold)
                b = xor_permute(b, "seq", k)
            got[k] = b
        hold = got[order[-1]]
        pieces.append(got)

    count = jnp.broadcast_to(jnp.sum(image_valid.astype(f32)), (8, 128))
    step = 1
    while step < dps:
        count = count + xor_permute(count, "dp", step)
        step *= 2
    vec = jnp.concatenate([
        first_gain, first_shift, query_value_bias, out_bias, second_gain, second_shift, down_bias,
        up_bias, jnp.zeros((4 * width,), bf),
    ]).astype(f32).reshape(-1, width)
    mb = jnp.broadcast_to(map_bias.astype(f32)[:, None], (tokens, 128))
    mapw = map_weight.T

    saved, learned = [], []
    acc = sm = tok = None
    for i in range(own):
        v = vec if tok is None else after(vec, tok)
        qa, key, val, caug, att, mid = attend_call(pieces[i], pieces[0], i, rows, v, qkv_weight, out_weight)
        gm, doa, learn, acc, sm = feed_call(
            i, own, rows_a, mid, att, caug, vec, mb, mapw, token_cotangent, image_valid, count,
            out_weight, up_weight, down_weight, acc, sm)
        tok = sm
        saved.append((qa, key, val, doa, caug, gm))
        learned.append(learn)
    red = Reduction()
    rider = halves(jnp.concatenate(learned, axis=0))
    big, small = red.core(acc, sm)

    dwq = smq = None
    sent = []
    for i in range(own):
        if i == 0:
            v = after(vec, tok)
        elif i == 1:
            v = after(vec, smq, small)
            big, small = red.plane(big, small)
        else:
            v = after(vec, smq, small)
        if i == own - 1:
            big, small = red.column(big, small)
        o = back_call(pieces[i], rows, rows_b, *saved[i], v, qkv_weight, dwq, smq)
        dwq, smq = o[depth], o[depth + 1]
        sent.append(o[:depth])
    got = [[g if k == 0 else xor_permute(g, "seq", k) for k, g in enumerate(s)] for s in sent]
    part, rider = red.spread_column(big, rider)
    part = red.spread_plane(part)
    a0, a1 = red.spread_core(part)
    bigb, smallb = red.core(dwq, smq)
    bigb, smallb = red.plane(bigb, smallb)
    bigb, smallb = red.column(bigb, smallb)
    partb, _ = red.spread_column(bigb)
    partb = red.spread_plane(partb)
    b0, b1 = red.spread_core(partb)
    gdn, gup, gout, gqkv = unpack_call(hidden, a0, a1, b0, b1)
    outs = place_call(got)

    n = own * tokens
    learned = (rider[:, :n].astype(f32) + rider[:, n:].astype(f32)).reshape(images, tokens, width)
    penalty = small[16, 1] / count[0, 0]
    return (
        learned, penalty, outs, smallb[0], smallb[1], gqkv, smallb[2:4].reshape(-1), gout, small[1],
        small[2], small[3], gup, small[4:4 + nb].reshape(-1), gdn, small[0],
        small[8:16].T, small[16:24, 0],
    )


def solution(mesh):
    rep = P()
    placed = (P("dp", "seq", None),) + (rep,) * 14 + (P("dp", "seq"), P("dp"), P("dp", None, None))
    return jax.shard_map(
        per_device, mesh=mesh, in_specs=placed,
        out_specs=(P("dp", None, None), rep, P("dp", "seq", None)) + (rep,) * 14,
        check_vma=False,
    )
```

```python
import jax
import jax.numpy as jnp
from jax import lax
from jax.experimental import pallas as pl
from jax.experimental.pallas import tpu as pltpu
from jax.sharding import PartitionSpec as P

f32, bf = jnp.float32, jnp.bfloat16
EPSILON = 1e-6
MASKED = -1e30
MIB = 1 << 20


def in_hbm(x):
    return pltpu.with_memory_space_constraint(x, pltpu.HBM)


def mm(a, b):
    return lax.dot_general(a, b, (((1,), (0,)), ((), ())), preferred_element_type=f32)


def mm_nt(a, b):
    return lax.dot_general(a, b, (((1,), (1,)), ((), ())), preferred_element_type=f32)


def mm_tn(a, b):
    return lax.dot_general(a, b, (((0,), (0,)), ((), ())), preferred_element_type=f32)


def row_mean(x):
    return jnp.sum(x, axis=-1, keepdims=True) * (1.0 / x.shape[-1])


def normalise(x):
    centred = x - row_mean(x)
    r = lax.rsqrt(row_mean(centred * centred) + EPSILON)
    return centred * r, r


def normal_parts(v):
    expo = jnp.exp(v * v * (-0.5))
    t = 1.0 / (1.0 + jnp.abs(v) * (0.3275911 * 0.7071067811865476))
    series = t * (0.127414796 + t * (-0.142248368 + t * (0.7107068705 + t * (-0.7265760135 + t * 0.5307027145))))
    tail = series * expo
    return jnp.where(v >= 0, 1.0 - tail, tail), expo * 0.3989422804014327


def split2(a):
    high = a.astype(bf)
    return high, (a - high.astype(f32)).astype(bf)


def attend_kernel(parts, rows, slot, base, *refs):
    x_refs, flag_refs = refs[:parts], refs[parts:2 * parts]
    vec_ref, wqkv, wout = refs[2 * parts:2 * parts + 3]
    qa_ref, k_ref, v_ref, caug_ref, att_ref, mid_ref = refs[2 * parts + 3:2 * parts + 9]
    nrm_s, q_s = refs[2 * parts + 9:]
    n, width = nrm_s.shape
    vec = lambda i: vec_ref[i:i + 1, :]
    r8 = lax.broadcasted_iota(jnp.int32, (8, 128), 0)
    l8 = lax.broadcasted_iota(jnp.int32, (8, 128), 1) & 63
    place = ((r8 == 0) & (l8 == 3)) | ((r8 == 1) & (l8 < 3)) | ((r8 == 2) & (l8 == 4))
    place = jnp.where(place, 1.0, 0.0).astype(bf)
    row = lax.broadcasted_iota(jnp.int32, (8, rows), 0)
    for i in range(parts):
        rs = slice(i * rows, (i + 1) * rows)
        xh, _ = normalise(x_refs[i][base:base + rows, :].astype(f32))
        nrm_s[rs, :] = (xh * vec(0) + vec(1)).astype(bf)
        keep = flag_refs[i][rows:rows + 16, 0:rows].astype(f32)[slot:slot + 1, :]
        marks = jnp.where(row == 0, (1.0 - keep) * MASKED, jnp.where(row == 1, 1.0, jnp.where(row == 2, keep, 0.0)))
        caug_ref[rs, :] = mm_tn(marks.astype(bf), place).astype(bf)
    nrm = nrm_s[...]
    q_s[...] = (mm(nrm, wqkv[:, 0:width]) + vec(2)).astype(bf) * jnp.asarray(0.125, bf)
    k_ref[...] = mm(nrm, wqkv[:, width:2 * width]).astype(bf)
    v_ref[...] = (mm(nrm, wqkv[:, 2 * width:3 * width]) + vec(3)).astype(bf)
    lane = lax.broadcasted_iota(jnp.int32, (n, 128), 1)
    lane64 = lane & 63
    ones = jnp.ones((n, 128), bf)
    for j in range(width // 128):
        sl = slice(128 * j, 128 * j + 128)
        outs = []
        for e in range(2):
            own = (lane < 64) if e == 0 else (lane >= 64)
            kp = jnp.where(own, k_ref[:, sl], caug_ref[...])
            qp = jnp.where(own, q_s[:, sl], jnp.where(lane64 == 3, 1.0, 0.0).astype(bf))
            s = mm_nt(qp, kp)
            m = jnp.max(s, axis=-1, keepdims=True)
            p = jnp.exp(s - m).astype(bf)
            o = mm(p, jnp.concatenate([v_ref[:, sl], ones], axis=1))
            total = o[:, 128:256]
            outs.append(o[:, 0:128] / total)
            logs = -(m + jnp.log(total))
            hi = logs.astype(bf).astype(f32)
            lo = (logs - hi).astype(bf).astype(f32)
            aug = jnp.where(lane64 == 0, hi, jnp.where(lane64 == 1, lo, jnp.where(lane64 == 2, logs - hi - lo, jnp.where(lane64 == 3, 1.0, 0.0))))
            h = 2 * j + e
            qa_ref[:, 128 * h:128 * h + 128] = jnp.where(own, q_s[:, sl], aug.astype(bf))
        att_ref[:, sl] = jnp.where(lane < 64, outs[0], outs[1]).astype(bf)
    pr = mm(att_ref[...], wout[...])
    for i in range(parts):
        rs = slice(i * rows, (i + 1) * rows)
        mid_ref[rs, :] = x_refs[i][base:base + rows, :].astype(f32) + pr[rs, :] + vec(4)


def attend_call(pieces, flags, slot, base, rows, vec, wqkv, wout):
    parts, width = len(pieces), wout.shape[0]
    n = parts * rows
    vm = pl.BlockSpec(memory_space=pltpu.VMEM)
    outs = [((n, 2 * width), bf), ((n, width), bf), ((n, width), bf), ((n, 128), bf), ((n, width), bf), ((n, width), f32)]
    return pl.pallas_call(
        lambda *refs: attend_kernel(parts, rows, slot, base, *refs),
        out_shape=[jax.ShapeDtypeStruct(s, d) for s, d in outs],
        in_specs=[vm] * (2 * parts + 3), out_specs=[vm] * 6,
        scratch_shapes=[pltpu.VMEM((n, width), bf), pltpu.VMEM((n, width), bf)],
        compiler_params=pltpu.CompilerParams(vmem_limit_bytes=VM_A * MIB),
        cost_estimate=pl.CostEstimate(flops=1_000_000, bytes_accessed=1000, transcendentals=0),
        name="attend",
    )(*pieces, *flags, vec, wqkv, wout)


def feed_kernel(slot, own_count, first, *refs):
    mid_ref, att_ref, caug_ref, vec_ref, mb_ref, cm_ref, valid_ref, count_ref, wout, wup, wdn = refs[:11]
    refs = refs[11:]
    if first:
        acc_in = dwo_in = sm_in = None
    else:
        acc_in, dwo_in, sm_in = refs[:3]
        refs = refs[3:]
    gm_ref, doa_ref, learn_ref, acc, dwo, sm = refs[:6]
    sec_s, hid_s, gp_s, g_s = refs[6:]
    n, width = mid_ref.shape
    blocks = hid_s.shape[1] // width
    tokens = mb_ref.shape[0]
    vec = lambda i: vec_ref[i:i + 1, :]
    place = lax.axis_index("seq") * own_count + slot

    def add(ref, ref_in, rows, value):
        ref[rows, :] = value if first else ref_in[rows, :] + value

    xh, _ = normalise(mid_ref[...])
    sec_s[...] = (xh * vec(5) + vec(6)).astype(bf)
    total = None
    for j in range(blocks):
        js = slice(width * j, width * (j + 1))
        pre = mm(sec_s[...], wup[:, js]) + vec(8 + j)
        upper, density = normal_parts(pre)
        hid_s[:, js] = (pre * upper).astype(bf)
        gp_s[:, js] = upper + pre * density
        t = mm(hid_s[:, js], wdn[js, :])
        total = t if total is None else total + t
    out = mid_ref[...] + total + vec(7)
    ohi, olo = split2(out)
    cm = cm_ref[slot]
    lg = mm_nt(cm, ohi) + mm_nt(cm, olo)
    pick = jnp.where(lax.broadcasted_iota(jnp.int32, (8, 128), 1) == 4, 1.0, 0.0).astype(bf)
    keep = mm_nt(pick, caug_ref[...])[0:1, :]
    maps = jax.nn.sigmoid(lg[0:tokens, :] + mb_ref[:, 0:1])
    inverse = 1.0 / jnp.sum(keep, axis=-1, keepdims=True)
    tot = jnp.sum(maps, axis=0, keepdims=True)
    inter = jnp.sum(keep * (tot * tot - jnp.sum(maps * maps, axis=0, keepdims=True)), axis=-1, keepdims=True)
    valid = valid_ref[place].astype(f32)
    gmaps = keep * (lg[tokens:2 * tokens, :] * inverse + (2.0 * valid / count_ref[0:1, 0:1]) * (tot - maps))
    gl = gmaps * maps * (1.0 - maps)
    mk = maps * keep
    mkh, mkl = split2(mk)
    glh, gll = split2(gl)
    st = jnp.concatenate([mkh.astype(f32), mkl.astype(f32), glh.astype(f32), gll.astype(f32)], axis=0).astype(bf)
    r1 = mm(st, ohi) + mm(st, olo)
    learn_ref[...] = (r1[0:tokens, :] + r1[tokens:2 * tokens, :]) * inverse
    add(sm, sm_in, slice(8, 16), r1[2 * tokens:3 * tokens, :] + r1[3 * tokens:, :])
    gah, gal = split2(mk * inverse)
    lhs = jnp.concatenate([glh.astype(f32), gah.astype(f32), gll.astype(f32), gal.astype(f32)], axis=0).astype(bf)
    g = mm_tn(lhs, jnp.concatenate([cm, cm], axis=0))
    g_s[...] = g
    add(sm, sm_in, slice(0, 1), jnp.sum(g, axis=0, keepdims=True))
    glow = g.astype(bf)
    g_t = glow.T
    sec_t = sec_s[...].T
    gsec = None
    for j in range(blocks):
        js = slice(width * j, width * (j + 1))
        gh = mm_nt(glow, wdn[js, :]).astype(bf).astype(f32)
        gpre = gh * gp_s[:, js]
        gpl = gpre.astype(bf)
        add(sm, sm_in, slice(4 + j, 5 + j), jnp.sum(gpre, axis=0, keepdims=True))
        t = mm_nt(gpl, wup[:, js])
        gsec = t if gsec is None else gsec + t
        add(acc, acc_in, js, mm(g_t, hid_s[:, js]))
        add(acc, acc_in, slice(width * (blocks + j), width * (blocks + j + 1)), mm(sec_t, gpl))
    xh, r = normalise(mid_ref[...])
    gg = gsec * vec(5)
    gm = g_s[...] + r * (gg - row_mean(gg) - xh * row_mean(gg * xh))
    gm_ref[...] = gm
    gml = gm.astype(bf)
    add(sm, sm_in, slice(1, 2), jnp.sum(gm, axis=0, keepdims=True))
    add(sm, sm_in, slice(2, 3), jnp.sum(gsec * xh, axis=0, keepdims=True))
    add(sm, sm_in, slice(3, 4), jnp.sum(gsec, axis=0, keepdims=True))
    glb = jnp.sum(gl, axis=-1, keepdims=True)
    lr = lax.broadcasted_iota(jnp.int32, (8, width), 1)
    rr = lax.broadcasted_iota(jnp.int32, (8, width), 0)
    line = jnp.sum(jnp.where(lr == rr, glb, 0.0), axis=0, keepdims=True)
    line = line + jnp.where(lr[0:1] == tokens, valid * inter * (1.0 / n), 0.0)
    add(sm, sm_in, slice(16, 24), jnp.where(rr == 0, line, 0.0))
    if first:
        sm[24:32, :] = jnp.zeros((8, width), f32)
        if acc.shape[0] > 2 * blocks * width:
            acc[2 * blocks * width:, :] = jnp.zeros((acc.shape[0] - 2 * blocks * width, width), f32)
    else:
        sm[24:32, :] = sm_in[24:32, :]
        if acc.shape[0] > 2 * blocks * width:
            acc[2 * blocks * width:, :] = acc_in[2 * blocks * width:, :]
    add(dwo, dwo_in, slice(0, width), mm(att_ref[...].T, gml))
    do = mm_nt(gml, wout[...]).astype(bf).astype(f32)
    lane = lax.broadcasted_iota(jnp.int32, (n, 128), 1)
    lane64 = lane & 63
    for j in range(width // 128):
        sl = slice(128 * j, 128 * j + 128)
        dj = do[:, sl]
        pd = dj * att_ref[:, sl].astype(f32)
        for e in range(2):
            own = (lane < 64) if e == 0 else (lane >= 64)
            dl = -jnp.sum(jnp.where(own, pd, 0.0), axis=-1, keepdims=True)
            hi = dl.astype(bf).astype(f32)
            aug = jnp.where(lane64 == 0, hi, jnp.where(lane64 == 1, dl - hi, 0.0))
            h = 2 * j + e
            doa_ref[:, 128 * h:128 * h + 128] = jnp.where(own, dj, aug).astype(bf)


def feed_call(slot, own_count, packed_rows, mid, att, caug, vec, mb, cm, valid, count, wout, wup, wdn, acc, dwo, sm):
    n, width = mid.shape
    hidden = wup.shape[1]
    first = acc is None
    vm = pl.BlockSpec(memory_space=pltpu.VMEM)
    smem = pl.BlockSpec(memory_space=pltpu.SMEM)
    outs = [((n, width), f32), ((n, 2 * width), bf), ((8, width), f32), ((packed_rows, width), f32), ((width, width), f32), ((32, width), f32)]
    args = (mid, att, caug, vec, mb, cm, valid, count, wout, wup, wdn)
    extra = () if first else (acc, dwo, sm)
    return pl.pallas_call(
        lambda *refs: feed_kernel(slot, own_count, first, *refs),
        out_shape=[jax.ShapeDtypeStruct(s, d) for s, d in outs],
        in_specs=[vm] * 6 + [smem] + [vm] * (4 + len(extra)), out_specs=[vm] * 6,
        input_output_aliases={} if first else {11: 3, 12: 4, 13: 5},
        scratch_shapes=[pltpu.VMEM((n, width), bf), pltpu.VMEM((n, hidden), bf), pltpu.VMEM((n, hidden), f32), pltpu.VMEM((n, width), f32)],
        compiler_params=pltpu.CompilerParams(vmem_limit_bytes=VM_F * MIB),
        cost_estimate=pl.CostEstimate(flops=1_000_000, bytes_accessed=1000, transcendentals=0),
        name="feed",
    )(*args, *extra)


def scores_back(js, qa, k_ref, v_ref, doa, caug, dm, sums):
    n, width = k_ref.shape
    step = n // 3 if n % 48 == 0 else n
    lane = lax.broadcasted_iota(jnp.int32, (step, 128), 1)
    ones = jnp.ones((step, 128), bf)
    for j in js:
        sl = slice(128 * j, 128 * j + 128)
        k_t = k_ref[:, sl].T
        dqt = [None, None]
        dvsum = None
        for c in range(n // step):
            cs = slice(c * step, c * step + step)
            dvs, dks = [], []
            for e in range(2):
                hs = slice(256 * j + 128 * e, 256 * j + 128 * e + 128)
                own = (lane < 64) if e == 0 else (lane >= 64)
                kp = jnp.where(own, k_ref[cs, sl], caug[cs, :])
                vp = jnp.where(own, v_ref[cs, sl], ones)
                p = jnp.exp(mm_nt(kp, qa[:, hs]))
                ds = (p * mm_nt(vp, doa[:, hs])).astype(bf)
                dvs.append(mm(p.astype(bf), doa[:, hs]))
                dks.append(mm(ds, qa[:, hs]))
                t = mm(k_t[64 * e:64 * e + 64, cs], ds)
                dqt[e] = t if dqt[e] is None else dqt[e] + t
            dm[cs, width + 128 * j:width + 128 * j + 128] = jnp.where(lane < 64, dks[0], dks[1]).astype(bf)
            dv = jnp.where(lane < 64, dvs[0], dvs[1])
            dm[cs, 2 * width + 128 * j:2 * width + 128 * j + 128] = dv.astype(bf)
            s = jnp.sum(dv, axis=0, keepdims=True)
            dvsum = s if dvsum is None else dvsum + s
        dq = jnp.concatenate(dqt, axis=0).T * 0.125
        dm[:, sl] = dq.astype(bf)
        sums[0:1, sl] = jnp.sum(dq, axis=0, keepdims=True)
        sums[1:2, sl] = dvsum


def norm_back(rows, base, x_refs, gm, dm, vec_ref, wqkv, g_refs, nrm_ref):
    vec = lambda i: vec_ref[i:i + 1, :]
    gf = mm_nt(dm[...], wqkv[...])
    x = jnp.concatenate([ref[base:base + rows, :] for ref in x_refs], axis=0).astype(f32)
    xh, r = normalise(x)
    nrm_ref[...] = (xh * vec(0) + vec(1)).astype(bf)
    gg = gf * vec(0)
    gx = gm[...] + r * (gg - row_mean(gg) - xh * row_mean(gg * xh))
    for i in range(len(x_refs)):
        g_refs[i][...] = gx[i * rows:(i + 1) * rows, :].astype(bf)
    return jnp.sum(gf * xh, axis=0, keepdims=True), jnp.sum(gf, axis=0, keepdims=True)


def start_kernel(qa, k_ref, v_ref, doa, caug, dm, sums):
    sums[...] = jnp.zeros_like(sums)
    scores_back([0], qa, k_ref, v_ref, doa, caug, dm, sums)


def start_call(*attn):
    n, width = attn[1].shape
    return small_call(start_kernel, attn, [((n, 3 * width), bf), ((8, width), f32)], "start", VM_B)


def back_kernel(parts, rows, base, started, *refs):
    attn, (vec_ref, wqkv), x_refs, gm = refs[:5], refs[5:7], refs[7:7 + parts], refs[7 + parts]
    refs = refs[8 + parts:]
    if started:
        dm0, sums0 = refs[:2]
        refs = refs[2:]
    dm, sums = refs[:2]
    width = gm.shape[1]
    pairs = range(width // 128)
    if started:
        sums[...] = sums0[...]
        for s in range(3):
            dm[:, width * s:width * s + 128] = dm0[:, width * s:width * s + 128]
        pairs = pairs[1:]
    else:
        sums[...] = jnp.zeros_like(sums)
    scores_back(pairs, *attn, dm, sums)
    if parts:
        g_refs, nrm = refs[2:2 + parts], refs[-1]
        gain, shift = norm_back(rows, base, x_refs, gm, dm, vec_ref, wqkv, g_refs, nrm)
        sums[2:3, :] = gain
        sums[3:4, :] = shift


def back_call(attn, rows, base, vec, wqkv, pieces, gm, started=()):
    n, width = attn[1].shape
    parts = len(pieces)
    outs = [((n, 3 * width), bf), ((8, width), f32)]
    if parts:
        outs += [((rows, width), bf)] * parts + [((n, width), bf)]
    return small_call(
        lambda *refs: back_kernel(parts, rows, base, len(started) > 0, *refs),
        (*attn, vec, wqkv, *pieces, gm, *started), outs, "back", VM_B)


def last_kernel(parts, rows, base, own, *refs):
    x_refs, gm, vec_ref, wqkv = refs[:parts], refs[parts], refs[parts + 1], refs[parts + 2]
    refs = refs[parts + 3:]
    dms, sums, nrms, dwo = refs[:own], refs[own:2 * own], refs[2 * own:3 * own - 1], refs[3 * own - 1]
    packed, sm, g_ref, nrm_s = refs[3 * own], refs[3 * own + 1], refs[3 * own + 2:-1], refs[-1]
    width = gm.shape[1]
    gain, shift = norm_back(rows, base, x_refs, gm, dms[-1], vec_ref, wqkv, g_ref, nrm_s)
    total = sum(ref[0:4, :] for ref in sums)
    sm[...] = jnp.zeros_like(sm)
    sm[0:1, :] = total[2:3, :] + gain
    sm[1:2, :] = total[3:4, :] + shift
    sm[2:4, :] = total[0:2, :]
    nrm_t = [ref[...].T for ref in nrms] + [nrm_s[...].T]
    for s in range(3):
        js = slice(width * s, width * (s + 1))
        value = None
        for i in range(own):
            t = mm(nrm_t[i], dms[i][:, js])
            value = t if value is None else value + t
        packed[js, :] = value
    packed[3 * width:4 * width, :] = dwo[...]
    if packed.shape[0] > 4 * width:
        packed[4 * width:, :] = jnp.zeros((packed.shape[0] - 4 * width, width), f32)


def last_call(packed_rows, rows, base, pieces, gm, vec, wqkv, dms, sums, nrms, dwo):
    own, parts = len(dms), len(pieces)
    n, width = gm.shape
    args = (*pieces, gm, vec, wqkv, *dms, *sums, *nrms, dwo)
    outs = [((packed_rows, width), f32), ((16, width), f32)] + [((rows, width), bf)] * parts
    return small_call(
        lambda *refs: last_kernel(parts, rows, base, own, *refs), args, outs, "last", VM_W,
        scratch=[pltpu.VMEM((n, width), bf)])


def aligned(start, rows):
    return pl.ds(pl.multiple_of(start, 16), rows)


def tree_sum(parts):
    while len(parts) > 1:
        parts = [parts[i] + parts[i + 1] for i in range(0, len(parts), 2)]
    return parts[0]


def store_small(ref, at, small):
    rows = small.shape[0]
    high = small.astype(bf)
    ref[at:at + rows, :] = high
    ref[at + rows:at + 2 * rows, :] = (small - high.astype(f32)).astype(bf)


def load_small(ref, at, rows):
    return ref[at:at + rows, :].astype(f32) + ref[at + rows:at + 2 * rows, :].astype(f32)


def rounded(small):
    high, low = split2(small)
    return high.astype(f32) + low.astype(f32)


def core_kernel(big, small, out):
    half = big.shape[0] // 2
    other = 1 - (lax.axis_index("dp") & 1)
    out[0:half, :] = big[aligned(other * half, half), :].astype(bf)
    store_small(out, half, small[...])


def core_call(big, small):
    rows, width = big.shape
    return small_call(core_kernel, (big, small), [((rows // 2 + 2 * small.shape[0], width), bf)], "core", 4)[0]


def plane_kernel(big, small, got, *outs):
    sends, keep, total = outs[:-2], outs[-2], outs[-1]
    half, rows = big.shape[0] // 2, keep.shape[0]
    dp = lax.axis_index("dp")
    base, mine = (dp & 1) * half, dp >> 1
    summed = rounded(small[...]) + load_small(got, half, small.shape[0])
    total[...] = summed
    for k in range(len(sends) + 1):
        at = (mine ^ k) * rows
        value = big[aligned(base + at, rows), :] + got[aligned(at, rows), :].astype(f32)
        if k == 0:
            keep[...] = value
        else:
            sends[k - 1][0:rows, :] = value.astype(bf)
            store_small(sends[k - 1], rows, summed)


def plane_call(big, small, got, count):
    width, s = big.shape[1], small.shape[0]
    rows = big.shape[0] // 2 // count
    outs = [((rows + 2 * s, width), bf)] * (count - 1) + [((rows, width), f32), ((s, width), f32)]
    o = small_call(plane_kernel, (big, small, got), outs, "plane", 4)
    return o[:count - 1], o[-2], o[-1]


def halve_kernel(shift, count, rider, *refs):
    kept, small, gots, riding = refs[0], refs[1], refs[2:2 + count], refs[2 + count:2 + count + rider]
    send, keep, total = refs[2 + count + rider:]
    whole, rows, s = kept.shape[0], keep.shape[0], small.shape[0]
    mine = (lax.axis_index("seq") >> shift) & 1
    summed = tree_sum([rounded(small[...])] + [load_small(got, whole, s) for got in gots])
    total[...] = summed
    for k in range(2):
        at = (mine ^ k) * rows
        value = tree_sum([kept[aligned(at, rows), :]] + [got[aligned(at, rows), :].astype(f32) for got in gots])
        if k == 0:
            keep[...] = value
        else:
            send[0:rows, :] = value.astype(bf)
    store_small(send, rows, summed)
    at = rows + 2 * s
    for ref in riding:
        send[at:at + ref.shape[0], :] = ref[...]
        at += ref.shape[0]


def halve_call(kept, small, gots, shift, riders=()):
    width, s = kept.shape[1], small.shape[0]
    rows = kept.shape[0] // 2
    outs = [((rows + 2 * s + sum(x.shape[0] for x in riders), width), bf), ((rows, width), f32), ((s, width), f32)]
    return small_call(
        lambda *refs: halve_kernel(shift, len(gots), len(riders), *refs),
        (kept, small, *gots, *riders), outs, "halve", 6)


def spread_kernel(learns, rider, *refs):
    kept, small, got = refs[:3]
    learnt, riding = refs[3:3 + learns], refs[3 + learns:3 + learns + rider]
    total, part = refs[3 + learns + rider:]
    rows, s = kept.shape[0], small.shape[0]
    total[...] = rounded(small[...]) + load_small(got, rows, s)
    part[0:rows, :] = (kept[...] + got[0:rows, :].astype(f32)).astype(bf)
    at = rows
    if learns:
        used = sum(ref.shape[0] for ref in learnt)
        blank = [jnp.zeros((-used % 16, kept.shape[1]), f32)] if used % 16 else []
        learnt = jnp.concatenate([ref[...] for ref in learnt] + blank, axis=0)
        store_small(part, rows, learnt)
        at += 2 * learnt.shape[0]
    for ref in riding:
        part[at:at + ref.shape[0], :] = ref[...]
        at += ref.shape[0]


def learned_rows(learns):
    used = sum(ref.shape[0] for ref in learns)
    return 2 * (used + -used % 16)


def spread_call(kept, small, got, learns=(), riders=()):
    rows, width = kept.shape
    rows += learned_rows(learns) + sum(ref.shape[0] for ref in riders)
    outs = [(small.shape, f32), ((rows, width), bf)]
    total, part = small_call(
        lambda *refs: spread_kernel(len(learns), len(riders), *refs), (kept, small, got, *learns, *riders), outs, "spread", 6)
    return part, total


def join_kernel(axis, shift, rows, riding, count, extra, *refs):
    parts, extras, out = refs[:count], refs[count:count + extra], refs[count + extra]
    mine = (lax.axis_index(axis) >> shift) & (count - 1)
    for k, part in enumerate(parts):
        out[aligned((mine ^ k) * rows, rows), :] = part[0:rows, :]
        if riding:
            out[aligned(count * rows + (mine ^ k) * riding, riding), :] = part[rows:rows + riding, :]
    at = count * (rows + riding)
    for ref in extras:
        out[at:at + ref.shape[0], :] = ref[...]
        at += ref.shape[0]


def join_call(parts, axis, shift, rows, riding=0, extras=()):
    width = parts[0].shape[1]
    total = (rows + riding) * len(parts) + sum(x.shape[0] for x in extras)
    return small_call(
        lambda *refs: join_kernel(axis, shift, rows, riding, len(parts), len(extras), *refs), (*parts, *extras),
        [((total, width), bf)], "join", 6)[0]


def first_kernel(x, out):
    out[...] = x[0:out.shape[0], :]


def first_rows(x, rows):
    return small_call(first_kernel, (x,), [((rows, x.shape[1]), x.dtype)], "first", 4)[0]


def small_call(kernel, args, outs, name, mib, scratch=()):
    vm = pl.BlockSpec(memory_space=pltpu.VMEM)
    return pl.pallas_call(
        kernel,
        out_shape=[jax.ShapeDtypeStruct(s, d) for s, d in outs],
        in_specs=[vm] * len(args), out_specs=[vm] * len(outs), scratch_shapes=list(scratch),
        compiler_params=pltpu.CompilerParams(vmem_limit_bytes=mib * MIB),
        cost_estimate=pl.CostEstimate(flops=1_000_000, bytes_accessed=1000, transcendentals=0),
        name=name,
    )(*args)


def prepare_kernel(own, rows, depth, patches, keep, valid, count, *refs):
    blocks, (keep_s, sems) = refs[:2 * depth], refs[2 * depth:]
    width = patches.shape[2]
    me = lax.axis_index("seq")
    flags_copy = pltpu.make_async_copy(keep, keep_s, sems.at[depth * own])
    flags_copy.start()
    copies = []
    for k in [k for k in range(1, depth)] + [0]:
        for i in range(own):
            target = blocks[2 * k].at[0:rows, :] if i == 0 else blocks[2 * k + 1].at[rows * (i - 1):rows * i, :]
            copies.append(pltpu.make_async_copy(patches.at[(me ^ k) * own + i], target, sems.at[k * own + i]))
            copies[-1].start()
    total = valid[0]
    for i in range(1, valid.shape[0]):
        total = total + valid[i]
    count[...] = jnp.full(count.shape, total.astype(f32), f32)
    flags_copy.wait()
    line = lax.broadcasted_iota(jnp.int32, (16, rows), 0)
    for k in range(depth):
        flags = jnp.zeros((16, rows), f32)
        for i in range(own):
            flags = jnp.where(line == i, keep_s[pl.ds((me ^ k) * own + i, 1), :].astype(f32), flags)
        blocks[2 * k][rows:rows + 16, :] = jnp.zeros((16, width), bf)
        blocks[2 * k][rows:rows + 16, 0:rows] = flags.astype(bf)
    for copy in copies:
        copy.wait()


def prepare_call(depth, patches, keep, valid):
    images, rows, width = patches.shape
    own = images // depth
    vm, hbm = pl.BlockSpec(memory_space=pltpu.VMEM), pl.BlockSpec(memory_space=pltpu.HBM)
    outs = [((8, 128), f32)]
    for k in range(depth):
        outs += [((rows + 16, width), bf), ((rows * (own - 1), width), bf)]
    o = pl.pallas_call(
        lambda *refs: prepare_kernel(own, rows, depth, *refs),
        out_shape=[jax.ShapeDtypeStruct(s, d) for s, d in outs],
        in_specs=[hbm, hbm, pl.BlockSpec(memory_space=pltpu.SMEM)], out_specs=[vm] * len(outs),
        scratch_shapes=[pltpu.VMEM(keep.shape, keep.dtype), pltpu.SemaphoreType.DMA((depth * own + 1,))],
        compiler_params=pltpu.CompilerParams(vmem_limit_bytes=8 * MIB),
        cost_estimate=pl.CostEstimate(flops=1_000_000, bytes_accessed=1000, transcendentals=0),
        name="prepare",
    )(in_hbm(patches), in_hbm(keep), valid)
    return o[0], o[1::2], o[2::2]


def vectors_kernel(own, mapw, cot, *refs):
    half = (len(refs) - 4) // 2
    sources, vec, mb, cm, held, sems = refs[:half], refs[half], refs[half + 1], refs[half + 2], refs[half + 3:-1], refs[-1]
    copies = [pltpu.make_async_copy(a, b, sems.at[i]) for i, (a, b) in enumerate(zip(sources, held))]
    for copy in copies:
        copy.start()
    vec[...] = jnp.zeros_like(vec)
    me = lax.axis_index("seq")
    for i in range(own):
        cm[i] = jnp.concatenate([mapw[...].astype(f32), cot[me * own + i].astype(f32)], axis=0).astype(bf)
    for copy in copies:
        copy.wait()
    width, tokens = vec.shape[1], mb.shape[0]
    line = 0
    for ref in held[:-1]:
        for j in range(ref.shape[0] // width):
            vec[line, :] = ref[width * j:width * (j + 1)].astype(f32)
            line += 1
    bias = jnp.broadcast_to(held[-1][...].astype(f32).reshape(1, tokens), (tokens, tokens))
    diag = lax.broadcasted_iota(jnp.int32, (tokens, tokens), 0) == lax.broadcasted_iota(jnp.int32, (tokens, tokens), 1)
    mb[...] = jnp.broadcast_to(jnp.sum(jnp.where(diag, bias, 0.0), axis=1, keepdims=True), mb.shape)


def vectors_call(own, mapw, cot, *sources):
    width, tokens = sources[0].shape[0], sources[-1].shape[0]
    vm, hbm = pl.BlockSpec(memory_space=pltpu.VMEM), pl.BlockSpec(memory_space=pltpu.HBM)
    outs = [((16, width), f32), ((tokens, 128), f32), ((own, 2 * tokens, width), bf)]
    return pl.pallas_call(
        lambda *refs: vectors_kernel(own, *refs),
        out_shape=[jax.ShapeDtypeStruct(s, d) for s, d in outs],
        in_specs=[vm] * 2 + [hbm] * len(sources), out_specs=[vm] * 3,
        scratch_shapes=[pltpu.VMEM(s.shape, s.dtype) for s in sources] + [pltpu.SemaphoreType.DMA((len(sources),))],
        compiler_params=pltpu.CompilerParams(vmem_limit_bytes=4 * MIB),
        cost_estimate=pl.CostEstimate(flops=1_000_000, bytes_accessed=1000, transcendentals=0),
        name="vectors",
    )(mapw, cot, *map(in_hbm, sources))


def plus_kernel(a, b, out):
    out[...] = a[...] + b[...]


def unpack_kernel(hidden, own, base, a0, a1, sm_ref, rider, count_ref, gdn, gup, down, outb, gain, shift, upb, mapw, mapb, learned, penalty, a_s):
    side = lax.axis_index("dp") & 1
    half, width = a0.shape
    a_s[pl.ds(pl.multiple_of(side * half, 16), half), :] = a0[...]
    a_s[pl.ds(pl.multiple_of((1 - side) * half, 16), half), :] = a1[...]
    blocks = hidden // width
    for j in range(blocks):
        js = slice(width * j, width * (j + 1))
        gdn[js, :] = a_s[js, :].T.astype(f32)
        gup[:, js] = a_s[width * (blocks + j):width * (blocks + j + 1), :].astype(f32)
    for i, ref in enumerate((down, outb, gain, shift)):
        ref[...] = sm_ref[i, :]
    for j in range(blocks):
        upb[width * j:width * (j + 1)] = sm_ref[4 + j, :]
    mapw[...] = sm_ref[8:16, :]
    tokens = learned.shape[1]
    penalty[...] = sm_ref[16:17, tokens:tokens + 1] / count_ref[0:1, 0:1]
    mapb[...] = sm_ref[16, 0:tokens]
    count = own * tokens
    depth = learned.shape[0] // own
    bits = depth.bit_length() - 1
    for z in range(depth):
        place = sum(((z >> b) & 1) << (bits - 1 - b) for b in range(bits))
        span = count + -count % 16
        at = base + 2 * span * place
        both = rider[at:at + span, :].astype(f32) + rider[at + span:at + 2 * span, :].astype(f32)
        for i in range(own):
            learned[z * own + i] = both[tokens * i:tokens * (i + 1), :]


def unpack_call(hidden, tokens, images, own, base, a0, a1, sm, rider, count):
    width = a0.shape[1]
    vm = pl.BlockSpec(memory_space=pltpu.VMEM)
    outs = [(hidden, width), (width, hidden)] + [(width,)] * 4 + [(hidden,), (tokens, width), (tokens,)]
    outs += [(images, tokens, width), (1, 1)]
    return pl.pallas_call(
        lambda *refs: unpack_kernel(hidden, own, base, *refs),
        out_shape=[jax.ShapeDtypeStruct(s, f32) for s in outs],
        in_specs=[vm] * 5, out_specs=[vm] * len(outs),
        scratch_shapes=[pltpu.VMEM((2 * a0.shape[0], width), bf)],
        compiler_params=pltpu.CompilerParams(vmem_limit_bytes=16 * MIB),
        cost_estimate=pl.CostEstimate(flops=1_000_000, bytes_accessed=1000, transcendentals=0),
        name="unpack",
    )(a0, a1, sm, rider, count)


def finish_kernel(b0, b1, sm_ref, gqkv, gout, gain, shift, biases, b_s):
    side = lax.axis_index("dp") & 1
    half, width = b0.shape
    b_s[pl.ds(pl.multiple_of(side * half, 16), half), :] = b0[...]
    b_s[pl.ds(pl.multiple_of((1 - side) * half, 16), half), :] = b1[...]
    for j in range(3):
        js = slice(width * j, width * (j + 1))
        gqkv[:, js] = b_s[js, :].astype(f32)
    gout[...] = b_s[3 * width:4 * width, :].astype(f32)
    gain[...] = sm_ref[0, :]
    shift[...] = sm_ref[1, :]
    for j in range(2):
        biases[width * j:width * (j + 1)] = sm_ref[2 + j, :]


def finish_call(b0, b1, sm):
    width = b0.shape[1]
    vm = pl.BlockSpec(memory_space=pltpu.VMEM)
    outs = [(width, 3 * width), (width, width), (width,), (width,), (2 * width,)]
    return pl.pallas_call(
        finish_kernel,
        out_shape=[jax.ShapeDtypeStruct(s, f32) for s in outs],
        in_specs=[vm] * 3, out_specs=[vm] * len(outs),
        scratch_shapes=[pltpu.VMEM((2 * b0.shape[0], width), bf)],
        compiler_params=pltpu.CompilerParams(vmem_limit_bytes=8 * MIB),
        cost_estimate=pl.CostEstimate(flops=1_000_000, bytes_accessed=1000, transcendentals=0),
        name="finish",
    )(b0, b1, sm)


def place_kernel(parts, bases, *refs):
    out = refs[-1]
    own, rows = len(bases) // parts, out.shape[1]
    me = lax.axis_index("seq")
    for i in range(own):
        for k in range(parts):
            base = bases[i * parts + k]
            out[(me ^ k) * own + i] = refs[i * parts + k][base:base + rows, :].astype(f32)


def place_call(sent, rows):
    own, parts = len(sent), len(sent[0])
    width = sent[0][0][0].shape[1]
    bases = [base for image in sent for _, base in image]
    return small_call(
        lambda *refs: place_kernel(parts, bases, *refs), [x for image in sent for x, _ in image],
        [((parts * own, rows, width), f32)], "place", 8)[0]


VM_A, VM_F, VM_B, VM_W = 10, 22, 14, 12


def xor_permute(x, axis, k):
    return lax.ppermute(x, axis, [(i, i ^ k) for i in range(lax.axis_size(axis))])


def after(x, *others):
    if not others:
        return x
    return lax.optimization_barrier((x,) + others)[0]


def plane_exchange(sends):
    return [xor_permute(x, "dp", (k + 1) << 1) for k, x in enumerate(sends)]


def to_peers(part, axis, count, shift):
    return [part] + [xor_permute(part, axis, k << shift) for k in range(1, count)]


def padded(rows, unit):
    return rows + -rows % unit


def per_device(
    patches, first_gain, first_shift, qkv_weight, query_value_bias, out_weight, out_bias,
    second_gain, second_shift, up_weight, up_bias, down_weight, down_bias, map_weight, map_bias,
    keep_mask, image_valid, token_cotangent,
):
    images, rows, width = patches.shape
    depth, dps = lax.axis_size("seq"), lax.axis_size("dp")
    chips = dps // 2
    own = images // depth
    hidden, tokens = up_weight.shape[1], map_weight.shape[1]
    pairs = width // 128
    unit = 16 * dps * depth
    rows_a, rows_b = padded(2 * hidden, unit), padded(4 * width, unit)

    count, first_blocks, rest_blocks = prepare_call(depth, patches, keep_mask, image_valid)
    order = sorted(range(1, depth), key=lambda k: (k == 1, k))

    def collect(blocks, holds):
        got = [blocks[0]] + [None] * (depth - 1)
        for k in order:
            got[k] = xor_permute(after(blocks[k], *holds), "seq", k)
        return got

    first = collect(first_blocks, [])
    vec, mb, cm = vectors_call(
        own, map_weight.T, token_cotangent, first_gain, first_shift, query_value_bias, out_bias, second_gain,
        second_shift, down_bias, up_bias, map_bias)
    plus = lambda a, b: small_call(plus_kernel, (a, b), [((8, 128), f32)], "plus", 1)[0]
    step, holds = 1, list(first[1:])
    while step < dps:
        if step == 2:
            count = after(count, vec)
        if step == dps // 2:
            holds.append(count)
            count_got = xor_permute(count, "dp", step)
        else:
            count = plus(count, xor_permute(count, "dp", step))
        step *= 2
    rest = collect(rest_blocks, holds)

    saved, learns = [], []
    bases = [0] + [rows * i for i in range(own - 1)]
    acc = dwo = sm = tok = None
    for i in range(own):
        v = vec if tok is None else after(vec, tok)
        qa, key, val, caug, att, mid = attend_call(
            first if i == 0 else rest, first, i, bases[i], rows, v, qkv_weight, out_weight)
        if i == 0:
            count = plus(after(count, caug), count_got)
        gm, doa, learn, acc, dwo, sm = feed_call(
            i, own, rows_a, mid, att, caug, vec, mb, cm, image_valid, count,
            out_weight, up_weight, down_weight, acc, dwo, sm)
        tok = sm
        saved.append((qa, key, val, doa, caug, gm))
        learns.append(learn)

    got = xor_permute(core_call(acc, sm), "dp", 1)
    bits = depth.bit_length() - 1
    dms, sums, nrms, sent = [], [], [], []
    for i in range(own):
        qa, key, val, doa, caug, gm = saved[i]
        mine = (first if i == 0 else rest) if i < own - 1 else ()
        started = ()
        if i == 0:
            started = start_call(qa, key, val, doa, after(caug, tok))
            sends, kept, small = plane_call(acc, after(sm, started[1]), got, chips)
            gots = plane_exchange(sends)
            tok = small
        o = back_call((qa, key, val, doa, after(caug, tok)), rows, bases[i], vec, qkv_weight, mine, gm, started)
        dms.append(o[0])
        sums.append(o[1])
        tok = o[1]
        leaving = o[2:2 + depth]
        if i < own - 1:
            nrms.append(o[-1])
        if i == own - 2:
            riders = [s[1][0] for s in sent]
            send, kept, small = halve_call(
                kept, after(small, tok, *[x for s in sent for x, _ in s[2:]]), gots, 0, riders)
            got = xor_permute(send, "seq", 1)
            base = kept.shape[0] + 2 * small.shape[0]
            for m, s in enumerate(sent):
                s[1] = (got, base + rows * m)
            tok = small
        if i < own - 1:
            near = (xor_permute(leaving[1], "seq", 1), 0) if i == own - 2 else (leaving[1], 0)
            far = [(xor_permute(x, "seq", k), 0) for k, x in enumerate(leaving) if k > 1]
            sent.append([(leaving[0], 0), near] + far)
    for bit in range(1, bits):
        send, kept, small = halve_call(kept, after(small, tok), [got], bit)
        got = xor_permute(send, "seq", 1 << bit)
        tok = small
    o = last_call(rows_b, rows, bases[-1], rest, saved[-1][5], after(vec, tok), qkv_weight, dms, sums, nrms, dwo)
    bigb, smb, tail = o[0], o[1], o[2:]
    early = [x for x, _ in sent[-1][1:]]
    part, small = spread_call(kept, small, got, learns)
    gotb = xor_permute(core_call(bigb, after(smb, small)), "dp", 1)
    size, riding = kept.shape[0], learned_rows(learns)
    got = xor_permute(part, "seq", depth // 2)
    sends, keptb, smallb = plane_call(bigb, smb, gotb, chips)
    gotsb = plane_exchange(sends)
    smallb = after(smallb, *early)
    steps = list(reversed(range(bits)))
    for m, bit in enumerate(steps):
        send, keptb, smallb = halve_call(keptb, smallb, gotsb, bit)
        gotsb = [xor_permute(send, "seq", 1 << bit)]
        part = join_call([after(part, smallb), got], "seq", bit, size, riding)
        size, riding = 2 * size, 2 * riding
        if bit:
            got = xor_permute(part, "seq", 1 << (bit - 1))
    rider = part
    peers = to_peers(first_rows(part, size), "dp", chips, 1)
    late = [tail[0]] + [xor_permute(after(x, smallb), "seq", k) for k, x in enumerate(tail) if k and k % 2 == 0]
    partb, smallb = spread_call(keptb, smallb, gotsb[0])
    odd = [xor_permute(after(x, smallb), "seq", k) for k, x in enumerate(tail) if k % 2]
    for bit in range(bits):
        pair = [partb, xor_permute(partb, "seq", 1 << bit)]
        partb = join_call([after(partb, *(late[1:] if bit == 0 else odd)), pair[1]], "seq", bit, partb.shape[0])
    sent.append([(x, 0) for both in zip(late, odd) for x in both])
    outs = place_call(sent, rows)
    part = join_call([after(peers[0], partb)] + peers[1:], "dp", 1, size)
    a0, a1 = part, xor_permute(part, "dp", 1)
    unpacked = unpack_call(hidden, tokens, images, own, size, a0, a1, small, rider, count)
    gdn, gup, gb_down, gb_out, g_gain2, g_shift2, gb_up, gmapw, gmapb, learned, penalty = unpacked
    peers = to_peers(partb, "dp", chips, 1)
    partb = join_call([after(peers[0], gmapw, outs)] + peers[1:], "dp", 1, partb.shape[0])
    b0, b1 = partb, xor_permute(partb, "dp", 1)
    gqkv, gout, g_gain1, g_shift1, gqv = finish_call(b0, b1, smallb)
    return (
        learned, penalty.reshape(()), outs, g_gain1, g_shift1, gqkv, gqv, gout, gb_out, g_gain2, g_shift2, gup,
        gb_up, gdn, gb_down, gmapw.T, gmapb,
    )


def solution(mesh):
    rep = P()
    placed = (P("dp", "seq", None),) + (rep,) * 14 + (P("dp", "seq"), P("dp"), P("dp", None, None))
    return jax.shard_map(
        per_device, mesh=mesh, in_specs=placed,
        out_specs=(P("dp", None, None), rep, P("dp", "seq", None)) + (rep,) * 14,
        check_vma=False,
    )
```

```python
import jax
import jax.numpy as jnp
from jax import lax
from jax.experimental import pallas as pl
from jax.experimental.pallas import tpu as pltpu
from jax.sharding import PartitionSpec as P

f32, bf = jnp.float32, jnp.bfloat16
EPSILON = 1e-6
MASKED = -1e30
MIB = 1 << 20


def in_hbm(x):
    return pltpu.with_memory_space_constraint(x, pltpu.HBM)


def mm(a, b):
    return lax.dot_general(a, b, (((1,), (0,)), ((), ())), preferred_element_type=f32)


def mm_nt(a, b):
    return lax.dot_general(a, b, (((1,), (1,)), ((), ())), preferred_element_type=f32)


def mm_tn(a, b):
    return lax.dot_general(a, b, (((0,), (0,)), ((), ())), preferred_element_type=f32)


def row_mean(x):
    return jnp.sum(x, axis=-1, keepdims=True) * (1.0 / x.shape[-1])


def normalise(x):
    centred = x - row_mean(x)
    r = lax.rsqrt(row_mean(centred * centred) + EPSILON)
    return centred * r, r


def normal_parts(v):
    expo = jnp.exp(v * v * (-0.5))
    t = 1.0 / (1.0 + jnp.abs(v) * (0.3275911 * 0.7071067811865476))
    series = t * (0.127414796 + t * (-0.142248368 + t * (0.7107068705 + t * (-0.7265760135 + t * 0.5307027145))))
    tail = series * expo
    return jnp.where(v >= 0, 1.0 - tail, tail), expo * 0.3989422804014327


def split2(a):
    high = a.astype(bf)
    return high, (a - high.astype(f32)).astype(bf)


def columns(j, count, base=0):
    if isinstance(j, int):
        return slice(base + j * count, base + (j + 1) * count)
    return pl.ds(pl.multiple_of(base + j * count, 128), count)


def row_at(j):
    return slice(j, j + 1) if isinstance(j, int) else pl.ds(j, 1)


def repeat(first, last, body, straight):
    if straight:
        for j in range(first, last):
            body(j, 0)
    else:
        lax.fori_loop(first, last, body, 0)


def row_counts(n):
    return [c for c in (384,) if c < n] + [n]


def for_rows(count, n, body):
    below = 0.0
    for c in row_counts(n):
        pl.when((count > below) & (count <= float(c)))(lambda c=c: body(c))
        below = float(c)


def kept_count(slots):
    return jnp.max(slots[4:5, 0:128])


def mover(slots, i, c, rows):
    at = lax.broadcasted_iota(jnp.int32, (c, rows), 0).astype(f32)
    return jnp.where(at == slots[i:i + 1, 0:rows], 1.0, 0.0).astype(bf)


def attend_kernel(parts, rows, slot, base, *refs):
    x_refs, flag_refs = refs[:parts], refs[parts:2 * parts]
    vec_ref, wqkv, wout = refs[2 * parts:2 * parts + 3]
    qa_ref, k_ref, v_ref, caug_ref, att_ref, mid_ref, x_ref, slots = refs[2 * parts + 3:2 * parts + 11]
    nrm_s, q_s = refs[2 * parts + 11:]
    n, width = nrm_s.shape
    vec = lambda i: vec_ref[i:i + 1, :]
    before = lax.broadcasted_iota(jnp.int32, (rows, rows), 0) < lax.broadcasted_iota(jnp.int32, (rows, rows), 1)
    before = jnp.where(before, 1.0, 0.0).astype(bf)
    total = jnp.zeros((1, 1), f32)
    slots[...] = jnp.full(slots.shape, -1.0, f32)
    for i in range(parts):
        keep = flag_refs[i][rows:rows + 16, 0:rows].astype(f32)[slot:slot + 1, :]
        rank = mm(jnp.broadcast_to(keep, (8, rows)).astype(bf), before)[0:1, :] + total
        slots[i:i + 1, 0:rows] = jnp.where(keep > 0.0, rank, -1.0)
        total = total + jnp.sum(keep, axis=-1, keepdims=True)
    slots[4:5, :] = jnp.broadcast_to(total, (1, slots.shape[1]))

    def body(c):
        x = None
        for i in range(parts):
            t = mm(mover(slots, i, c, rows), x_refs[i][base:base + rows, :])
            x = t if x is None else x + t
        x_ref[0:c, :] = x.astype(bf)
        xh, _ = normalise(x)
        nrm_s[0:c, :] = (xh * vec(0) + vec(1)).astype(bf)
        nrm = nrm_s[0:c, :]
        q_s[0:c, :] = (mm(nrm, wqkv[:, 0:width]) + vec(2)).astype(bf) * jnp.asarray(0.125, bf)
        k_ref[0:c, :] = mm(nrm, wqkv[:, width:2 * width]).astype(bf)
        v_ref[0:c, :] = (mm(nrm, wqkv[:, 2 * width:3 * width]) + vec(3)).astype(bf)
        lane = lax.broadcasted_iota(jnp.int32, (c, 128), 1)
        lane64 = lane & 63
        real = lax.broadcasted_iota(jnp.int32, (c, 128), 0).astype(f32) < slots[4:5, 0:128]
        caug_ref[0:c, :] = jnp.where(
            lane64 == 3, jnp.where(real, 0.0, MASKED), jnp.where(lane64 < 3, 1.0, 0.0)).astype(bf)
        ones = jnp.ones((c, 128), bf)
        def pair(j, carry):
            sl = columns(j, 128)
            outs = []
            for e in range(2):
                own = (lane < 64) if e == 0 else (lane >= 64)
                kp = jnp.where(own, k_ref[0:c, sl], caug_ref[0:c, :])
                qp = jnp.where(own, q_s[0:c, sl], jnp.where(lane64 == 3, 1.0, 0.0).astype(bf))
                s = mm_nt(qp, kp)
                m = jnp.max(s, axis=-1, keepdims=True)
                p = jnp.exp(s - m).astype(bf)
                o = mm(p, jnp.concatenate([v_ref[0:c, sl], ones], axis=1))
                whole = o[:, 128:256]
                outs.append(o[:, 0:128] / whole)
                logs = -(m + jnp.log(whole))
                hi = logs.astype(bf).astype(f32)
                lo = (logs - hi).astype(bf).astype(f32)
                aug = jnp.where(lane64 == 0, hi, jnp.where(lane64 == 1, lo, jnp.where(
                    lane64 == 2, logs - hi - lo, jnp.where(lane64 == 3, 1.0, 0.0))))
                qa_ref[0:c, columns(2 * j + e, 128)] = jnp.where(own, q_s[0:c, sl], aug.astype(bf))
            att_ref[0:c, sl] = jnp.where(lane < 64, outs[0], outs[1]).astype(bf)
            return carry

        repeat(0, width // 128, pair, c < n)
        mid_ref[0:c, :] = x_ref[0:c, :].astype(f32) + mm(att_ref[0:c, :], wout[...]) + vec(4)

    for_rows(kept_count(slots), n, body)


def attend_call(pieces, flags, slot, base, rows, vec, wqkv, wout):
    parts, width = len(pieces), wout.shape[0]
    n = parts * rows
    outs = [((n, 2 * width), bf), ((n, width), bf), ((n, width), bf), ((n, 128), bf), ((n, width), bf), ((n, width), f32)]
    outs += [((n, width), bf), ((8, 256), f32)]
    return small_call(
        lambda *refs: attend_kernel(parts, rows, slot, base, *refs), (*pieces, *flags, vec, wqkv, wout), outs, "attend",
        VM_A, scratch=[pltpu.VMEM((n, width), bf), pltpu.VMEM((n, width), bf)])


def feed_kernel(slot, own_count, first, *refs):
    mid_ref, att_ref, slots, vec_ref, mb_ref, cm_ref, valid_ref, count_ref, wout, wup, wdn = refs[:11]
    refs = refs[11:]
    if first:
        acc_in = dwo_in = sm_in = None
    else:
        acc_in, dwo_in, sm_in = refs[:3]
        refs = refs[3:]
    gm_ref, doa_ref, learn_ref, acc, dwo, sm = refs[:6]
    sec_s, hid_s, gp_s, g_s, total, gt_s, st_s = refs[6:]
    n, width = mid_ref.shape
    blocks = hid_s.shape[1] // width
    tokens = mb_ref.shape[0]
    vec = lambda i: vec_ref[i:i + 1, :]
    place = lax.axis_index("seq") * own_count + slot

    def add(ref, ref_in, rows, value):
        ref[rows, :] = value if first else ref_in[rows, :] + value

    def body(c):
        xh, _ = normalise(mid_ref[0:c, :])
        sec_s[0:c, :] = (xh * vec(5) + vec(6)).astype(bf)
        total[0:c, :] = mid_ref[0:c, :] + vec(7)

        def up(j, carry):
            js = columns(j, width)
            pre = mm(sec_s[0:c, :], wup[:, js]) + vec_ref[row_at(8 + j), :]
            upper, density = normal_parts(pre)
            hid_s[0:c, js] = (pre * upper).astype(bf)
            gp_s[0:c, js] = upper + pre * density
            total[0:c, :] = total[0:c, :] + mm(hid_s[0:c, js], wdn[js, :])
            return carry

        repeat(0, blocks, up, c < n)
        ohi, olo = split2(total[0:c, :])
        cm = cm_ref[slot]
        lg = mm_nt(cm, ohi) + mm_nt(cm, olo)
        kept = slots[4:5, 0:1]
        keep = jnp.where(lax.broadcasted_iota(jnp.int32, (1, c), 1).astype(f32) < kept, 1.0, 0.0)
        maps = jax.nn.sigmoid(lg[0:tokens, :] + mb_ref[:, 0:1])
        inverse = 1.0 / kept
        tot = jnp.sum(maps, axis=0, keepdims=True)
        inter = jnp.sum(keep * (tot * tot - jnp.sum(maps * maps, axis=0, keepdims=True)), axis=-1, keepdims=True)
        valid = valid_ref[place].astype(f32)
        gmaps = keep * (lg[tokens:2 * tokens, :] * inverse + (2.0 * valid / count_ref[0:1, 0:1]) * (tot - maps))
        gl = gmaps * maps * (1.0 - maps)
        mk = maps * keep
        mkh, mkl = split2(mk)
        glh, gll = split2(gl)
        st = jnp.concatenate([mkh.astype(f32), mkl.astype(f32), glh.astype(f32), gll.astype(f32)], axis=0).astype(bf)
        r1 = mm(st, ohi) + mm(st, olo)
        learn_ref[...] = (r1[0:tokens, :] + r1[tokens:2 * tokens, :]) * inverse
        add(sm, sm_in, slice(8, 16), r1[2 * tokens:3 * tokens, :] + r1[3 * tokens:, :])
        gah, gal = split2(mk * inverse)
        lhs = jnp.concatenate([glh.astype(f32), gah.astype(f32), gll.astype(f32), gal.astype(f32)], axis=0).astype(bf)
        g = mm_tn(lhs, jnp.concatenate([cm, cm], axis=0))
        g_s[0:c, :] = g
        add(sm, sm_in, slice(0, 1), jnp.sum(g, axis=0, keepdims=True))
        glow = g.astype(bf)
        gt_s[:, 0:c] = glow.T
        st_s[:, 0:c] = sec_s[0:c, :].T
        total[0:c, :] = jnp.zeros((c, width), f32)

        def down(j, carry):
            js = columns(j, width)
            gh = mm_nt(glow, wdn[js, :]).astype(bf).astype(f32)
            gpre = gh * gp_s[0:c, js]
            gpl = gpre.astype(bf)
            add(sm, sm_in, row_at(4 + j), jnp.sum(gpre, axis=0, keepdims=True))
            total[0:c, :] = total[0:c, :] + mm_nt(gpl, wup[:, js])
            add(acc, acc_in, js, mm(gt_s[:, 0:c], hid_s[0:c, js]))
            add(acc, acc_in, columns(j, width, blocks * width), mm(st_s[:, 0:c], gpl))
            return carry

        repeat(0, blocks, down, c < n)
        gsec = total[0:c, :]
        xh, r = normalise(mid_ref[0:c, :])
        gg = gsec * vec(5)
        gm = g_s[0:c, :] + r * (gg - row_mean(gg) - xh * row_mean(gg * xh))
        gm_ref[0:c, :] = gm
        gml = gm.astype(bf)
        add(sm, sm_in, slice(1, 2), jnp.sum(gm, axis=0, keepdims=True))
        add(sm, sm_in, slice(2, 3), jnp.sum(gsec * xh, axis=0, keepdims=True))
        add(sm, sm_in, slice(3, 4), jnp.sum(gsec, axis=0, keepdims=True))
        glb = jnp.sum(gl, axis=-1, keepdims=True)
        lr = lax.broadcasted_iota(jnp.int32, (8, width), 1)
        rr = lax.broadcasted_iota(jnp.int32, (8, width), 0)
        line = jnp.sum(jnp.where(lr == rr, glb, 0.0), axis=0, keepdims=True)
        line = line + jnp.where(lr[0:1] == tokens, valid * inter * (1.0 / n), 0.0)
        add(sm, sm_in, slice(16, 24), jnp.where(rr == 0, line, 0.0))
        if first:
            sm[24:32, :] = jnp.zeros((8, width), f32)
            if acc.shape[0] > 2 * blocks * width:
                acc[2 * blocks * width:, :] = jnp.zeros((acc.shape[0] - 2 * blocks * width, width), f32)
        else:
            sm[24:32, :] = sm_in[24:32, :]
            if acc.shape[0] > 2 * blocks * width:
                acc[2 * blocks * width:, :] = acc_in[2 * blocks * width:, :]
        add(dwo, dwo_in, slice(0, width), mm(att_ref[0:c, :].T, gml))
        do = mm_nt(gml, wout[...]).astype(bf).astype(f32)
        lane = lax.broadcasted_iota(jnp.int32, (c, 128), 1)
        lane64 = lane & 63
        for j in range(width // 128):
            sl = slice(128 * j, 128 * j + 128)
            dj = do[:, sl]
            pd = dj * att_ref[0:c, sl].astype(f32)
            for e in range(2):
                own = (lane < 64) if e == 0 else (lane >= 64)
                dl = -jnp.sum(jnp.where(own, pd, 0.0), axis=-1, keepdims=True)
                hi = dl.astype(bf).astype(f32)
                aug = jnp.where(lane64 == 0, hi, jnp.where(lane64 == 1, dl - hi, 0.0))
                h = 2 * j + e
                doa_ref[0:c, 128 * h:128 * h + 128] = jnp.where(own, dj, aug).astype(bf)

    for_rows(kept_count(slots), n, body)


def feed_call(slot, own_count, packed_rows, mid, att, slots, vec, mb, cm, valid, count, wout, wup, wdn, acc, dwo, sm):
    n, width = mid.shape
    hidden = wup.shape[1]
    first = acc is None
    vm = pl.BlockSpec(memory_space=pltpu.VMEM)
    smem = pl.BlockSpec(memory_space=pltpu.SMEM)
    outs = [((n, width), f32), ((n, 2 * width), bf), ((8, width), f32), ((packed_rows, width), f32), ((width, width), f32), ((32, width), f32)]
    args = (mid, att, slots, vec, mb, cm, valid, count, wout, wup, wdn)
    extra = () if first else (acc, dwo, sm)
    return pl.pallas_call(
        lambda *refs: feed_kernel(slot, own_count, first, *refs),
        out_shape=[jax.ShapeDtypeStruct(s, d) for s, d in outs],
        in_specs=[vm] * 6 + [smem] + [vm] * (4 + len(extra)), out_specs=[vm] * 6,
        input_output_aliases={} if first else {11: 3, 12: 4, 13: 5},
        scratch_shapes=[pltpu.VMEM((n, width), bf), pltpu.VMEM((n, hidden), bf), pltpu.VMEM((n, hidden), f32), pltpu.VMEM((n, width), f32)]
        + [pltpu.VMEM((n, width), f32), pltpu.VMEM((width, n), bf), pltpu.VMEM((width, n), bf)],
        compiler_params=pltpu.CompilerParams(vmem_limit_bytes=VM_F * MIB),
        cost_estimate=pl.CostEstimate(flops=1_000_000, bytes_accessed=1000, transcendentals=0),
        name="feed",
    )(*args, *extra)


def scores_back(js, c, qa, k_ref, v_ref, doa, caug, dm, sums):
    width = k_ref.shape[1]
    step = 192 if c % 192 == 0 else c
    lane = lax.broadcasted_iota(jnp.int32, (step, 128), 1)
    ones = jnp.ones((step, 128), bf)
    def pair(j, carry):
        sl = columns(j, 128)
        k_t = k_ref[0:c, sl].T
        dqt = [None, None]
        dvsum = None
        for start in range(0, c, step):
            cs = slice(start, start + step)
            dvs, dks = [], []
            for e in range(2):
                hs = columns(2 * j + e, 128)
                own = (lane < 64) if e == 0 else (lane >= 64)
                kp = jnp.where(own, k_ref[cs, sl], caug[cs, :])
                vp = jnp.where(own, v_ref[cs, sl], ones)
                p = jnp.exp(mm_nt(kp, qa[0:c, hs]))
                ds = (p * mm_nt(vp, doa[0:c, hs])).astype(bf)
                dvs.append(mm(p.astype(bf), doa[0:c, hs]))
                dks.append(mm(ds, qa[0:c, hs]))
                t = mm(k_t[64 * e:64 * e + 64, cs], ds)
                dqt[e] = t if dqt[e] is None else dqt[e] + t
            dm[cs, columns(j, 128, width)] = jnp.where(lane < 64, dks[0], dks[1]).astype(bf)
            dv = jnp.where(lane < 64, dvs[0], dvs[1])
            dm[cs, columns(j, 128, 2 * width)] = dv.astype(bf)
            s = jnp.sum(dv, axis=0, keepdims=True)
            dvsum = s if dvsum is None else dvsum + s
        dq = jnp.concatenate(dqt, axis=0).T * 0.125
        dm[0:c, sl] = dq.astype(bf)
        sums[0:1, sl] = jnp.sum(dq, axis=0, keepdims=True)
        sums[1:2, sl] = dvsum
        return carry

    lax.fori_loop(js[0], js[-1] + 1, pair, 0)


def norm_back(c, slots, x_ref, gm, dm, vec_ref, wqkv, g_refs, nrm_ref):
    vec = lambda i: vec_ref[i:i + 1, :]
    gf = mm_nt(dm[0:c, :], wqkv[...])
    xh, r = normalise(x_ref[0:c, :].astype(f32))
    nrm_ref[0:c, :] = (xh * vec(0) + vec(1)).astype(bf)
    gg = gf * vec(0)
    gx = (gm[0:c, :] + r * (gg - row_mean(gg) - xh * row_mean(gg * xh))).astype(bf)
    for i, ref in enumerate(g_refs):
        ref[...] = mm_tn(mover(slots, i, c, ref.shape[0]), gx).astype(bf)
    return jnp.sum(gf * xh, axis=0, keepdims=True), jnp.sum(gf, axis=0, keepdims=True)


def start_kernel(slots, qa, k_ref, v_ref, doa, caug, dm, sums):
    sums[...] = jnp.zeros_like(sums)
    for_rows(
        kept_count(slots), k_ref.shape[0], lambda c: scores_back([0], c, qa, k_ref, v_ref, doa, caug, dm, sums))


def start_call(slots, *attn):
    n, width = attn[1].shape
    return small_call(start_kernel, (slots, *attn), [((n, 3 * width), bf), ((8, width), f32)], "start", VM_B)


def back_kernel(parts, started, *refs):
    slots, attn, (vec_ref, wqkv, x_ref, gm) = refs[0], refs[1:6], refs[6:10]
    refs = refs[10:]
    if started:
        dm0, sums0 = refs[:2]
        refs = refs[2:]
    dm, sums = refs[:2]
    n, width = gm.shape

    def body(c):
        pairs = range(width // 128)
        if started:
            sums[...] = sums0[...]
            for s in range(3):
                dm[0:c, width * s:width * s + 128] = dm0[0:c, width * s:width * s + 128]
            pairs = pairs[1:]
        else:
            sums[...] = jnp.zeros_like(sums)
        scores_back(pairs, c, *attn, dm, sums)
        if parts:
            gain, shift = norm_back(c, slots, x_ref, gm, dm, vec_ref, wqkv, refs[2:2 + parts], refs[-1])
            sums[2:3, :] = gain
            sums[3:4, :] = shift

    for_rows(kept_count(slots), n, body)


def back_call(slots, attn, rows, parts, vec, wqkv, x, gm, started=()):
    n, width = attn[1].shape
    outs = [((n, 3 * width), bf), ((8, width), f32)]
    if parts:
        outs += [((rows, width), bf)] * parts + [((n, width), bf)]
    return small_call(
        lambda *refs: back_kernel(parts, len(started) > 0, *refs),
        (slots, *attn, vec, wqkv, x, gm, *started), outs, "back", VM_B)


def last_kernel(parts, own, *refs):
    x_ref, gm, vec_ref, wqkv, dwo = refs[:5]
    refs = refs[5:]
    slots, dms, sums, nrms = refs[:own], refs[own:2 * own], refs[2 * own:3 * own], list(refs[3 * own:4 * own - 1])
    packed, sm, g_refs, nrm_s = refs[4 * own - 1], refs[4 * own], refs[4 * own + 1:-1], refs[-1]
    n, width = gm.shape
    nrms.append(nrm_s)
    total = sum(ref[0:4, :] for ref in sums)
    sm[...] = jnp.zeros_like(sm)
    sm[2:4, :] = total[0:2, :]

    def finish(c):
        gain, shift = norm_back(c, slots[-1], x_ref, gm, dms[-1], vec_ref, wqkv, g_refs, nrm_s)
        sm[0:1, :] = total[2:3, :] + gain
        sm[1:2, :] = total[3:4, :] + shift

    for_rows(kept_count(slots[-1]), n, finish)
    for i in range(own):

        def add(c, i=i):
            nrm_t = nrms[i][0:c, :].T

            def block(s, carry):
                js = columns(s, width)
                value = mm(nrm_t, dms[i][0:c, js])
                packed[js, :] = value if i == 0 else packed[js, :] + value
                return carry

            lax.fori_loop(0, 3, block, 0)

        for_rows(kept_count(slots[i]), n, add)
    packed[3 * width:4 * width, :] = dwo[...]
    if packed.shape[0] > 4 * width:
        packed[4 * width:, :] = jnp.zeros((packed.shape[0] - 4 * width, width), f32)


def last_call(packed_rows, rows, parts, x, gm, vec, wqkv, slots, dms, sums, nrms, dwo):
    own = len(dms)
    n, width = gm.shape
    outs = [((packed_rows, width), f32), ((16, width), f32)] + [((rows, width), bf)] * parts
    return small_call(
        lambda *refs: last_kernel(parts, own, *refs), (x, gm, vec, wqkv, dwo, *slots, *dms, *sums, *nrms), outs, "last",
        VM_W, scratch=[pltpu.VMEM((n, width), bf)])


def aligned(start, rows):
    return pl.ds(pl.multiple_of(start, 16), rows)


def tree_sum(parts):
    while len(parts) > 1:
        parts = [parts[i] + parts[i + 1] for i in range(0, len(parts), 2)]
    return parts[0]


def store_small(ref, at, small):
    rows = small.shape[0]
    high = small.astype(bf)
    ref[at:at + rows, :] = high
    ref[at + rows:at + 2 * rows, :] = (small - high.astype(f32)).astype(bf)


def load_small(ref, at, rows):
    return ref[at:at + rows, :].astype(f32) + ref[at + rows:at + 2 * rows, :].astype(f32)


def rounded(small):
    high, low = split2(small)
    return high.astype(f32) + low.astype(f32)


def core_kernel(big, small, out):
    half = big.shape[0] // 2
    other = 1 - (lax.axis_index("dp") & 1)
    out[0:half, :] = big[aligned(other * half, half), :].astype(bf)
    store_small(out, half, small[...])


def core_call(big, small):
    rows, width = big.shape
    return small_call(core_kernel, (big, small), [((rows // 2 + 2 * small.shape[0], width), bf)], "core", 4)[0]


def plane_kernel(big, small, got, *outs):
    sends, keep, total = outs[:-2], outs[-2], outs[-1]
    half, rows = big.shape[0] // 2, keep.shape[0]
    dp = lax.axis_index("dp")
    base, mine = (dp & 1) * half, dp >> 1
    summed = rounded(small[...]) + load_small(got, half, small.shape[0])
    total[...] = summed
    for k in range(len(sends) + 1):
        at = (mine ^ k) * rows
        value = big[aligned(base + at, rows), :] + got[aligned(at, rows), :].astype(f32)
        if k == 0:
            keep[...] = value
        else:
            sends[k - 1][0:rows, :] = value.astype(bf)
            store_small(sends[k - 1], rows, summed)


def plane_call(big, small, got, count):
    width, s = big.shape[1], small.shape[0]
    rows = big.shape[0] // 2 // count
    outs = [((rows + 2 * s, width), bf)] * (count - 1) + [((rows, width), f32), ((s, width), f32)]
    o = small_call(plane_kernel, (big, small, got), outs, "plane", 4)
    return o[:count - 1], o[-2], o[-1]


def halve_kernel(shift, count, rider, *refs):
    kept, small, gots, riding = refs[0], refs[1], refs[2:2 + count], refs[2 + count:2 + count + rider]
    send, keep, total = refs[2 + count + rider:]
    whole, rows, s = kept.shape[0], keep.shape[0], small.shape[0]
    mine = (lax.axis_index("seq") >> shift) & 1
    summed = tree_sum([rounded(small[...])] + [load_small(got, whole, s) for got in gots])
    total[...] = summed
    for k in range(2):
        at = (mine ^ k) * rows
        value = tree_sum([kept[aligned(at, rows), :]] + [got[aligned(at, rows), :].astype(f32) for got in gots])
        if k == 0:
            keep[...] = value
        else:
            send[0:rows, :] = value.astype(bf)
    store_small(send, rows, summed)
    at = rows + 2 * s
    for ref in riding:
        send[at:at + ref.shape[0], :] = ref[...]
        at += ref.shape[0]


def halve_call(kept, small, gots, shift, riders=()):
    width, s = kept.shape[1], small.shape[0]
    rows = kept.shape[0] // 2
    outs = [((rows + 2 * s + sum(x.shape[0] for x in riders), width), bf), ((rows, width), f32), ((s, width), f32)]
    return small_call(
        lambda *refs: halve_kernel(shift, len(gots), len(riders), *refs),
        (kept, small, *gots, *riders), outs, "halve", 6)


def spread_kernel(learns, rider, *refs):
    kept, small, got = refs[:3]
    learnt, riding = refs[3:3 + learns], refs[3 + learns:3 + learns + rider]
    total, part = refs[3 + learns + rider:]
    rows, s = kept.shape[0], small.shape[0]
    total[...] = rounded(small[...]) + load_small(got, rows, s)
    part[0:rows, :] = (kept[...] + got[0:rows, :].astype(f32)).astype(bf)
    at = rows
    if learns:
        used = sum(ref.shape[0] for ref in learnt)
        blank = [jnp.zeros((-used % 16, kept.shape[1]), f32)] if used % 16 else []
        learnt = jnp.concatenate([ref[...] for ref in learnt] + blank, axis=0)
        store_small(part, rows, learnt)
        at += 2 * learnt.shape[0]
    for ref in riding:
        part[at:at + ref.shape[0], :] = ref[...]
        at += ref.shape[0]


def learned_rows(learns):
    used = sum(ref.shape[0] for ref in learns)
    return 2 * (used + -used % 16)


def spread_call(kept, small, got, learns=(), riders=()):
    rows, width = kept.shape
    rows += learned_rows(learns) + sum(ref.shape[0] for ref in riders)
    outs = [(small.shape, f32), ((rows, width), bf)]
    total, part = small_call(
        lambda *refs: spread_kernel(len(learns), len(riders), *refs), (kept, small, got, *learns, *riders), outs, "spread", 6)
    return part, total


def join_kernel(axis, shift, rows, riding, count, extra, *refs):
    parts, extras, out = refs[:count], refs[count:count + extra], refs[count + extra]
    mine = (lax.axis_index(axis) >> shift) & (count - 1)
    for k, part in enumerate(parts):
        out[aligned((mine ^ k) * rows, rows), :] = part[0:rows, :]
        if riding:
            out[aligned(count * rows + (mine ^ k) * riding, riding), :] = part[rows:rows + riding, :]
    at = count * (rows + riding)
    for ref in extras:
        out[at:at + ref.shape[0], :] = ref[...]
        at += ref.shape[0]


def join_call(parts, axis, shift, rows, riding=0, extras=()):
    width = parts[0].shape[1]
    total = (rows + riding) * len(parts) + sum(x.shape[0] for x in extras)
    return small_call(
        lambda *refs: join_kernel(axis, shift, rows, riding, len(parts), len(extras), *refs), (*parts, *extras),
        [((total, width), bf)], "join", 6)[0]


def first_kernel(x, out):
    out[...] = x[0:out.shape[0], :]


def first_rows(x, rows):
    return small_call(first_kernel, (x,), [((rows, x.shape[1]), x.dtype)], "first", 4)[0]


def small_call(kernel, args, outs, name, mib, scratch=()):
    vm = pl.BlockSpec(memory_space=pltpu.VMEM)
    return pl.pallas_call(
        kernel,
        out_shape=[jax.ShapeDtypeStruct(s, d) for s, d in outs],
        in_specs=[vm] * len(args), out_specs=[vm] * len(outs), scratch_shapes=list(scratch),
        compiler_params=pltpu.CompilerParams(vmem_limit_bytes=mib * MIB),
        cost_estimate=pl.CostEstimate(flops=1_000_000, bytes_accessed=1000, transcendentals=0),
        name=name,
    )(*args)


def prepare_kernel(own, rows, depth, patches, keep, valid, count, *refs):
    blocks, (keep_s, sems) = refs[:2 * depth], refs[2 * depth:]
    width = patches.shape[2]
    me = lax.axis_index("seq")
    flags_copy = pltpu.make_async_copy(keep, keep_s, sems.at[depth * own])
    flags_copy.start()
    copies = []
    for k in [k for k in range(1, depth)] + [0]:
        for i in range(own):
            target = blocks[2 * k].at[0:rows, :] if i == 0 else blocks[2 * k + 1].at[rows * (i - 1):rows * i, :]
            copies.append(pltpu.make_async_copy(patches.at[(me ^ k) * own + i], target, sems.at[k * own + i]))
            copies[-1].start()
    total = valid[0]
    for i in range(1, valid.shape[0]):
        total = total + valid[i]
    count[...] = jnp.full(count.shape, total.astype(f32), f32)
    flags_copy.wait()
    line = lax.broadcasted_iota(jnp.int32, (16, rows), 0)
    for k in range(depth):
        flags = jnp.zeros((16, rows), f32)
        for i in range(own):
            flags = jnp.where(line == i, keep_s[pl.ds((me ^ k) * own + i, 1), :].astype(f32), flags)
        blocks[2 * k][rows:rows + 16, :] = jnp.zeros((16, width), bf)
        blocks[2 * k][rows:rows + 16, 0:rows] = flags.astype(bf)
    for copy in copies:
        copy.wait()


def prepare_call(depth, patches, keep, valid):
    images, rows, width = patches.shape
    own = images // depth
    vm, hbm = pl.BlockSpec(memory_space=pltpu.VMEM), pl.BlockSpec(memory_space=pltpu.HBM)
    outs = [((8, 128), f32)]
    for k in range(depth):
        outs += [((rows + 16, width), bf), ((rows * (own - 1), width), bf)]
    o = pl.pallas_call(
        lambda *refs: prepare_kernel(own, rows, depth, *refs),
        out_shape=[jax.ShapeDtypeStruct(s, d) for s, d in outs],
        in_specs=[hbm, hbm, pl.BlockSpec(memory_space=pltpu.SMEM)], out_specs=[vm] * len(outs),
        scratch_shapes=[pltpu.VMEM(keep.shape, keep.dtype), pltpu.SemaphoreType.DMA((depth * own + 1,))],
        compiler_params=pltpu.CompilerParams(vmem_limit_bytes=8 * MIB),
        cost_estimate=pl.CostEstimate(flops=1_000_000, bytes_accessed=1000, transcendentals=0),
        name="prepare",
    )(in_hbm(patches), in_hbm(keep), valid)
    return o[0], o[1::2], o[2::2]


def vectors_kernel(own, mapw, cot, *refs):
    half = (len(refs) - 4) // 2
    sources, vec, mb, cm, held, sems = refs[:half], refs[half], refs[half + 1], refs[half + 2], refs[half + 3:-1], refs[-1]
    copies = [pltpu.make_async_copy(a, b, sems.at[i]) for i, (a, b) in enumerate(zip(sources, held))]
    for copy in copies:
        copy.start()
    vec[...] = jnp.zeros_like(vec)
    me = lax.axis_index("seq")
    for i in range(own):
        cm[i] = jnp.concatenate([mapw[...].astype(f32), cot[me * own + i].astype(f32)], axis=0).astype(bf)
    for copy in copies:
        copy.wait()
    width, tokens = vec.shape[1], mb.shape[0]
    line = 0
    for ref in held[:-1]:
        for j in range(ref.shape[0] // width):
            vec[line, :] = ref[width * j:width * (j + 1)].astype(f32)
            line += 1
    bias = jnp.broadcast_to(held[-1][...].astype(f32).reshape(1, tokens), (tokens, tokens))
    diag = lax.broadcasted_iota(jnp.int32, (tokens, tokens), 0) == lax.broadcasted_iota(jnp.int32, (tokens, tokens), 1)
    mb[...] = jnp.broadcast_to(jnp.sum(jnp.where(diag, bias, 0.0), axis=1, keepdims=True), mb.shape)


def vectors_call(own, mapw, cot, *sources):
    width, tokens = sources[0].shape[0], sources[-1].shape[0]
    vm, hbm = pl.BlockSpec(memory_space=pltpu.VMEM), pl.BlockSpec(memory_space=pltpu.HBM)
    outs = [((16, width), f32), ((tokens, 128), f32), ((own, 2 * tokens, width), bf)]
    return pl.pallas_call(
        lambda *refs: vectors_kernel(own, *refs),
        out_shape=[jax.ShapeDtypeStruct(s, d) for s, d in outs],
        in_specs=[vm] * 2 + [hbm] * len(sources), out_specs=[vm] * 3,
        scratch_shapes=[pltpu.VMEM(s.shape, s.dtype) for s in sources] + [pltpu.SemaphoreType.DMA((len(sources),))],
        compiler_params=pltpu.CompilerParams(vmem_limit_bytes=4 * MIB),
        cost_estimate=pl.CostEstimate(flops=1_000_000, bytes_accessed=1000, transcendentals=0),
        name="vectors",
    )(mapw, cot, *map(in_hbm, sources))


def plus_kernel(a, b, out):
    out[...] = a[...] + b[...]


def unpack_kernel(hidden, own, base, a0, a1, sm_ref, rider, count_ref, gdn, gup, down, outb, gain, shift, upb, mapw, mapb, learned, penalty, a_s):
    side = lax.axis_index("dp") & 1
    half, width = a0.shape
    a_s[pl.ds(pl.multiple_of(side * half, 16), half), :] = a0[...]
    a_s[pl.ds(pl.multiple_of((1 - side) * half, 16), half), :] = a1[...]
    blocks = hidden // width
    for j in range(blocks):
        js = slice(width * j, width * (j + 1))
        gdn[js, :] = a_s[js, :].T.astype(f32)
        gup[:, js] = a_s[width * (blocks + j):width * (blocks + j + 1), :].astype(f32)
    for i, ref in enumerate((down, outb, gain, shift)):
        ref[...] = sm_ref[i, :]
    for j in range(blocks):
        upb[width * j:width * (j + 1)] = sm_ref[4 + j, :]
    mapw[...] = sm_ref[8:16, :]
    tokens = learned.shape[1]
    penalty[...] = sm_ref[16:17, tokens:tokens + 1] / count_ref[0:1, 0:1]
    mapb[...] = sm_ref[16, 0:tokens]
    count = own * tokens
    depth = learned.shape[0] // own
    bits = depth.bit_length() - 1
    for z in range(depth):
        place = sum(((z >> b) & 1) << (bits - 1 - b) for b in range(bits))
        span = count + -count % 16
        at = base + 2 * span * place
        both = rider[at:at + span, :].astype(f32) + rider[at + span:at + 2 * span, :].astype(f32)
        for i in range(own):
            learned[z * own + i] = both[tokens * i:tokens * (i + 1), :]


def unpack_call(hidden, tokens, images, own, base, a0, a1, sm, rider, count):
    width = a0.shape[1]
    vm = pl.BlockSpec(memory_space=pltpu.VMEM)
    outs = [(hidden, width), (width, hidden)] + [(width,)] * 4 + [(hidden,), (tokens, width), (tokens,)]
    outs += [(images, tokens, width), (1, 1)]
    return pl.pallas_call(
        lambda *refs: unpack_kernel(hidden, own, base, *refs),
        out_shape=[jax.ShapeDtypeStruct(s, f32) for s in outs],
        in_specs=[vm] * 5, out_specs=[vm] * len(outs),
        scratch_shapes=[pltpu.VMEM((2 * a0.shape[0], width), bf)],
        compiler_params=pltpu.CompilerParams(vmem_limit_bytes=16 * MIB),
        cost_estimate=pl.CostEstimate(flops=1_000_000, bytes_accessed=1000, transcendentals=0),
        name="unpack",
    )(a0, a1, sm, rider, count)


def finish_kernel(b0, b1, sm_ref, gqkv, gout, gain, shift, biases, b_s):
    side = lax.axis_index("dp") & 1
    half, width = b0.shape
    b_s[pl.ds(pl.multiple_of(side * half, 16), half), :] = b0[...]
    b_s[pl.ds(pl.multiple_of((1 - side) * half, 16), half), :] = b1[...]
    for j in range(3):
        js = slice(width * j, width * (j + 1))
        gqkv[:, js] = b_s[js, :].astype(f32)
    gout[...] = b_s[3 * width:4 * width, :].astype(f32)
    gain[...] = sm_ref[0, :]
    shift[...] = sm_ref[1, :]
    for j in range(2):
        biases[width * j:width * (j + 1)] = sm_ref[2 + j, :]


def finish_call(b0, b1, sm):
    width = b0.shape[1]
    vm = pl.BlockSpec(memory_space=pltpu.VMEM)
    outs = [(width, 3 * width), (width, width), (width,), (width,), (2 * width,)]
    return pl.pallas_call(
        finish_kernel,
        out_shape=[jax.ShapeDtypeStruct(s, f32) for s in outs],
        in_specs=[vm] * 3, out_specs=[vm] * len(outs),
        scratch_shapes=[pltpu.VMEM((2 * b0.shape[0], width), bf)],
        compiler_params=pltpu.CompilerParams(vmem_limit_bytes=8 * MIB),
        cost_estimate=pl.CostEstimate(flops=1_000_000, bytes_accessed=1000, transcendentals=0),
        name="finish",
    )(b0, b1, sm)


def place_kernel(parts, bases, *refs):
    out = refs[-1]
    own, rows = len(bases) // parts, out.shape[1]
    me = lax.axis_index("seq")
    for i in range(own):
        for k in range(parts):
            base = bases[i * parts + k]
            out[(me ^ k) * own + i] = refs[i * parts + k][base:base + rows, :].astype(f32)


def place_call(sent, rows):
    own, parts = len(sent), len(sent[0])
    width = sent[0][0][0].shape[1]
    bases = [base for image in sent for _, base in image]
    return small_call(
        lambda *refs: place_kernel(parts, bases, *refs), [x for image in sent for x, _ in image],
        [((parts * own, rows, width), f32)], "place", 8)[0]


VM_A, VM_F, VM_B, VM_W = 12, 24, 14, 14


def xor_permute(x, axis, k):
    return lax.ppermute(x, axis, [(i, i ^ k) for i in range(lax.axis_size(axis))])


def after(x, *others):
    if not others:
        return x
    return lax.optimization_barrier((x,) + others)[0]


def plane_exchange(sends):
    return [xor_permute(x, "dp", (k + 1) << 1) for k, x in enumerate(sends)]


def to_peers(part, axis, count, shift):
    return [part] + [xor_permute(part, axis, k << shift) for k in range(1, count)]


def padded(rows, unit):
    return rows + -rows % unit


def per_device(
    patches, first_gain, first_shift, qkv_weight, query_value_bias, out_weight, out_bias,
    second_gain, second_shift, up_weight, up_bias, down_weight, down_bias, map_weight, map_bias,
    keep_mask, image_valid, token_cotangent,
):
    images, rows, width = patches.shape
    depth, dps = lax.axis_size("seq"), lax.axis_size("dp")
    chips = dps // 2
    own = images // depth
    hidden, tokens = up_weight.shape[1], map_weight.shape[1]
    pairs = width // 128
    unit = 16 * dps * depth
    rows_a, rows_b = padded(2 * hidden, unit), padded(4 * width, unit)

    count, first_blocks, rest_blocks = prepare_call(depth, patches, keep_mask, image_valid)
    order = sorted(range(1, depth), key=lambda k: (k == 1, k))

    def collect(blocks, holds):
        got = [blocks[0]] + [None] * (depth - 1)
        for k in order:
            got[k] = xor_permute(after(blocks[k], *holds), "seq", k)
        return got

    first = collect(first_blocks, [])
    vec, mb, cm = vectors_call(
        own, map_weight.T, token_cotangent, first_gain, first_shift, query_value_bias, out_bias, second_gain,
        second_shift, down_bias, up_bias, map_bias)
    plus = lambda a, b: small_call(plus_kernel, (a, b), [((8, 128), f32)], "plus", 1)[0]
    step, holds = 1, list(first[1:])
    while step < dps:
        if step == 2:
            count = after(count, vec)
        if step == dps // 2:
            holds.append(count)
            count_got = xor_permute(count, "dp", step)
        else:
            count = plus(count, xor_permute(count, "dp", step))
        step *= 2
    rest = collect(rest_blocks, holds)

    saved, learns = [], []
    bases = [0] + [rows * i for i in range(own - 1)]
    acc = dwo = sm = tok = None
    for i in range(own):
        v = vec if tok is None else after(vec, tok)
        qa, key, val, caug, att, mid, x, slots = attend_call(
            first if i == 0 else rest, first, i, bases[i], rows, v, qkv_weight, out_weight)
        if i == 0:
            count = plus(after(count, caug), count_got)
        gm, doa, learn, acc, dwo, sm = feed_call(
            i, own, rows_a, mid, att, slots, vec, mb, cm, image_valid, count,
            out_weight, up_weight, down_weight, acc, dwo, sm)
        tok = sm
        saved.append((qa, key, val, doa, caug, gm, x, slots))
        learns.append(learn)

    got = xor_permute(core_call(acc, sm), "dp", 1)
    bits = depth.bit_length() - 1
    dms, sums, nrms, sent = [], [], [], []
    for i in range(own):
        qa, key, val, doa, caug, gm, x, slots = saved[i]
        started = ()
        if i == 0:
            started = start_call(slots, qa, key, val, doa, after(caug, tok))
            sends, kept, small = plane_call(acc, after(sm, started[1]), got, chips)
            gots = plane_exchange(sends)
            tok = small
        o = back_call(
            slots, (qa, key, val, doa, after(caug, tok)), rows, depth if i < own - 1 else 0, vec, qkv_weight, x, gm, started)
        dms.append(o[0])
        sums.append(o[1])
        tok = o[1]
        leaving = o[2:2 + depth]
        if i < own - 1:
            nrms.append(o[-1])
        if i == own - 2:
            riders = [s[1][0] for s in sent]
            send, kept, small = halve_call(
                kept, after(small, tok, *[x for s in sent for x, _ in s[2:]]), gots, 0, riders)
            got = xor_permute(send, "seq", 1)
            base = kept.shape[0] + 2 * small.shape[0]
            for m, s in enumerate(sent):
                s[1] = (got, base + rows * m)
            tok = small
        if i < own - 1:
            near = (xor_permute(leaving[1], "seq", 1), 0) if i == own - 2 else (leaving[1], 0)
            far = [(xor_permute(x, "seq", k), 0) for k, x in enumerate(leaving) if k > 1]
            sent.append([(leaving[0], 0), near] + far)
    for bit in range(1, bits):
        send, kept, small = halve_call(kept, after(small, tok), [got], bit)
        got = xor_permute(send, "seq", 1 << bit)
        tok = small
    o = last_call(
        rows_b, rows, depth, saved[-1][6], saved[-1][5], after(vec, tok), qkv_weight, [s[7] for s in saved], dms, sums,
        nrms, dwo)
    bigb, smb, tail = o[0], o[1], o[2:]
    early = [x for x, _ in sent[-1][1:]]
    part, small = spread_call(kept, small, got, learns)
    gotb = xor_permute(core_call(bigb, after(smb, small)), "dp", 1)
    size, riding = kept.shape[0], learned_rows(learns)
    got = xor_permute(part, "seq", depth // 2)
    sends, keptb, smallb = plane_call(bigb, smb, gotb, chips)
    gotsb = plane_exchange(sends)
    smallb = after(smallb, *early)
    steps = list(reversed(range(bits)))
    for m, bit in enumerate(steps):
        send, keptb, smallb = halve_call(keptb, smallb, gotsb, bit)
        gotsb = [xor_permute(send, "seq", 1 << bit)]
        part = join_call([after(part, smallb), got], "seq", bit, size, riding)
        size, riding = 2 * size, 2 * riding
        if bit:
            got = xor_permute(part, "seq", 1 << (bit - 1))
    rider = part
    peers = to_peers(first_rows(part, size), "dp", chips, 1)
    late = [tail[0]] + [xor_permute(after(x, smallb), "seq", k) for k, x in enumerate(tail) if k and k % 2 == 0]
    partb, smallb = spread_call(keptb, smallb, gotsb[0])
    odd = [xor_permute(after(x, smallb), "seq", k) for k, x in enumerate(tail) if k % 2]
    for bit in range(bits):
        pair = [partb, xor_permute(partb, "seq", 1 << bit)]
        partb = join_call([after(partb, *(late[1:] if bit == 0 else odd)), pair[1]], "seq", bit, partb.shape[0])
    sent.append([(x, 0) for both in zip(late, odd) for x in both])
    outs = place_call(sent, rows)
    part = join_call([after(peers[0], partb)] + peers[1:], "dp", 1, size)
    a0, a1 = part, xor_permute(part, "dp", 1)
    unpacked = unpack_call(hidden, tokens, images, own, size, a0, a1, small, rider, count)
    gdn, gup, gb_down, gb_out, g_gain2, g_shift2, gb_up, gmapw, gmapb, learned, penalty = unpacked
    peers = to_peers(partb, "dp", chips, 1)
    partb = join_call([after(peers[0], gmapw, outs)] + peers[1:], "dp", 1, partb.shape[0])
    b0, b1 = partb, xor_permute(partb, "dp", 1)
    gqkv, gout, g_gain1, g_shift1, gqv = finish_call(b0, b1, smallb)
    return (
        learned, penalty.reshape(()), outs, g_gain1, g_shift1, gqkv, gqv, gout, gb_out, g_gain2, g_shift2, gup,
        gb_up, gdn, gb_down, gmapw.T, gmapb,
    )


def solution(mesh):
    rep = P()
    placed = (P("dp", "seq", None),) + (rep,) * 14 + (P("dp", "seq"), P("dp"), P("dp", None, None))
    return jax.shard_map(
        per_device, mesh=mesh, in_specs=placed,
        out_specs=(P("dp", None, None), rep, P("dp", "seq", None)) + (rep,) * 14,
        check_vma=False,
    )
```

```python
import jax
import jax.numpy as jnp
from jax import lax
from jax.experimental import pallas as pl
from jax.experimental.pallas import tpu as pltpu
from jax.sharding import PartitionSpec as P

f32, bf = jnp.float32, jnp.bfloat16
EPSILON = 1e-6
MASKED = -1e30
MIB = 1 << 20


def in_hbm(x):
    return pltpu.with_memory_space_constraint(x, pltpu.HBM)


def mm(a, b):
    return lax.dot_general(a, b, (((1,), (0,)), ((), ())), preferred_element_type=f32)


def mm_nt(a, b):
    return lax.dot_general(a, b, (((1,), (1,)), ((), ())), preferred_element_type=f32)


def mm_tn(a, b):
    return lax.dot_general(a, b, (((0,), (0,)), ((), ())), preferred_element_type=f32)


def row_mean(x):
    return jnp.sum(x, axis=-1, keepdims=True) * (1.0 / x.shape[-1])


def normalise(x):
    centred = x - row_mean(x)
    r = lax.rsqrt(row_mean(centred * centred) + EPSILON)
    return centred * r, r


def normal_parts(v):
    expo = jnp.exp(v * v * (-0.5))
    t = 1.0 / (1.0 + jnp.abs(v) * (0.3275911 * 0.7071067811865476))
    series = t * (0.127414796 + t * (-0.142248368 + t * (0.7107068705 + t * (-0.7265760135 + t * 0.5307027145))))
    tail = series * expo
    return jnp.where(v >= 0, 1.0 - tail, tail), expo * 0.3989422804014327


def split2(a):
    high = a.astype(bf)
    return high, (a - high.astype(f32)).astype(bf)


def columns(j, count, base=0):
    if isinstance(j, int):
        return slice(base + j * count, base + (j + 1) * count)
    return pl.ds(pl.multiple_of(base + j * count, 128), count)


def row_at(j):
    return slice(j, j + 1) if isinstance(j, int) else pl.ds(j, 1)


def repeat(first, last, body, straight):
    if straight:
        for j in range(first, last):
            body(j, 0)
    else:
        lax.fori_loop(first, last, body, 0)


def row_counts(n):
    return [c for c in (384,) if c < n] + [n]


def for_rows(count, n, body):
    below = 0.0
    for c in row_counts(n):
        pl.when((count > below) & (count <= float(c)))(lambda c=c: body(c))
        below = float(c)


def kept_count(slots):
    return jnp.max(slots[4:5, 0:128])


def mover(slots, i, c, rows):
    at = lax.broadcasted_iota(jnp.int32, (c, rows), 0).astype(f32)
    return jnp.where(at == slots[i:i + 1, 0:rows], 1.0, 0.0).astype(bf)


def attend_kernel(parts, rows, slot, base, *refs):
    x_refs, flag_refs = refs[:parts], refs[parts:2 * parts]
    vec_ref, wqkv, wout = refs[2 * parts:2 * parts + 3]
    qa_ref, k_ref, v_ref, caug_ref, att_ref, mid_ref, x_ref, slots = refs[2 * parts + 3:2 * parts + 11]
    nrm_s, q_s = refs[2 * parts + 11:]
    n, width = nrm_s.shape
    vec = lambda i: vec_ref[i:i + 1, :]
    before = lax.broadcasted_iota(jnp.int32, (rows, rows), 0) < lax.broadcasted_iota(jnp.int32, (rows, rows), 1)
    before = jnp.where(before, 1.0, 0.0).astype(bf)
    total = jnp.zeros((1, 1), f32)
    slots[...] = jnp.full(slots.shape, -1.0, f32)
    for i in range(parts):
        keep = flag_refs[i][rows:rows + 16, 0:rows].astype(f32)[slot:slot + 1, :]
        rank = mm(jnp.broadcast_to(keep, (8, rows)).astype(bf), before)[0:1, :] + total
        slots[i:i + 1, 0:rows] = jnp.where(keep > 0.0, rank, -1.0)
        total = total + jnp.sum(keep, axis=-1, keepdims=True)
    slots[4:5, :] = jnp.broadcast_to(total, (1, slots.shape[1]))

    def body(c):
        x = None
        for i in range(parts):
            t = mm(mover(slots, i, c, rows), x_refs[i][base:base + rows, :])
            x = t if x is None else x + t
        x_ref[0:c, :] = x.astype(bf)
        xh, _ = normalise(x)
        nrm_s[0:c, :] = (xh * vec(0) + vec(1)).astype(bf)
        nrm = nrm_s[0:c, :]
        q_s[0:c, :] = (mm(nrm, wqkv[:, 0:width]) + vec(2)).astype(bf) * jnp.asarray(0.125, bf)
        k_ref[0:c, :] = mm(nrm, wqkv[:, width:2 * width]).astype(bf)
        v_ref[0:c, :] = (mm(nrm, wqkv[:, 2 * width:3 * width]) + vec(3)).astype(bf)
        lane = lax.broadcasted_iota(jnp.int32, (c, 128), 1)
        lane64 = lane & 63
        real = lax.broadcasted_iota(jnp.int32, (c, 128), 0).astype(f32) < slots[4:5, 0:128]
        caug_ref[0:c, :] = jnp.where(
            lane64 == 3, jnp.where(real, 0.0, MASKED), jnp.where(lane64 < 3, 1.0, 0.0)).astype(bf)
        ones = jnp.ones((c, 128), bf)
        def pair(j, carry):
            sl = columns(j, 128)
            outs = []
            for e in range(2):
                own = (lane < 64) if e == 0 else (lane >= 64)
                kp = jnp.where(own, k_ref[0:c, sl], caug_ref[0:c, :])
                qp = jnp.where(own, q_s[0:c, sl], jnp.where(lane64 == 3, 1.0, 0.0).astype(bf))
                s = mm_nt(qp, kp)
                m = jnp.max(s, axis=-1, keepdims=True)
                p = jnp.exp(s - m).astype(bf)
                o = mm(p, jnp.concatenate([v_ref[0:c, sl], ones], axis=1))
                whole = o[:, 128:256]
                outs.append(o[:, 0:128] / whole)
                logs = -(m + jnp.log(whole))
                hi = logs.astype(bf).astype(f32)
                lo = (logs - hi).astype(bf).astype(f32)
                aug = jnp.where(lane64 == 0, hi, jnp.where(lane64 == 1, lo, jnp.where(
                    lane64 == 2, logs - hi - lo, jnp.where(lane64 == 3, 1.0, 0.0))))
                qa_ref[0:c, columns(2 * j + e, 128)] = jnp.where(own, q_s[0:c, sl], aug.astype(bf))
            att_ref[0:c, sl] = jnp.where(lane < 64, outs[0], outs[1]).astype(bf)
            return carry

        repeat(0, width // 128, pair, c < n and slot == 0)
        mid_ref[0:c, :] = x_ref[0:c, :].astype(f32) + mm(att_ref[0:c, :], wout[...]) + vec(4)

    for_rows(kept_count(slots), n, body)


def attend_call(pieces, flags, slot, base, rows, vec, wqkv, wout):
    parts, width = len(pieces), wout.shape[0]
    n = parts * rows
    outs = [((n, 2 * width), bf), ((n, width), bf), ((n, width), bf), ((n, 128), bf), ((n, width), bf), ((n, width), f32)]
    outs += [((n, width), bf), ((8, 256), f32)]
    return small_call(
        lambda *refs: attend_kernel(parts, rows, slot, base, *refs), (*pieces, *flags, vec, wqkv, wout), outs, "attend",
        VM_A, scratch=[pltpu.VMEM((n, width), bf), pltpu.VMEM((n, width), bf)])


def feed_kernel(slot, own_count, first, *refs):
    mid_ref, att_ref, slots, vec_ref, mb_ref, cm_ref, valid_ref, count_ref, wout, wup, wdn = refs[:11]
    refs = refs[11:]
    if first:
        acc_in = dwo_in = sm_in = None
    else:
        acc_in, dwo_in, sm_in = refs[:3]
        refs = refs[3:]
    gm_ref, doa_ref, learn_ref, acc, dwo, sm = refs[:6]
    sec_s, hid_s, gp_s, g_s, total, gt_s, st_s, gpl_s = refs[6:]
    n, width = mid_ref.shape
    blocks = hid_s.shape[1] // width
    tokens = mb_ref.shape[0]
    vec = lambda i: vec_ref[i:i + 1, :]
    place = lax.axis_index("seq") * own_count + slot

    def add(ref, ref_in, rows, value):
        ref[rows, :] = value if first else ref_in[rows, :] + value

    def body(c):
        xh, _ = normalise(mid_ref[0:c, :])
        sec_s[0:c, :] = (xh * vec(5) + vec(6)).astype(bf)
        def up(j, carry):
            js = columns(j, width)
            pre = mm(sec_s[0:c, :], wup[:, js]) + vec_ref[row_at(8 + j), :]
            upper, density = normal_parts(pre)
            hid_s[0:c, js] = (pre * upper).astype(bf)
            gp_s[0:c, js] = upper + pre * density
            return carry

        repeat(0, blocks, up, c < n)
        total[0:c, :] = mid_ref[0:c, :] + vec(7) + mm(hid_s[0:c, :], wdn[...])
        ohi, olo = split2(total[0:c, :])
        cm = cm_ref[slot]
        lg = mm_nt(cm, ohi) + mm_nt(cm, olo)
        kept = slots[4:5, 0:1]
        keep = jnp.where(lax.broadcasted_iota(jnp.int32, (1, c), 1).astype(f32) < kept, 1.0, 0.0)
        maps = jax.nn.sigmoid(lg[0:tokens, :] + mb_ref[:, 0:1])
        inverse = 1.0 / kept
        tot = jnp.sum(maps, axis=0, keepdims=True)
        inter = jnp.sum(keep * (tot * tot - jnp.sum(maps * maps, axis=0, keepdims=True)), axis=-1, keepdims=True)
        valid = valid_ref[place].astype(f32)
        gmaps = keep * (lg[tokens:2 * tokens, :] * inverse + (2.0 * valid / count_ref[0:1, 0:1]) * (tot - maps))
        gl = gmaps * maps * (1.0 - maps)
        mk = maps * keep
        mkh, mkl = split2(mk)
        glh, gll = split2(gl)
        st = jnp.concatenate([mkh.astype(f32), mkl.astype(f32), glh.astype(f32), gll.astype(f32)], axis=0).astype(bf)
        r1 = mm(st, ohi) + mm(st, olo)
        learn_ref[...] = (r1[0:tokens, :] + r1[tokens:2 * tokens, :]) * inverse
        add(sm, sm_in, slice(8, 16), r1[2 * tokens:3 * tokens, :] + r1[3 * tokens:, :])
        gah, gal = split2(mk * inverse)
        lhs = jnp.concatenate([glh.astype(f32), gah.astype(f32), gll.astype(f32), gal.astype(f32)], axis=0).astype(bf)
        g = mm_tn(lhs, jnp.concatenate([cm, cm], axis=0))
        g_s[0:c, :] = g
        add(sm, sm_in, slice(0, 1), jnp.sum(g, axis=0, keepdims=True))
        glow = g.astype(bf)
        gt_s[:, 0:c] = glow.T
        st_s[:, 0:c] = sec_s[0:c, :].T
        def down(j, carry):
            js = columns(j, width)
            gpre = mm_nt(glow, wdn[js, :]).astype(bf).astype(f32) * gp_s[0:c, js]
            gpl_s[0:c, js] = gpre.astype(bf)
            add(sm, sm_in, row_at(4 + j), jnp.sum(gpre, axis=0, keepdims=True))
            add(acc, acc_in, js, mm(gt_s[:, 0:c], hid_s[0:c, js]))
            add(acc, acc_in, columns(j, width, blocks * width), mm(st_s[:, 0:c], gpl_s[0:c, js]))
            return carry

        repeat(0, blocks, down, c < n)
        total[0:c, :] = mm_nt(gpl_s[0:c, :], wup[...])
        gsec = total[0:c, :]
        xh, r = normalise(mid_ref[0:c, :])
        gg = gsec * vec(5)
        gm = g_s[0:c, :] + r * (gg - row_mean(gg) - xh * row_mean(gg * xh))
        gm_ref[0:c, :] = gm
        gml = gm.astype(bf)
        add(sm, sm_in, slice(1, 2), jnp.sum(gm, axis=0, keepdims=True))
        add(sm, sm_in, slice(2, 3), jnp.sum(gsec * xh, axis=0, keepdims=True))
        add(sm, sm_in, slice(3, 4), jnp.sum(gsec, axis=0, keepdims=True))
        glb = jnp.sum(gl, axis=-1, keepdims=True)
        lr = lax.broadcasted_iota(jnp.int32, (8, width), 1)
        rr = lax.broadcasted_iota(jnp.int32, (8, width), 0)
        line = jnp.sum(jnp.where(lr == rr, glb, 0.0), axis=0, keepdims=True)
        line = line + jnp.where(lr[0:1] == tokens, valid * inter * (1.0 / n), 0.0)
        add(sm, sm_in, slice(16, 24), jnp.where(rr == 0, line, 0.0))
        if first:
            sm[24:32, :] = jnp.zeros((8, width), f32)
            if acc.shape[0] > 2 * blocks * width:
                acc[2 * blocks * width:, :] = jnp.zeros((acc.shape[0] - 2 * blocks * width, width), f32)
        else:
            sm[24:32, :] = sm_in[24:32, :]
            if acc.shape[0] > 2 * blocks * width:
                acc[2 * blocks * width:, :] = acc_in[2 * blocks * width:, :]
        add(dwo, dwo_in, slice(0, width), mm(att_ref[0:c, :].T, gml))
        do = mm_nt(gml, wout[...]).astype(bf).astype(f32)
        lane = lax.broadcasted_iota(jnp.int32, (c, 128), 1)
        lane64 = lane & 63
        for j in range(width // 128):
            sl = slice(128 * j, 128 * j + 128)
            dj = do[:, sl]
            pd = dj * att_ref[0:c, sl].astype(f32)
            for e in range(2):
                own = (lane < 64) if e == 0 else (lane >= 64)
                dl = -jnp.sum(jnp.where(own, pd, 0.0), axis=-1, keepdims=True)
                hi = dl.astype(bf).astype(f32)
                aug = jnp.where(lane64 == 0, hi, jnp.where(lane64 == 1, dl - hi, 0.0))
                h = 2 * j + e
                doa_ref[0:c, 128 * h:128 * h + 128] = jnp.where(own, dj, aug).astype(bf)

    for_rows(kept_count(slots), n, body)


def feed_call(slot, own_count, packed_rows, mid, att, slots, vec, mb, cm, valid, count, wout, wup, wdn, acc, dwo, sm):
    n, width = mid.shape
    hidden = wup.shape[1]
    first = acc is None
    vm = pl.BlockSpec(memory_space=pltpu.VMEM)
    smem = pl.BlockSpec(memory_space=pltpu.SMEM)
    outs = [((n, width), f32), ((n, 2 * width), bf), ((8, width), f32), ((packed_rows, width), f32), ((width, width), f32), ((32, width), f32)]
    args = (mid, att, slots, vec, mb, cm, valid, count, wout, wup, wdn)
    extra = () if first else (acc, dwo, sm)
    return pl.pallas_call(
        lambda *refs: feed_kernel(slot, own_count, first, *refs),
        out_shape=[jax.ShapeDtypeStruct(s, d) for s, d in outs],
        in_specs=[vm] * 6 + [smem] + [vm] * (4 + len(extra)), out_specs=[vm] * 6,
        input_output_aliases={} if first else {11: 3, 12: 4, 13: 5},
        scratch_shapes=[pltpu.VMEM((n, width), bf), pltpu.VMEM((n, hidden), bf), pltpu.VMEM((n, hidden), f32), pltpu.VMEM((n, width), f32)]
        + [pltpu.VMEM((n, width), f32), pltpu.VMEM((width, n), bf), pltpu.VMEM((width, n), bf), pltpu.VMEM((n, hidden), bf)],
        compiler_params=pltpu.CompilerParams(vmem_limit_bytes=VM_F * MIB),
        cost_estimate=pl.CostEstimate(flops=1_000_000, bytes_accessed=1000, transcendentals=0),
        name="feed",
    )(*args, *extra)


def scores_back(js, c, qa, k_ref, v_ref, doa, caug, dm, sums):
    width = k_ref.shape[1]
    step = 192 if c % 192 == 0 else c
    lane = lax.broadcasted_iota(jnp.int32, (step, 128), 1)
    ones = jnp.ones((step, 128), bf)
    def pair(j, carry):
        sl = columns(j, 128)
        k_t = k_ref[0:c, sl].T
        dqt = [None, None]
        dvsum = None
        for start in range(0, c, step):
            cs = slice(start, start + step)
            dvs, dks = [], []
            for e in range(2):
                hs = columns(2 * j + e, 128)
                own = (lane < 64) if e == 0 else (lane >= 64)
                kp = jnp.where(own, k_ref[cs, sl], caug[cs, :])
                vp = jnp.where(own, v_ref[cs, sl], ones)
                p = jnp.exp(mm_nt(kp, qa[0:c, hs]))
                ds = (p * mm_nt(vp, doa[0:c, hs])).astype(bf)
                dvs.append(mm(p.astype(bf), doa[0:c, hs]))
                dks.append(mm(ds, qa[0:c, hs]))
                t = mm(k_t[64 * e:64 * e + 64, cs], ds)
                dqt[e] = t if dqt[e] is None else dqt[e] + t
            dm[cs, columns(j, 128, width)] = jnp.where(lane < 64, dks[0], dks[1]).astype(bf)
            dv = jnp.where(lane < 64, dvs[0], dvs[1])
            dm[cs, columns(j, 128, 2 * width)] = dv.astype(bf)
            s = jnp.sum(dv, axis=0, keepdims=True)
            dvsum = s if dvsum is None else dvsum + s
        dq = jnp.concatenate(dqt, axis=0).T * 0.125
        dm[0:c, sl] = dq.astype(bf)
        sums[0:1, sl] = jnp.sum(dq, axis=0, keepdims=True)
        sums[1:2, sl] = dvsum
        return carry

    repeat(js[0], js[-1] + 1, pair, c < k_ref.shape[0])


def norm_back(c, slots, x_ref, gm, dm, vec_ref, wqkv, g_refs, nrm_ref):
    vec = lambda i: vec_ref[i:i + 1, :]
    gf = mm_nt(dm[0:c, :], wqkv[...])
    xh, r = normalise(x_ref[0:c, :].astype(f32))
    nrm_ref[0:c, :] = (xh * vec(0) + vec(1)).astype(bf)
    gg = gf * vec(0)
    gx = (gm[0:c, :] + r * (gg - row_mean(gg) - xh * row_mean(gg * xh))).astype(bf)
    for i, ref in enumerate(g_refs):
        ref[...] = mm_tn(mover(slots, i, c, ref.shape[0]), gx).astype(bf)
    return jnp.sum(gf * xh, axis=0, keepdims=True), jnp.sum(gf, axis=0, keepdims=True)


def start_kernel(slots, qa, k_ref, v_ref, doa, caug, dm, sums):
    sums[...] = jnp.zeros_like(sums)
    for_rows(
        kept_count(slots), k_ref.shape[0], lambda c: scores_back([0], c, qa, k_ref, v_ref, doa, caug, dm, sums))


def start_call(slots, *attn):
    n, width = attn[1].shape
    return small_call(start_kernel, (slots, *attn), [((n, 3 * width), bf), ((8, width), f32)], "start", VM_B)


def back_kernel(parts, started, *refs):
    slots, attn, (vec_ref, wqkv, x_ref, gm) = refs[0], refs[1:6], refs[6:10]
    refs = refs[10:]
    if started:
        dm0, sums0 = refs[:2]
        refs = refs[2:]
    dm, sums = refs[:2]
    n, width = gm.shape

    def body(c):
        pairs = range(width // 128)
        if started:
            sums[...] = sums0[...]
            for s in range(3):
                dm[0:c, width * s:width * s + 128] = dm0[0:c, width * s:width * s + 128]
            pairs = pairs[1:]
        else:
            sums[...] = jnp.zeros_like(sums)
        scores_back(pairs, c, *attn, dm, sums)
        if parts:
            gain, shift = norm_back(c, slots, x_ref, gm, dm, vec_ref, wqkv, refs[2:2 + parts], refs[-1])
            sums[2:3, :] = gain
            sums[3:4, :] = shift

    for_rows(kept_count(slots), n, body)


def back_call(slots, attn, rows, parts, vec, wqkv, x, gm, started=()):
    n, width = attn[1].shape
    outs = [((n, 3 * width), bf), ((8, width), f32)]
    if parts:
        outs += [((rows, width), bf)] * parts + [((n, width), bf)]
    return small_call(
        lambda *refs: back_kernel(parts, len(started) > 0, *refs),
        (slots, *attn, vec, wqkv, x, gm, *started), outs, "back", VM_B)


def last_kernel(parts, own, *refs):
    x_ref, gm, vec_ref, wqkv, dwo = refs[:5]
    refs = refs[5:]
    slots, dms, sums, nrms = refs[:own], refs[own:2 * own], refs[2 * own:3 * own], list(refs[3 * own:4 * own - 1])
    packed, sm, g_refs, nrm_s = refs[4 * own - 1], refs[4 * own], refs[4 * own + 1:-1], refs[-1]
    n, width = gm.shape
    nrms.append(nrm_s)
    total = sum(ref[0:4, :] for ref in sums)
    sm[...] = jnp.zeros_like(sm)
    sm[2:4, :] = total[0:2, :]

    def finish(c):
        gain, shift = norm_back(c, slots[-1], x_ref, gm, dms[-1], vec_ref, wqkv, g_refs, nrm_s)
        sm[0:1, :] = total[2:3, :] + gain
        sm[1:2, :] = total[3:4, :] + shift

    for_rows(kept_count(slots[-1]), n, finish)
    for i in range(own):

        def add(c, i=i):
            nrm_t = nrms[i][0:c, :].T

            def block(s, carry):
                js = columns(s, width)
                value = mm(nrm_t, dms[i][0:c, js])
                packed[js, :] = value if i == 0 else packed[js, :] + value
                return carry

            repeat(0, 3, block, c < n)

        for_rows(kept_count(slots[i]), n, add)
    packed[3 * width:4 * width, :] = dwo[...]
    if packed.shape[0] > 4 * width:
        packed[4 * width:, :] = jnp.zeros((packed.shape[0] - 4 * width, width), f32)


def last_call(packed_rows, rows, parts, x, gm, vec, wqkv, slots, dms, sums, nrms, dwo):
    own = len(dms)
    n, width = gm.shape
    outs = [((packed_rows, width), f32), ((16, width), f32)] + [((rows, width), bf)] * parts
    return small_call(
        lambda *refs: last_kernel(parts, own, *refs), (x, gm, vec, wqkv, dwo, *slots, *dms, *sums, *nrms), outs, "last",
        VM_W, scratch=[pltpu.VMEM((n, width), bf)])


def aligned(start, rows):
    return pl.ds(pl.multiple_of(start, 16), rows)


def tree_sum(parts):
    while len(parts) > 1:
        parts = [parts[i] + parts[i + 1] for i in range(0, len(parts), 2)]
    return parts[0]


def store_small(ref, at, small):
    rows = small.shape[0]
    high = small.astype(bf)
    ref[at:at + rows, :] = high
    ref[at + rows:at + 2 * rows, :] = (small - high.astype(f32)).astype(bf)


def load_small(ref, at, rows):
    return ref[at:at + rows, :].astype(f32) + ref[at + rows:at + 2 * rows, :].astype(f32)


def rounded(small):
    high, low = split2(small)
    return high.astype(f32) + low.astype(f32)


def core_kernel(big, small, out):
    half = big.shape[0] // 2
    other = 1 - (lax.axis_index("dp") & 1)
    out[0:half, :] = big[aligned(other * half, half), :].astype(bf)
    store_small(out, half, small[...])


def core_call(big, small):
    rows, width = big.shape
    return small_call(core_kernel, (big, small), [((rows // 2 + 2 * small.shape[0], width), bf)], "core", 4)[0]


def plane_kernel(big, small, got, *outs):
    sends, keep, total = outs[:-2], outs[-2], outs[-1]
    half, rows = big.shape[0] // 2, keep.shape[0]
    dp = lax.axis_index("dp")
    base, mine = (dp & 1) * half, dp >> 1
    summed = rounded(small[...]) + load_small(got, half, small.shape[0])
    total[...] = summed
    for k in range(len(sends) + 1):
        at = (mine ^ k) * rows
        value = big[aligned(base + at, rows), :] + got[aligned(at, rows), :].astype(f32)
        if k == 0:
            keep[...] = value
        else:
            sends[k - 1][0:rows, :] = value.astype(bf)
            store_small(sends[k - 1], rows, summed)


def plane_call(big, small, got, count):
    width, s = big.shape[1], small.shape[0]
    rows = big.shape[0] // 2 // count
    outs = [((rows + 2 * s, width), bf)] * (count - 1) + [((rows, width), f32), ((s, width), f32)]
    o = small_call(plane_kernel, (big, small, got), outs, "plane", 4)
    return o[:count - 1], o[-2], o[-1]


def halve_kernel(shift, count, rider, *refs):
    kept, small, gots, riding = refs[0], refs[1], refs[2:2 + count], refs[2 + count:2 + count + rider]
    send, keep, total = refs[2 + count + rider:]
    whole, rows, s = kept.shape[0], keep.shape[0], small.shape[0]
    mine = (lax.axis_index("seq") >> shift) & 1
    summed = tree_sum([rounded(small[...])] + [load_small(got, whole, s) for got in gots])
    total[...] = summed
    for k in range(2):
        at = (mine ^ k) * rows
        value = tree_sum([kept[aligned(at, rows), :]] + [got[aligned(at, rows), :].astype(f32) for got in gots])
        if k == 0:
            keep[...] = value
        else:
            send[0:rows, :] = value.astype(bf)
    store_small(send, rows, summed)
    at = rows + 2 * s
    for ref in riding:
        send[at:at + ref.shape[0], :] = ref[...]
        at += ref.shape[0]


def halve_call(kept, small, gots, shift, riders=()):
    width, s = kept.shape[1], small.shape[0]
    rows = kept.shape[0] // 2
    outs = [((rows + 2 * s + sum(x.shape[0] for x in riders), width), bf), ((rows, width), f32), ((s, width), f32)]
    return small_call(
        lambda *refs: halve_kernel(shift, len(gots), len(riders), *refs),
        (kept, small, *gots, *riders), outs, "halve", 6)


def spread_kernel(learns, rider, *refs):
    kept, small, got = refs[:3]
    learnt, riding = refs[3:3 + learns], refs[3 + learns:3 + learns + rider]
    total, part = refs[3 + learns + rider:]
    rows, s = kept.shape[0], small.shape[0]
    total[...] = rounded(small[...]) + load_small(got, rows, s)
    part[0:rows, :] = (kept[...] + got[0:rows, :].astype(f32)).astype(bf)
    at = rows
    if learns:
        used = sum(ref.shape[0] for ref in learnt)
        blank = [jnp.zeros((-used % 16, kept.shape[1]), f32)] if used % 16 else []
        learnt = jnp.concatenate([ref[...] for ref in learnt] + blank, axis=0)
        part[rows:rows + learnt.shape[0], :] = learnt.astype(bf)
        at += learnt.shape[0]
    for ref in riding:
        part[at:at + ref.shape[0], :] = ref[...]
        at += ref.shape[0]


def learned_rows(learns):
    used = sum(ref.shape[0] for ref in learns)
    return used + -used % 16


def spread_call(kept, small, got, learns=(), riders=()):
    rows, width = kept.shape
    rows += learned_rows(learns) + sum(ref.shape[0] for ref in riders)
    outs = [(small.shape, f32), ((rows, width), bf)]
    total, part = small_call(
        lambda *refs: spread_kernel(len(learns), len(riders), *refs), (kept, small, got, *learns, *riders), outs, "spread", 6)
    return part, total


def join_kernel(axis, shift, rows, riding, count, extra, *refs):
    parts, extras, out = refs[:count], refs[count:count + extra], refs[count + extra]
    mine = (lax.axis_index(axis) >> shift) & (count - 1)
    for k, part in enumerate(parts):
        out[aligned((mine ^ k) * rows, rows), :] = part[0:rows, :]
        if riding:
            out[aligned(count * rows + (mine ^ k) * riding, riding), :] = part[rows:rows + riding, :]
    at = count * (rows + riding)
    for ref in extras:
        out[at:at + ref.shape[0], :] = ref[...]
        at += ref.shape[0]


def join_call(parts, axis, shift, rows, riding=0, extras=()):
    width = parts[0].shape[1]
    total = (rows + riding) * len(parts) + sum(x.shape[0] for x in extras)
    return small_call(
        lambda *refs: join_kernel(axis, shift, rows, riding, len(parts), len(extras), *refs), (*parts, *extras),
        [((total, width), bf)], "join", 6)[0]


def first_kernel(x, out):
    out[...] = x[0:out.shape[0], :]


def first_rows(x, rows):
    return small_call(first_kernel, (x,), [((rows, x.shape[1]), x.dtype)], "first", 4)[0]


def small_call(kernel, args, outs, name, mib, scratch=()):
    vm = pl.BlockSpec(memory_space=pltpu.VMEM)
    return pl.pallas_call(
        kernel,
        out_shape=[jax.ShapeDtypeStruct(s, d) for s, d in outs],
        in_specs=[vm] * len(args), out_specs=[vm] * len(outs), scratch_shapes=list(scratch),
        compiler_params=pltpu.CompilerParams(vmem_limit_bytes=mib * MIB),
        cost_estimate=pl.CostEstimate(flops=1_000_000, bytes_accessed=1000, transcendentals=0),
        name=name,
    )(*args)


def prepare_kernel(own, rows, depth, patches, keep, valid, count, *refs):
    blocks, (keep_s, sems) = refs[:2 * depth], refs[2 * depth:]
    width = patches.shape[2]
    me = lax.axis_index("seq")
    flags_copy = pltpu.make_async_copy(keep, keep_s, sems.at[depth * own])
    flags_copy.start()
    copies = []
    for k in [k for k in range(1, depth)] + [0]:
        for i in range(own):
            target = blocks[2 * k].at[0:rows, :] if i == 0 else blocks[2 * k + 1].at[rows * (i - 1):rows * i, :]
            copies.append(pltpu.make_async_copy(patches.at[(me ^ k) * own + i], target, sems.at[k * own + i]))
            copies[-1].start()
    total = valid[0]
    for i in range(1, valid.shape[0]):
        total = total + valid[i]
    count[...] = jnp.full(count.shape, total.astype(f32), f32)
    flags_copy.wait()
    line = lax.broadcasted_iota(jnp.int32, (16, rows), 0)
    for k in range(depth):
        flags = jnp.zeros((16, rows), f32)
        for i in range(own):
            flags = jnp.where(line == i, keep_s[pl.ds((me ^ k) * own + i, 1), :].astype(f32), flags)
        blocks[2 * k][rows:rows + 16, :] = jnp.zeros((16, width), bf)
        blocks[2 * k][rows:rows + 16, 0:rows] = flags.astype(bf)
    for copy in copies:
        copy.wait()


def prepare_call(depth, patches, keep, valid):
    images, rows, width = patches.shape
    own = images // depth
    vm, hbm = pl.BlockSpec(memory_space=pltpu.VMEM), pl.BlockSpec(memory_space=pltpu.HBM)
    outs = [((8, 128), f32)]
    for k in range(depth):
        outs += [((rows + 16, width), bf), ((rows * (own - 1), width), bf)]
    o = pl.pallas_call(
        lambda *refs: prepare_kernel(own, rows, depth, *refs),
        out_shape=[jax.ShapeDtypeStruct(s, d) for s, d in outs],
        in_specs=[hbm, hbm, pl.BlockSpec(memory_space=pltpu.SMEM)], out_specs=[vm] * len(outs),
        scratch_shapes=[pltpu.VMEM(keep.shape, keep.dtype), pltpu.SemaphoreType.DMA((depth * own + 1,))],
        compiler_params=pltpu.CompilerParams(vmem_limit_bytes=8 * MIB),
        cost_estimate=pl.CostEstimate(flops=1_000_000, bytes_accessed=1000, transcendentals=0),
        name="prepare",
    )(in_hbm(patches), in_hbm(keep), valid)
    return o[0], o[1::2], o[2::2]


def vectors_kernel(own, mapw, cot, *refs):
    half = (len(refs) - 4) // 2
    sources, vec, mb, cm, held, sems = refs[:half], refs[half], refs[half + 1], refs[half + 2], refs[half + 3:-1], refs[-1]
    copies = [pltpu.make_async_copy(a, b, sems.at[i]) for i, (a, b) in enumerate(zip(sources, held))]
    for copy in copies:
        copy.start()
    vec[...] = jnp.zeros_like(vec)
    me = lax.axis_index("seq")
    for i in range(own):
        cm[i] = jnp.concatenate([mapw[...].astype(f32), cot[me * own + i].astype(f32)], axis=0).astype(bf)
    for copy in copies:
        copy.wait()
    width, tokens = vec.shape[1], mb.shape[0]
    line = 0
    for ref in held[:-1]:
        for j in range(ref.shape[0] // width):
            vec[line, :] = ref[width * j:width * (j + 1)].astype(f32)
            line += 1
    bias = jnp.broadcast_to(held[-1][...].astype(f32).reshape(1, tokens), (tokens, tokens))
    diag = lax.broadcasted_iota(jnp.int32, (tokens, tokens), 0) == lax.broadcasted_iota(jnp.int32, (tokens, tokens), 1)
    mb[...] = jnp.broadcast_to(jnp.sum(jnp.where(diag, bias, 0.0), axis=1, keepdims=True), mb.shape)


def vectors_call(own, mapw, cot, *sources):
    width, tokens = sources[0].shape[0], sources[-1].shape[0]
    vm, hbm = pl.BlockSpec(memory_space=pltpu.VMEM), pl.BlockSpec(memory_space=pltpu.HBM)
    outs = [((16, width), f32), ((tokens, 128), f32), ((own, 2 * tokens, width), bf)]
    return pl.pallas_call(
        lambda *refs: vectors_kernel(own, *refs),
        out_shape=[jax.ShapeDtypeStruct(s, d) for s, d in outs],
        in_specs=[vm] * 2 + [hbm] * len(sources), out_specs=[vm] * 3,
        scratch_shapes=[pltpu.VMEM(s.shape, s.dtype) for s in sources] + [pltpu.SemaphoreType.DMA((len(sources),))],
        compiler_params=pltpu.CompilerParams(vmem_limit_bytes=4 * MIB),
        cost_estimate=pl.CostEstimate(flops=1_000_000, bytes_accessed=1000, transcendentals=0),
        name="vectors",
    )(mapw, cot, *map(in_hbm, sources))


def plus_kernel(a, b, out):
    out[...] = a[...] + b[...]


def unpack_kernel(hidden, own, base, a0, a1, sm_ref, rider, count_ref, gdn, gup, down, outb, gain, shift, upb, mapw, mapb, learned, penalty, a_s):
    side = lax.axis_index("dp") & 1
    half, width = a0.shape
    a_s[pl.ds(pl.multiple_of(side * half, 16), half), :] = a0[...]
    a_s[pl.ds(pl.multiple_of((1 - side) * half, 16), half), :] = a1[...]
    blocks = hidden // width
    for j in range(blocks):
        js = slice(width * j, width * (j + 1))
        gdn[js, :] = a_s[js, :].T.astype(f32)
        gup[:, js] = a_s[width * (blocks + j):width * (blocks + j + 1), :].astype(f32)
    for i, ref in enumerate((down, outb, gain, shift)):
        ref[...] = sm_ref[i, :]
    for j in range(blocks):
        upb[width * j:width * (j + 1)] = sm_ref[4 + j, :]
    mapw[...] = sm_ref[8:16, :]
    tokens = learned.shape[1]
    penalty[...] = sm_ref[16:17, tokens:tokens + 1] / count_ref[0:1, 0:1]
    mapb[...] = sm_ref[16, 0:tokens]
    count = own * tokens
    depth = learned.shape[0] // own
    bits = depth.bit_length() - 1
    for z in range(depth):
        place = sum(((z >> b) & 1) << (bits - 1 - b) for b in range(bits))
        span = count + -count % 16
        at = base + span * place
        both = rider[at:at + span, :].astype(f32)
        for i in range(own):
            learned[z * own + i] = both[tokens * i:tokens * (i + 1), :]


def unpack_call(hidden, tokens, images, own, base, a0, a1, sm, rider, count):
    width = a0.shape[1]
    vm = pl.BlockSpec(memory_space=pltpu.VMEM)
    outs = [(hidden, width), (width, hidden)] + [(width,)] * 4 + [(hidden,), (tokens, width), (tokens,)]
    outs += [(images, tokens, width), (1, 1)]
    return pl.pallas_call(
        lambda *refs: unpack_kernel(hidden, own, base, *refs),
        out_shape=[jax.ShapeDtypeStruct(s, f32) for s in outs],
        in_specs=[vm] * 5, out_specs=[vm] * len(outs),
        scratch_shapes=[pltpu.VMEM((2 * a0.shape[0], width), bf)],
        compiler_params=pltpu.CompilerParams(vmem_limit_bytes=16 * MIB),
        cost_estimate=pl.CostEstimate(flops=1_000_000, bytes_accessed=1000, transcendentals=0),
        name="unpack",
    )(a0, a1, sm, rider, count)


def finish_kernel(b0, b1, sm_ref, gqkv, gout, gain, shift, biases, b_s):
    side = lax.axis_index("dp") & 1
    half, width = b0.shape
    b_s[pl.ds(pl.multiple_of(side * half, 16), half), :] = b0[...]
    b_s[pl.ds(pl.multiple_of((1 - side) * half, 16), half), :] = b1[...]
    for j in range(3):
        js = slice(width * j, width * (j + 1))
        gqkv[:, js] = b_s[js, :].astype(f32)
    gout[...] = b_s[3 * width:4 * width, :].astype(f32)
    gain[...] = sm_ref[0, :]
    shift[...] = sm_ref[1, :]
    for j in range(2):
        biases[width * j:width * (j + 1)] = sm_ref[2 + j, :]


def finish_call(b0, b1, sm):
    width = b0.shape[1]
    vm = pl.BlockSpec(memory_space=pltpu.VMEM)
    outs = [(width, 3 * width), (width, width), (width,), (width,), (2 * width,)]
    return pl.pallas_call(
        finish_kernel,
        out_shape=[jax.ShapeDtypeStruct(s, f32) for s in outs],
        in_specs=[vm] * 3, out_specs=[vm] * len(outs),
        scratch_shapes=[pltpu.VMEM((2 * b0.shape[0], width), bf)],
        compiler_params=pltpu.CompilerParams(vmem_limit_bytes=8 * MIB),
        cost_estimate=pl.CostEstimate(flops=1_000_000, bytes_accessed=1000, transcendentals=0),
        name="finish",
    )(b0, b1, sm)


def place_kernel(parts, bases, *refs):
    out = refs[-1]
    own, rows = len(bases) // parts, out.shape[1]
    me = lax.axis_index("seq")
    for i in range(own):
        for k in range(parts):
            base = bases[i * parts + k]
            out[(me ^ k) * own + i] = refs[i * parts + k][base:base + rows, :].astype(f32)


def place_call(sent, rows):
    own, parts = len(sent), len(sent[0])
    width = sent[0][0][0].shape[1]
    bases = [base for image in sent for _, base in image]
    return small_call(
        lambda *refs: place_kernel(parts, bases, *refs), [x for image in sent for x, _ in image],
        [((parts * own, rows, width), f32)], "place", 8)[0]


VM_A, VM_F, VM_B, VM_W = 12, 26, 14, 14


def xor_permute(x, axis, k):
    return lax.ppermute(x, axis, [(i, i ^ k) for i in range(lax.axis_size(axis))])


def after(x, *others):
    if not others:
        return x
    return lax.optimization_barrier((x,) + others)[0]


def plane_exchange(sends):
    return [xor_permute(x, "dp", (k + 1) << 1) for k, x in enumerate(sends)]


def to_peers(part, axis, count, shift):
    return [part] + [xor_permute(part, axis, k << shift) for k in range(1, count)]


def padded(rows, unit):
    return rows + -rows % unit


def per_device(
    patches, first_gain, first_shift, qkv_weight, query_value_bias, out_weight, out_bias,
    second_gain, second_shift, up_weight, up_bias, down_weight, down_bias, map_weight, map_bias,
    keep_mask, image_valid, token_cotangent,
):
    images, rows, width = patches.shape
    depth, dps = lax.axis_size("seq"), lax.axis_size("dp")
    chips = dps // 2
    own = images // depth
    hidden, tokens = up_weight.shape[1], map_weight.shape[1]
    pairs = width // 128
    unit = 16 * dps * depth
    rows_a, rows_b = padded(2 * hidden, unit), padded(4 * width, unit)

    count, first_blocks, rest_blocks = prepare_call(depth, patches, keep_mask, image_valid)
    order = sorted(range(1, depth), key=lambda k: (k == 1, k))

    def collect(blocks, holds):
        got = [blocks[0]] + [None] * (depth - 1)
        for k in order:
            got[k] = xor_permute(after(blocks[k], *holds), "seq", k)
        return got

    first = collect(first_blocks, [])
    vec, mb, cm = vectors_call(
        own, map_weight.T, token_cotangent, first_gain, first_shift, query_value_bias, out_bias, second_gain,
        second_shift, down_bias, up_bias, map_bias)
    plus = lambda a, b: small_call(plus_kernel, (a, b), [((8, 128), f32)], "plus", 1)[0]
    step, holds = 1, list(first[1:])
    while step < dps:
        if step == 2:
            count = after(count, vec)
        if step == dps // 2:
            holds.append(count)
            count_got = xor_permute(count, "dp", step)
        else:
            count = plus(count, xor_permute(count, "dp", step))
        step *= 2
    rest = collect(rest_blocks, holds)

    saved, learns = [], []
    bases = [0] + [rows * i for i in range(own - 1)]
    acc = dwo = sm = tok = None
    for i in range(own):
        v = vec if tok is None else after(vec, tok)
        qa, key, val, caug, att, mid, x, slots = attend_call(
            first if i == 0 else rest, first, i, bases[i], rows, v, qkv_weight, out_weight)
        if i == 0:
            count = plus(after(count, caug), count_got)
        gm, doa, learn, acc, dwo, sm = feed_call(
            i, own, rows_a, mid, att, slots, vec, mb, cm, image_valid, count,
            out_weight, up_weight, down_weight, acc, dwo, sm)
        tok = sm
        saved.append((qa, key, val, doa, caug, gm, x, slots))
        learns.append(learn)

    got = xor_permute(core_call(acc, sm), "dp", 1)
    bits = depth.bit_length() - 1
    dms, sums, nrms, sent = [], [], [], []
    for i in range(own):
        qa, key, val, doa, caug, gm, x, slots = saved[i]
        started = ()
        if i == 0:
            started = start_call(slots, qa, key, val, doa, after(caug, tok))
            sends, kept, small = plane_call(acc, after(sm, started[1]), got, chips)
            gots = plane_exchange(sends)
            tok = small
        o = back_call(
            slots, (qa, key, val, doa, after(caug, tok)), rows, depth if i < own - 1 else 0, vec, qkv_weight, x, gm, started)
        dms.append(o[0])
        sums.append(o[1])
        tok = o[1]
        leaving = o[2:2 + depth]
        if i < own - 1:
            nrms.append(o[-1])
        if i == own - 2:
            riders = [s[1][0] for s in sent]
            send, kept, small = halve_call(
                kept, after(small, tok, *[x for s in sent for x, _ in s[2:]]), gots, 0, riders)
            got = xor_permute(send, "seq", 1)
            base = kept.shape[0] + 2 * small.shape[0]
            for m, s in enumerate(sent):
                s[1] = (got, base + rows * m)
            tok = small
        if i < own - 1:
            near = (xor_permute(leaving[1], "seq", 1), 0) if i == own - 2 else (leaving[1], 0)
            far = [(xor_permute(x, "seq", k), 0) for k, x in enumerate(leaving) if k > 1]
            sent.append([(leaving[0], 0), near] + far)
    for bit in range(1, bits):
        send, kept, small = halve_call(kept, after(small, tok), [got], bit)
        got = xor_permute(send, "seq", 1 << bit)
        tok = small
    o = last_call(
        rows_b, rows, depth, saved[-1][6], saved[-1][5], after(vec, tok), qkv_weight, [s[7] for s in saved], dms, sums,
        nrms, dwo)
    bigb, smb, tail = o[0], o[1], o[2:]
    early = [x for x, _ in sent[-1][1:]]
    part, small = spread_call(kept, small, got, learns)
    gotb = xor_permute(core_call(bigb, after(smb, small)), "dp", 1)
    size, riding = kept.shape[0], learned_rows(learns)
    got = xor_permute(part, "seq", depth // 2)
    sends, keptb, smallb = plane_call(bigb, smb, gotb, chips)
    gotsb = plane_exchange(sends)
    smallb = after(smallb, *early)
    steps = list(reversed(range(bits)))
    for m, bit in enumerate(steps):
        send, keptb, smallb = halve_call(keptb, smallb, gotsb, bit)
        gotsb = [xor_permute(send, "seq", 1 << bit)]
        part = join_call([after(part, smallb), got], "seq", bit, size, riding)
        size, riding = 2 * size, 2 * riding
        if bit:
            got = xor_permute(part, "seq", 1 << (bit - 1))
    rider = part
    peers = to_peers(first_rows(part, size), "dp", chips, 1)
    late = [tail[0]] + [xor_permute(after(x, smallb), "seq", k) for k, x in enumerate(tail) if k and k % 2 == 0]
    partb, smallb = spread_call(keptb, smallb, gotsb[0])
    odd = [xor_permute(after(x, smallb), "seq", k) for k, x in enumerate(tail) if k % 2]
    for bit in range(bits):
        pair = [partb, xor_permute(partb, "seq", 1 << bit)]
        partb = join_call([after(partb, *(late[1:] if bit == 0 else odd)), pair[1]], "seq", bit, partb.shape[0])
    sent.append([(x, 0) for both in zip(late, odd) for x in both])
    outs = place_call(sent, rows)
    part = join_call([after(peers[0], partb)] + peers[1:], "dp", 1, size)
    a0, a1 = part, xor_permute(part, "dp", 1)
    unpacked = unpack_call(hidden, tokens, images, own, size, a0, a1, small, rider, count)
    gdn, gup, gb_down, gb_out, g_gain2, g_shift2, gb_up, gmapw, gmapb, learned, penalty = unpacked
    peers = to_peers(partb, "dp", chips, 1)
    partb = join_call([after(peers[0], gmapw, outs)] + peers[1:], "dp", 1, partb.shape[0])
    b0, b1 = partb, xor_permute(partb, "dp", 1)
    gqkv, gout, g_gain1, g_shift1, gqv = finish_call(b0, b1, smallb)
    return (
        learned, penalty.reshape(()), outs, g_gain1, g_shift1, gqkv, gqv, gout, gb_out, g_gain2, g_shift2, gup,
        gb_up, gdn, gb_down, gmapw.T, gmapb,
    )


def solution(mesh):
    rep = P()
    placed = (P("dp", "seq", None),) + (rep,) * 14 + (P("dp", "seq"), P("dp"), P("dp", None, None))
    return jax.shard_map(
        per_device, mesh=mesh, in_specs=placed,
        out_specs=(P("dp", None, None), rep, P("dp", "seq", None)) + (rep,) * 14,
        check_vma=False,
    )
```

```python
import jax
import jax.numpy as jnp
from jax import lax
from jax.experimental import pallas as pl
from jax.experimental.pallas import tpu as pltpu
from jax.sharding import PartitionSpec as P

f32, bf = jnp.float32, jnp.bfloat16
EPSILON = 1e-6
MASKED = -1e30
MIB = 1 << 20


def in_hbm(x):
    return pltpu.with_memory_space_constraint(x, pltpu.HBM)


def mm(a, b):
    return lax.dot_general(a, b, (((1,), (0,)), ((), ())), preferred_element_type=f32)


def mm_nt(a, b):
    return lax.dot_general(a, b, (((1,), (1,)), ((), ())), preferred_element_type=f32)


def mm_tn(a, b):
    return lax.dot_general(a, b, (((0,), (0,)), ((), ())), preferred_element_type=f32)


def row_mean(x):
    return jnp.sum(x, axis=-1, keepdims=True) * (1.0 / x.shape[-1])


def normalise(x):
    centred = x - row_mean(x)
    r = lax.rsqrt(row_mean(centred * centred) + EPSILON)
    return centred * r, r


def normal_parts(v):
    expo = jnp.exp(v * v * (-0.5))
    t = 1.0 / (1.0 + jnp.abs(v) * (0.3275911 * 0.7071067811865476))
    series = t * (0.127414796 + t * (-0.142248368 + t * (0.7107068705 + t * (-0.7265760135 + t * 0.5307027145))))
    tail = series * expo
    return jnp.where(v >= 0, 1.0 - tail, tail), expo * 0.3989422804014327


def split2(a):
    high = a.astype(bf)
    return high, (a - high.astype(f32)).astype(bf)


def columns(j, count, base=0):
    if isinstance(j, int):
        return slice(base + j * count, base + (j + 1) * count)
    return pl.ds(pl.multiple_of(base + j * count, 128), count)


def row_at(j):
    return slice(j, j + 1) if isinstance(j, int) else pl.ds(j, 1)


def repeat(first, last, body, straight):
    if straight:
        for j in range(first, last):
            body(j, 0)
    else:
        lax.fori_loop(first, last, body, 0)


def row_counts(n):
    return [c for c in (384,) if c < n] + [n]


def for_rows(count, n, body):
    below = 0.0
    for c in row_counts(n):
        pl.when((count > below) & (count <= float(c)))(lambda c=c: body(c))
        below = float(c)


def kept_count(slots):
    return jnp.max(slots[4:5, 0:128])


def mover(slots, i, c, rows):
    at = lax.broadcasted_iota(jnp.int32, (c, rows), 0).astype(f32)
    return jnp.where(at == slots[i:i + 1, 0:rows], 1.0, 0.0).astype(bf)


def attend_kernel(parts, rows, slot, base, *refs):
    x_refs, flag_refs = refs[:parts], refs[parts:2 * parts]
    vec_ref, wqkv, wout = refs[2 * parts:2 * parts + 3]
    qa_ref, k_ref, v_ref, caug_ref, att_ref, mid_ref, x_ref, slots = refs[2 * parts + 3:2 * parts + 11]
    nrm_s, q_s = refs[2 * parts + 11:]
    n, width = nrm_s.shape
    vec = lambda i: vec_ref[i:i + 1, :]
    before = lax.broadcasted_iota(jnp.int32, (rows, rows), 0) < lax.broadcasted_iota(jnp.int32, (rows, rows), 1)
    before = jnp.where(before, 1.0, 0.0).astype(bf)
    total = jnp.zeros((1, 1), f32)
    slots[...] = jnp.full(slots.shape, -1.0, f32)
    for i in range(parts):
        keep = flag_refs[i][rows:rows + 16, 0:rows].astype(f32)[slot:slot + 1, :]
        rank = mm(jnp.broadcast_to(keep, (8, rows)).astype(bf), before)[0:1, :] + total
        slots[i:i + 1, 0:rows] = jnp.where(keep > 0.0, rank, -1.0)
        total = total + jnp.sum(keep, axis=-1, keepdims=True)
    slots[4:5, :] = jnp.broadcast_to(total, (1, slots.shape[1]))

    def body(c):
        x = None
        for i in range(parts):
            t = mm(mover(slots, i, c, rows), x_refs[i][base:base + rows, :])
            x = t if x is None else x + t
        x_ref[0:c, :] = x.astype(bf)
        xh, _ = normalise(x)
        nrm_s[0:c, :] = (xh * vec(0) + vec(1)).astype(bf)
        nrm = nrm_s[0:c, :]
        q_s[0:c, :] = (mm(nrm, wqkv[:, 0:width]) + vec(2)).astype(bf) * jnp.asarray(0.125, bf)
        k_ref[0:c, :] = mm(nrm, wqkv[:, width:2 * width]).astype(bf)
        v_ref[0:c, :] = (mm(nrm, wqkv[:, 2 * width:3 * width]) + vec(3)).astype(bf)
        lane = lax.broadcasted_iota(jnp.int32, (c, 128), 1)
        lane64 = lane & 63
        real = lax.broadcasted_iota(jnp.int32, (c, 128), 0).astype(f32) < slots[4:5, 0:128]
        caug_ref[0:c, :] = jnp.where(
            lane64 == 3, jnp.where(real, 0.0, MASKED), jnp.where(lane64 < 3, 1.0, 0.0)).astype(bf)
        ones = jnp.ones((c, 128), bf)
        def pair(j, carry):
            sl = columns(j, 128)
            outs = []
            for e in range(2):
                own = (lane < 64) if e == 0 else (lane >= 64)
                kp = jnp.where(own, k_ref[0:c, sl], caug_ref[0:c, :])
                qp = jnp.where(own, q_s[0:c, sl], jnp.where(lane64 == 3, 1.0, 0.0).astype(bf))
                s = mm_nt(qp, kp)
                m = jnp.max(s, axis=-1, keepdims=True)
                p = jnp.exp(s - m).astype(bf)
                o = mm(p, jnp.concatenate([v_ref[0:c, sl], ones], axis=1))
                whole = o[:, 128:256]
                outs.append(o[:, 0:128] / whole)
                logs = -(m + jnp.log(whole))
                hi = logs.astype(bf).astype(f32)
                lo = (logs - hi).astype(bf).astype(f32)
                aug = jnp.where(lane64 == 0, hi, jnp.where(lane64 == 1, lo, jnp.where(
                    lane64 == 2, logs - hi - lo, jnp.where(lane64 == 3, 1.0, 0.0))))
                qa_ref[0:c, columns(2 * j + e, 128)] = jnp.where(own, q_s[0:c, sl], aug.astype(bf))
            att_ref[0:c, sl] = jnp.where(lane < 64, outs[0], outs[1]).astype(bf)
            return carry

        repeat(0, width // 128, pair, c < n and slot == 0)
        mid_ref[0:c, :] = x_ref[0:c, :].astype(f32) + mm(att_ref[0:c, :], wout[...]) + vec(4)

    for_rows(kept_count(slots), n, body)


def attend_call(pieces, flags, slot, base, rows, vec, wqkv, wout):
    parts, width = len(pieces), wout.shape[0]
    n = parts * rows
    outs = [((n, 2 * width), bf), ((n, width), bf), ((n, width), bf), ((n, 128), bf), ((n, width), bf), ((n, width), f32)]
    outs += [((n, width), bf), ((8, 256), f32)]
    return small_call(
        lambda *refs: attend_kernel(parts, rows, slot, base, *refs), (*pieces, *flags, vec, wqkv, wout), outs, "attend",
        VM_A, scratch=[pltpu.VMEM((n, width), bf), pltpu.VMEM((n, width), bf)])


def feed_kernel(slot, own_count, first, *refs):
    mid_ref, att_ref, slots, vec_ref, mb_ref, cm_ref, valid_ref, count_ref, wout, wup, wdn = refs[:11]
    refs = refs[11:]
    if first:
        acc_in = dwo_in = sm_in = None
    else:
        acc_in, dwo_in, sm_in = refs[:3]
        refs = refs[3:]
    gm_ref, doa_ref, learn_ref, acc, dwo, sm = refs[:6]
    sec_s, hid_s, gp_s, g_s, total, gt_s, st_s, gpl_s = refs[6:]
    n, width = mid_ref.shape
    blocks = hid_s.shape[1] // width
    tokens = mb_ref.shape[0]
    vec = lambda i: vec_ref[i:i + 1, :]
    place = lax.axis_index("seq") * own_count + slot

    def add(ref, ref_in, rows, value):
        ref[rows, :] = value if first else ref_in[rows, :] + value

    def body(c):
        xh, _ = normalise(mid_ref[0:c, :])
        sec_s[0:c, :] = (xh * vec(5) + vec(6)).astype(bf)
        def up(j, carry):
            js = columns(j, width)
            pre = mm(sec_s[0:c, :], wup[:, js]) + vec_ref[row_at(8 + j), :]
            upper, density = normal_parts(pre)
            hid_s[0:c, js] = (pre * upper).astype(bf)
            gp_s[0:c, js] = upper + pre * density
            return carry

        repeat(0, blocks, up, c < n)
        total[0:c, :] = mid_ref[0:c, :] + vec(7) + mm(hid_s[0:c, :], wdn[...])
        ohi, olo = split2(total[0:c, :])
        cm = cm_ref[slot]
        lg = mm_nt(cm, ohi) + mm_nt(cm, olo)
        kept = slots[4:5, 0:1]
        keep = jnp.where(lax.broadcasted_iota(jnp.int32, (1, c), 1).astype(f32) < kept, 1.0, 0.0)
        maps = jax.nn.sigmoid(lg[0:tokens, :] + mb_ref[:, 0:1])
        inverse = 1.0 / kept
        tot = jnp.sum(maps, axis=0, keepdims=True)
        inter = jnp.sum(keep * (tot * tot - jnp.sum(maps * maps, axis=0, keepdims=True)), axis=-1, keepdims=True)
        valid = valid_ref[place].astype(f32)
        gmaps = keep * (lg[tokens:2 * tokens, :] * inverse + (2.0 * valid / count_ref[0:1, 0:1]) * (tot - maps))
        gl = gmaps * maps * (1.0 - maps)
        mk = maps * keep
        mkh, mkl = split2(mk)
        glh, gll = split2(gl)
        st = jnp.concatenate([mkh.astype(f32), mkl.astype(f32), glh.astype(f32), gll.astype(f32)], axis=0).astype(bf)
        r1 = mm(st, ohi) + mm(st, olo)
        learn_ref[...] = (r1[0:tokens, :] + r1[tokens:2 * tokens, :]) * inverse
        add(sm, sm_in, slice(8, 16), r1[2 * tokens:3 * tokens, :] + r1[3 * tokens:, :])
        gah, gal = split2(mk * inverse)
        lhs = jnp.concatenate([glh.astype(f32), gah.astype(f32), gll.astype(f32), gal.astype(f32)], axis=0).astype(bf)
        g = mm_tn(lhs, jnp.concatenate([cm, cm], axis=0))
        g_s[0:c, :] = g
        add(sm, sm_in, slice(0, 1), jnp.sum(g, axis=0, keepdims=True))
        glow = g.astype(bf)
        gt_s[:, 0:c] = glow.T
        st_s[:, 0:c] = sec_s[0:c, :].T
        def down(j, carry):
            js = columns(j, width)
            gpre = mm_nt(glow, wdn[js, :]).astype(bf).astype(f32) * gp_s[0:c, js]
            gpl_s[0:c, js] = gpre.astype(bf)
            add(sm, sm_in, row_at(4 + j), jnp.sum(gpre, axis=0, keepdims=True))
            add(acc, acc_in, js, mm(gt_s[:, 0:c], hid_s[0:c, js]))
            add(acc, acc_in, columns(j, width, blocks * width), mm(st_s[:, 0:c], gpl_s[0:c, js]))
            return carry

        repeat(0, blocks, down, c < n)
        total[0:c, :] = mm_nt(gpl_s[0:c, :], wup[...])
        gsec = total[0:c, :]
        xh, r = normalise(mid_ref[0:c, :])
        gg = gsec * vec(5)
        gm = g_s[0:c, :] + r * (gg - row_mean(gg) - xh * row_mean(gg * xh))
        gm_ref[0:c, :] = gm
        gml = gm.astype(bf)
        add(sm, sm_in, slice(1, 2), jnp.sum(gm, axis=0, keepdims=True))
        add(sm, sm_in, slice(2, 3), jnp.sum(gsec * xh, axis=0, keepdims=True))
        add(sm, sm_in, slice(3, 4), jnp.sum(gsec, axis=0, keepdims=True))
        glb = jnp.sum(gl, axis=-1, keepdims=True)
        lr = lax.broadcasted_iota(jnp.int32, (8, width), 1)
        rr = lax.broadcasted_iota(jnp.int32, (8, width), 0)
        line = jnp.sum(jnp.where(lr == rr, glb, 0.0), axis=0, keepdims=True)
        line = line + jnp.where(lr[0:1] == tokens, valid * inter * (1.0 / n), 0.0)
        add(sm, sm_in, slice(16, 24), jnp.where(rr == 0, line, 0.0))
        if first:
            sm[24:32, :] = jnp.zeros((8, width), f32)
            if acc.shape[0] > 2 * blocks * width:
                acc[2 * blocks * width:, :] = jnp.zeros((acc.shape[0] - 2 * blocks * width, width), f32)
        else:
            sm[24:32, :] = sm_in[24:32, :]
            if acc.shape[0] > 2 * blocks * width:
                acc[2 * blocks * width:, :] = acc_in[2 * blocks * width:, :]
        add(dwo, dwo_in, slice(0, width), mm(att_ref[0:c, :].T, gml))
        do = mm_nt(gml, wout[...]).astype(bf).astype(f32)
        lane = lax.broadcasted_iota(jnp.int32, (c, 128), 1)
        lane64 = lane & 63
        for j in range(width // 128):
            sl = slice(128 * j, 128 * j + 128)
            dj = do[:, sl]
            pd = dj * att_ref[0:c, sl].astype(f32)
            for e in range(2):
                own = (lane < 64) if e == 0 else (lane >= 64)
                dl = -jnp.sum(jnp.where(own, pd, 0.0), axis=-1, keepdims=True)
                hi = dl.astype(bf).astype(f32)
                aug = jnp.where(lane64 == 0, hi, jnp.where(lane64 == 1, dl - hi, 0.0))
                h = 2 * j + e
                doa_ref[0:c, 128 * h:128 * h + 128] = jnp.where(own, dj, aug).astype(bf)

    for_rows(kept_count(slots), n, body)


def feed_call(slot, own_count, packed_rows, mid, att, slots, vec, mb, cm, valid, count, wout, wup, wdn, acc, dwo, sm):
    n, width = mid.shape
    hidden = wup.shape[1]
    first = acc is None
    vm = pl.BlockSpec(memory_space=pltpu.VMEM)
    smem = pl.BlockSpec(memory_space=pltpu.SMEM)
    outs = [((n, width), f32), ((n, 2 * width), bf), ((8, width), f32), ((packed_rows, width), f32), ((width, width), f32), ((32, width), f32)]
    args = (mid, att, slots, vec, mb, cm, valid, count, wout, wup, wdn)
    extra = () if first else (acc, dwo, sm)
    return pl.pallas_call(
        lambda *refs: feed_kernel(slot, own_count, first, *refs),
        out_shape=[jax.ShapeDtypeStruct(s, d) for s, d in outs],
        in_specs=[vm] * 6 + [smem] + [vm] * (4 + len(extra)), out_specs=[vm] * 6,
        input_output_aliases={} if first else {11: 3, 12: 4, 13: 5},
        scratch_shapes=[pltpu.VMEM((n, width), bf), pltpu.VMEM((n, hidden), bf), pltpu.VMEM((n, hidden), f32), pltpu.VMEM((n, width), f32)]
        + [pltpu.VMEM((n, width), f32), pltpu.VMEM((width, n), bf), pltpu.VMEM((width, n), bf), pltpu.VMEM((n, hidden), bf)],
        compiler_params=pltpu.CompilerParams(vmem_limit_bytes=VM_F * MIB),
        cost_estimate=pl.CostEstimate(flops=1_000_000, bytes_accessed=1000, transcendentals=0),
        name="feed",
    )(*args, *extra)


def scores_back(js, c, qa, k_ref, v_ref, doa, caug, dm, sums):
    width = k_ref.shape[1]
    step = 192 if c % 192 == 0 else c
    lane = lax.broadcasted_iota(jnp.int32, (step, 128), 1)
    ones = jnp.ones((step, 128), bf)
    def pair(j, carry):
        sl = columns(j, 128)
        k_t = k_ref[0:c, sl].T
        dqt = [None, None]
        dvsum = None
        for start in range(0, c, step):
            cs = slice(start, start + step)
            dvs, dks = [], []
            for e in range(2):
                hs = columns(2 * j + e, 128)
                own = (lane < 64) if e == 0 else (lane >= 64)
                kp = jnp.where(own, k_ref[cs, sl], caug[cs, :])
                vp = jnp.where(own, v_ref[cs, sl], ones)
                p = jnp.exp(mm_nt(kp, qa[0:c, hs]))
                ds = (p * mm_nt(vp, doa[0:c, hs])).astype(bf)
                dvs.append(mm(p.astype(bf), doa[0:c, hs]))
                dks.append(mm(ds, qa[0:c, hs]))
                t = mm(k_t[64 * e:64 * e + 64, cs], ds)
                dqt[e] = t if dqt[e] is None else dqt[e] + t
            dm[cs, columns(j, 128, width)] = jnp.where(lane < 64, dks[0], dks[1]).astype(bf)
            dv = jnp.where(lane < 64, dvs[0], dvs[1])
            dm[cs, columns(j, 128, 2 * width)] = dv.astype(bf)
            s = jnp.sum(dv, axis=0, keepdims=True)
            dvsum = s if dvsum is None else dvsum + s
        dq = jnp.concatenate(dqt, axis=0).T * 0.125
        dm[0:c, sl] = dq.astype(bf)
        sums[0:1, sl] = jnp.sum(dq, axis=0, keepdims=True)
        sums[1:2, sl] = dvsum
        return carry

    repeat(js[0], js[-1] + 1, pair, c < k_ref.shape[0])


def norm_back(c, slots, x_ref, gm, dm, vec_ref, wqkv, g_refs, nrm_ref):
    vec = lambda i: vec_ref[i:i + 1, :]
    gf = mm_nt(dm[0:c, :], wqkv[...])
    xh, r = normalise(x_ref[0:c, :].astype(f32))
    nrm_ref[0:c, :] = (xh * vec(0) + vec(1)).astype(bf)
    gg = gf * vec(0)
    gx = (gm[0:c, :] + r * (gg - row_mean(gg) - xh * row_mean(gg * xh))).astype(bf)
    for i, ref in enumerate(g_refs):
        ref[...] = mm_tn(mover(slots, i, c, ref.shape[0]), gx).astype(bf)
    return jnp.sum(gf * xh, axis=0, keepdims=True), jnp.sum(gf, axis=0, keepdims=True)


def start_kernel(slots, qa, k_ref, v_ref, doa, caug, dm, sums):
    sums[...] = jnp.zeros_like(sums)
    for_rows(
        kept_count(slots), k_ref.shape[0], lambda c: scores_back([0], c, qa, k_ref, v_ref, doa, caug, dm, sums))


def start_call(slots, *attn):
    n, width = attn[1].shape
    return small_call(start_kernel, (slots, *attn), [((n, 3 * width), bf), ((8, width), f32)], "start", VM_B)


def back_kernel(parts, started, *refs):
    slots, attn, (vec_ref, wqkv, x_ref, gm) = refs[0], refs[1:6], refs[6:10]
    refs = refs[10:]
    if started:
        dm0, sums0 = refs[:2]
        refs = refs[2:]
    dm, sums = refs[:2]
    n, width = gm.shape

    def body(c):
        pairs = range(width // 128)
        if started:
            sums[...] = sums0[...]
            for s in range(3):
                dm[0:c, width * s:width * s + 128] = dm0[0:c, width * s:width * s + 128]
            pairs = pairs[1:]
        else:
            sums[...] = jnp.zeros_like(sums)
        scores_back(pairs, c, *attn, dm, sums)
        if parts:
            gain, shift = norm_back(c, slots, x_ref, gm, dm, vec_ref, wqkv, refs[2:2 + parts], refs[-1])
            sums[2:3, :] = gain
            sums[3:4, :] = shift

    for_rows(kept_count(slots), n, body)


def back_call(slots, attn, rows, parts, vec, wqkv, x, gm, started=()):
    n, width = attn[1].shape
    outs = [((n, 3 * width), bf), ((8, width), f32)]
    if parts:
        outs += [((rows, width), bf)] * parts + [((n, width), bf)]
    return small_call(
        lambda *refs: back_kernel(parts, len(started) > 0, *refs),
        (slots, *attn, vec, wqkv, x, gm, *started), outs, "back", VM_B)


def last_kernel(parts, own, *refs):
    x_ref, gm, vec_ref, wqkv, dwo = refs[:5]
    refs = refs[5:]
    slots, dms, sums, nrms = refs[:own], refs[own:2 * own], refs[2 * own:3 * own], list(refs[3 * own:4 * own - 1])
    packed, sm, g_refs, nrm_s = refs[4 * own - 1], refs[4 * own], refs[4 * own + 1:-1], refs[-1]
    n, width = gm.shape
    nrms.append(nrm_s)
    total = sum(ref[0:4, :] for ref in sums)
    sm[...] = jnp.zeros_like(sm)
    sm[2:4, :] = total[0:2, :]

    def finish(c):
        gain, shift = norm_back(c, slots[-1], x_ref, gm, dms[-1], vec_ref, wqkv, g_refs, nrm_s)
        sm[0:1, :] = total[2:3, :] + gain
        sm[1:2, :] = total[3:4, :] + shift

    for_rows(kept_count(slots[-1]), n, finish)
    for i in range(own):

        def add(c, i=i):
            nrm_t = nrms[i][0:c, :].T

            def block(s, carry):
                js = columns(s, width)
                value = mm(nrm_t, dms[i][0:c, js])
                packed[js, :] = value if i == 0 else packed[js, :] + value
                return carry

            repeat(0, 3, block, c < n)

        for_rows(kept_count(slots[i]), n, add)
    packed[3 * width:4 * width, :] = dwo[...]
    if packed.shape[0] > 4 * width:
        packed[4 * width:, :] = jnp.zeros((packed.shape[0] - 4 * width, width), f32)


def last_call(packed_rows, rows, parts, x, gm, vec, wqkv, slots, dms, sums, nrms, dwo):
    own = len(dms)
    n, width = gm.shape
    outs = [((packed_rows, width), f32), ((16, width), f32)] + [((rows, width), bf)] * parts
    return small_call(
        lambda *refs: last_kernel(parts, own, *refs), (x, gm, vec, wqkv, dwo, *slots, *dms, *sums, *nrms), outs, "last",
        VM_W, scratch=[pltpu.VMEM((n, width), bf)])


def aligned(start, rows):
    return pl.ds(pl.multiple_of(start, 16), rows)


def tree_sum(parts):
    while len(parts) > 1:
        parts = [parts[i] + parts[i + 1] for i in range(0, len(parts), 2)]
    return parts[0]


def store_small(ref, at, small):
    rows = small.shape[0]
    high = small.astype(bf)
    ref[at:at + rows, :] = high
    ref[at + rows:at + 2 * rows, :] = (small - high.astype(f32)).astype(bf)


def load_small(ref, at, rows):
    return ref[at:at + rows, :].astype(f32) + ref[at + rows:at + 2 * rows, :].astype(f32)


def rounded(small):
    high, low = split2(small)
    return high.astype(f32) + low.astype(f32)


def core_kernel(big, small, out):
    half = big.shape[0] // 2
    other = 1 - (lax.axis_index("dp") & 1)
    out[0:half, :] = big[aligned(other * half, half), :].astype(bf)
    store_small(out, half, small[...])


def core_call(big, small):
    rows, width = big.shape
    return small_call(core_kernel, (big, small), [((rows // 2 + 2 * small.shape[0], width), bf)], "core", 4)[0]


def plane_kernel(big, small, got, *outs):
    sends, keep, total = outs[:-2], outs[-2], outs[-1]
    half, rows = big.shape[0] // 2, keep.shape[0]
    dp = lax.axis_index("dp")
    base, mine = (dp & 1) * half, dp >> 1
    summed = rounded(small[...]) + load_small(got, half, small.shape[0])
    total[...] = summed
    for k in range(len(sends) + 1):
        at = (mine ^ k) * rows
        value = big[aligned(base + at, rows), :] + got[aligned(at, rows), :].astype(f32)
        if k == 0:
            keep[...] = value
        else:
            sends[k - 1][0:rows, :] = value.astype(bf)
            store_small(sends[k - 1], rows, summed)


def plane_call(big, small, got, count):
    width, s = big.shape[1], small.shape[0]
    rows = big.shape[0] // 2 // count
    outs = [((rows + 2 * s, width), bf)] * (count - 1) + [((rows, width), f32), ((s, width), f32)]
    o = small_call(plane_kernel, (big, small, got), outs, "plane", 4)
    return o[:count - 1], o[-2], o[-1]


def halve_kernel(shift, count, rider, *refs):
    kept, small, gots, riding = refs[0], refs[1], refs[2:2 + count], refs[2 + count:2 + count + rider]
    send, keep, total = refs[2 + count + rider:]
    whole, rows, s = kept.shape[0], keep.shape[0], small.shape[0]
    mine = (lax.axis_index("seq") >> shift) & 1
    summed = tree_sum([rounded(small[...])] + [load_small(got, whole, s) for got in gots])
    total[...] = summed
    for k in range(2):
        at = (mine ^ k) * rows
        value = tree_sum([kept[aligned(at, rows), :]] + [got[aligned(at, rows), :].astype(f32) for got in gots])
        if k == 0:
            keep[...] = value
        else:
            send[0:rows, :] = value.astype(bf)
    store_small(send, rows, summed)
    at = rows + 2 * s
    for ref in riding:
        send[at:at + ref.shape[0], :] = ref[...]
        at += ref.shape[0]


def halve_call(kept, small, gots, shift, riders=()):
    width, s = kept.shape[1], small.shape[0]
    rows = kept.shape[0] // 2
    outs = [((rows + 2 * s + sum(x.shape[0] for x in riders), width), bf), ((rows, width), f32), ((s, width), f32)]
    return small_call(
        lambda *refs: halve_kernel(shift, len(gots), len(riders), *refs),
        (kept, small, *gots, *riders), outs, "halve", 6)


def spread_kernel(learns, rider, *refs):
    kept, small, got = refs[:3]
    learnt, riding = refs[3:3 + learns], refs[3 + learns:3 + learns + rider]
    total, part = refs[3 + learns + rider:]
    rows, s = kept.shape[0], small.shape[0]
    total[...] = rounded(small[...]) + load_small(got, rows, s)
    part[0:rows, :] = (kept[...] + got[0:rows, :].astype(f32)).astype(bf)
    at = rows
    if learns:
        used = sum(ref.shape[0] for ref in learnt)
        blank = [jnp.zeros((-used % 16, kept.shape[1]), f32)] if used % 16 else []
        learnt = jnp.concatenate([ref[...] for ref in learnt] + blank, axis=0)
        part[rows:rows + learnt.shape[0], :] = learnt.astype(bf)
        at += learnt.shape[0]
    for ref in riding:
        part[at:at + ref.shape[0], :] = ref[...]
        at += ref.shape[0]


def learned_rows(learns):
    used = sum(ref.shape[0] for ref in learns)
    return used + -used % 16


def spread_call(kept, small, got, learns=(), riders=()):
    rows, width = kept.shape
    rows += learned_rows(learns) + sum(ref.shape[0] for ref in riders)
    outs = [(small.shape, f32), ((rows, width), bf)]
    total, part = small_call(
        lambda *refs: spread_kernel(len(learns), len(riders), *refs), (kept, small, got, *learns, *riders), outs, "spread", 6)
    return part, total


def join_kernel(axis, shift, rows, riding, count, extra, *refs):
    parts, extras, out = refs[:count], refs[count:count + extra], refs[count + extra]
    mine = (lax.axis_index(axis) >> shift) & (count - 1)
    for k, part in enumerate(parts):
        out[aligned((mine ^ k) * rows, rows), :] = part[0:rows, :]
        if riding:
            out[aligned(count * rows + (mine ^ k) * riding, riding), :] = part[rows:rows + riding, :]
    at = count * (rows + riding)
    for ref in extras:
        out[at:at + ref.shape[0], :] = ref[...]
        at += ref.shape[0]


def join_call(parts, axis, shift, rows, riding=0, extras=()):
    width = parts[0].shape[1]
    total = (rows + riding) * len(parts) + sum(x.shape[0] for x in extras)
    return small_call(
        lambda *refs: join_kernel(axis, shift, rows, riding, len(parts), len(extras), *refs), (*parts, *extras),
        [((total, width), bf)], "join", 6)[0]


def first_kernel(x, out):
    out[...] = x[0:out.shape[0], :]


def first_rows(x, rows):
    return small_call(first_kernel, (x,), [((rows, x.shape[1]), x.dtype)], "first", 4)[0]


def small_call(kernel, args, outs, name, mib, scratch=()):
    vm = pl.BlockSpec(memory_space=pltpu.VMEM)
    return pl.pallas_call(
        kernel,
        out_shape=[jax.ShapeDtypeStruct(s, d) for s, d in outs],
        in_specs=[vm] * len(args), out_specs=[vm] * len(outs), scratch_shapes=list(scratch),
        compiler_params=pltpu.CompilerParams(vmem_limit_bytes=mib * MIB),
        cost_estimate=pl.CostEstimate(flops=1_000_000, bytes_accessed=1000, transcendentals=0),
        name=name,
    )(*args)


def prepare_kernel(own, rows, depth, patches, keep, valid, count, *refs):
    blocks, (keep_s, sems) = refs[:2 * depth], refs[2 * depth:]
    width = patches.shape[2]
    me = lax.axis_index("seq")
    flags_copy = pltpu.make_async_copy(keep, keep_s, sems.at[depth * own])
    flags_copy.start()
    copies = []
    for k in [k for k in range(1, depth)] + [0]:
        for i in range(own):
            target = blocks[2 * k].at[0:rows, :] if i == 0 else blocks[2 * k + 1].at[rows * (i - 1):rows * i, :]
            copies.append(pltpu.make_async_copy(patches.at[(me ^ k) * own + i], target, sems.at[k * own + i]))
            copies[-1].start()
    total = valid[0]
    for i in range(1, valid.shape[0]):
        total = total + valid[i]
    count[...] = jnp.full(count.shape, total.astype(f32), f32)
    flags_copy.wait()
    line = lax.broadcasted_iota(jnp.int32, (16, rows), 0)
    for k in range(depth):
        flags = jnp.zeros((16, rows), f32)
        for i in range(own):
            flags = jnp.where(line == i, keep_s[pl.ds((me ^ k) * own + i, 1), :].astype(f32), flags)
        blocks[2 * k][rows:rows + 16, :] = jnp.zeros((16, width), bf)
        blocks[2 * k][rows:rows + 16, 0:rows] = flags.astype(bf)
    for copy in copies:
        copy.wait()


def prepare_call(depth, patches, keep, valid):
    images, rows, width = patches.shape
    own = images // depth
    vm, hbm = pl.BlockSpec(memory_space=pltpu.VMEM), pl.BlockSpec(memory_space=pltpu.HBM)
    outs = [((8, 128), f32)]
    for k in range(depth):
        outs += [((rows + 16, width), bf), ((rows * (own - 1), width), bf)]
    o = pl.pallas_call(
        lambda *refs: prepare_kernel(own, rows, depth, *refs),
        out_shape=[jax.ShapeDtypeStruct(s, d) for s, d in outs],
        in_specs=[hbm, hbm, pl.BlockSpec(memory_space=pltpu.SMEM)], out_specs=[vm] * len(outs),
        scratch_shapes=[pltpu.VMEM(keep.shape, keep.dtype), pltpu.SemaphoreType.DMA((depth * own + 1,))],
        compiler_params=pltpu.CompilerParams(vmem_limit_bytes=8 * MIB),
        cost_estimate=pl.CostEstimate(flops=1_000_000, bytes_accessed=1000, transcendentals=0),
        name="prepare",
    )(in_hbm(patches), in_hbm(keep), valid)
    return o[0], o[1::2], o[2::2]


def vectors_kernel(own, mapw, cot, *refs):
    half = (len(refs) - 4) // 2
    sources, vec, mb, cm, held, sems = refs[:half], refs[half], refs[half + 1], refs[half + 2], refs[half + 3:-1], refs[-1]
    copies = [pltpu.make_async_copy(a, b, sems.at[i]) for i, (a, b) in enumerate(zip(sources, held))]
    for copy in copies:
        copy.start()
    vec[...] = jnp.zeros_like(vec)
    me = lax.axis_index("seq")
    for i in range(own):
        cm[i] = jnp.concatenate([mapw[...].astype(f32), cot[me * own + i].astype(f32)], axis=0).astype(bf)
    for copy in copies:
        copy.wait()
    width, tokens = vec.shape[1], mb.shape[0]
    line = 0
    for ref in held[:-1]:
        for j in range(ref.shape[0] // width):
            vec[line, :] = ref[width * j:width * (j + 1)].astype(f32)
            line += 1
    bias = jnp.broadcast_to(held[-1][...].astype(f32).reshape(1, tokens), (tokens, tokens))
    diag = lax.broadcasted_iota(jnp.int32, (tokens, tokens), 0) == lax.broadcasted_iota(jnp.int32, (tokens, tokens), 1)
    mb[...] = jnp.broadcast_to(jnp.sum(jnp.where(diag, bias, 0.0), axis=1, keepdims=True), mb.shape)


def vectors_call(own, mapw, cot, *sources):
    width, tokens = sources[0].shape[0], sources[-1].shape[0]
    vm, hbm = pl.BlockSpec(memory_space=pltpu.VMEM), pl.BlockSpec(memory_space=pltpu.HBM)
    outs = [((16, width), f32), ((tokens, 128), f32), ((own, 2 * tokens, width), bf)]
    return pl.pallas_call(
        lambda *refs: vectors_kernel(own, *refs),
        out_shape=[jax.ShapeDtypeStruct(s, d) for s, d in outs],
        in_specs=[vm] * 2 + [hbm] * len(sources), out_specs=[vm] * 3,
        scratch_shapes=[pltpu.VMEM(s.shape, s.dtype) for s in sources] + [pltpu.SemaphoreType.DMA((len(sources),))],
        compiler_params=pltpu.CompilerParams(vmem_limit_bytes=4 * MIB),
        cost_estimate=pl.CostEstimate(flops=1_000_000, bytes_accessed=1000, transcendentals=0),
        name="vectors",
    )(mapw, cot, *map(in_hbm, sources))


def plus_kernel(a, b, out):
    out[...] = a[...] + b[...]


def unpack_kernel(hidden, own, base, a0, a1, sm_ref, rider, count_ref, gdn, gup, down, outb, gain, shift, upb, mapw, mapb, learned, penalty, a_s):
    side = lax.axis_index("dp") & 1
    half, width = a0.shape
    a_s[pl.ds(pl.multiple_of(side * half, 16), half), :] = a0[...]
    a_s[pl.ds(pl.multiple_of((1 - side) * half, 16), half), :] = a1[...]
    blocks = hidden // width
    for j in range(blocks):
        js = slice(width * j, width * (j + 1))
        gdn[js, :] = a_s[js, :].T.astype(f32)
        gup[:, js] = a_s[width * (blocks + j):width * (blocks + j + 1), :].astype(f32)
    for i, ref in enumerate((down, outb, gain, shift)):
        ref[...] = sm_ref[i, :]
    for j in range(blocks):
        upb[width * j:width * (j + 1)] = sm_ref[4 + j, :]
    mapw[...] = sm_ref[8:16, :]
    tokens = learned.shape[1]
    penalty[...] = sm_ref[16:17, tokens:tokens + 1] / count_ref[0:1, 0:1]
    mapb[...] = sm_ref[16, 0:tokens]
    count = own * tokens
    depth = learned.shape[0] // own
    bits = depth.bit_length() - 1
    for z in range(depth):
        place = sum(((z >> b) & 1) << (bits - 1 - b) for b in range(bits))
        span = count + -count % 16
        at = base + span * place
        both = rider[at:at + span, :].astype(f32)
        for i in range(own):
            learned[z * own + i] = both[tokens * i:tokens * (i + 1), :]


def unpack_call(hidden, tokens, images, own, base, a0, a1, sm, rider, count):
    width = a0.shape[1]
    vm = pl.BlockSpec(memory_space=pltpu.VMEM)
    outs = [(hidden, width), (width, hidden)] + [(width,)] * 4 + [(hidden,), (tokens, width), (tokens,)]
    outs += [(images, tokens, width), (1, 1)]
    return pl.pallas_call(
        lambda *refs: unpack_kernel(hidden, own, base, *refs),
        out_shape=[jax.ShapeDtypeStruct(s, f32) for s in outs],
        in_specs=[vm] * 5, out_specs=[vm] * len(outs),
        scratch_shapes=[pltpu.VMEM((2 * a0.shape[0], width), bf)],
        compiler_params=pltpu.CompilerParams(vmem_limit_bytes=16 * MIB),
        cost_estimate=pl.CostEstimate(flops=1_000_000, bytes_accessed=1000, transcendentals=0),
        name="unpack",
    )(a0, a1, sm, rider, count)


def finish_kernel(b0, b1, sm_ref, gqkv, gout, gain, shift, biases, b_s):
    side = lax.axis_index("dp") & 1
    half, width = b0.shape
    b_s[pl.ds(pl.multiple_of(side * half, 16), half), :] = b0[...]
    b_s[pl.ds(pl.multiple_of((1 - side) * half, 16), half), :] = b1[...]
    for j in range(3):
        js = slice(width * j, width * (j + 1))
        gqkv[:, js] = b_s[js, :].astype(f32)
    gout[...] = b_s[3 * width:4 * width, :].astype(f32)
    gain[...] = sm_ref[0, :]
    shift[...] = sm_ref[1, :]
    for j in range(2):
        biases[width * j:width * (j + 1)] = sm_ref[2 + j, :]


def finish_call(b0, b1, sm):
    width = b0.shape[1]
    vm = pl.BlockSpec(memory_space=pltpu.VMEM)
    outs = [(width, 3 * width), (width, width), (width,), (width,), (2 * width,)]
    return pl.pallas_call(
        finish_kernel,
        out_shape=[jax.ShapeDtypeStruct(s, f32) for s in outs],
        in_specs=[vm] * 3, out_specs=[vm] * len(outs),
        scratch_shapes=[pltpu.VMEM((2 * b0.shape[0], width), bf)],
        compiler_params=pltpu.CompilerParams(vmem_limit_bytes=8 * MIB),
        cost_estimate=pl.CostEstimate(flops=1_000_000, bytes_accessed=1000, transcendentals=0),
        name="finish",
    )(b0, b1, sm)


def place_kernel(parts, bases, *refs):
    out = refs[-1]
    own, rows = len(bases) // parts, out.shape[1]
    me = lax.axis_index("seq")
    for i in range(own):
        for k in range(parts):
            base = bases[i * parts + k]
            out[(me ^ k) * own + i] = refs[i * parts + k][base:base + rows, :].astype(f32)


def place_call(sent, rows):
    own, parts = len(sent), len(sent[0])
    width = sent[0][0][0].shape[1]
    bases = [base for image in sent for _, base in image]
    return small_call(
        lambda *refs: place_kernel(parts, bases, *refs), [x for image in sent for x, _ in image],
        [((parts * own, rows, width), f32)], "place", 8)[0]


VM_A, VM_F, VM_B, VM_W = 12, 26, 14, 14


def xor_permute(x, axis, k):
    return lax.ppermute(x, axis, [(i, i ^ k) for i in range(lax.axis_size(axis))])


def after(x, *others):
    if not others:
        return x
    return lax.optimization_barrier((x,) + others)[0]


def plane_exchange(sends):
    return [xor_permute(x, "dp", (k + 1) << 1) for k, x in enumerate(sends)]


def to_peers(part, axis, count, shift):
    return [part] + [xor_permute(part, axis, k << shift) for k in range(1, count)]


def padded(rows, unit):
    return rows + -rows % unit


def per_device(
    patches, first_gain, first_shift, qkv_weight, query_value_bias, out_weight, out_bias,
    second_gain, second_shift, up_weight, up_bias, down_weight, down_bias, map_weight, map_bias,
    keep_mask, image_valid, token_cotangent,
):
    images, rows, width = patches.shape
    depth, dps = lax.axis_size("seq"), lax.axis_size("dp")
    chips = dps // 2
    own = images // depth
    hidden, tokens = up_weight.shape[1], map_weight.shape[1]
    pairs = width // 128
    unit = 16 * dps * depth
    rows_a, rows_b = padded(2 * hidden, unit), padded(4 * width, unit)

    count, first_blocks, rest_blocks = prepare_call(depth, patches, keep_mask, image_valid)
    order = sorted(range(1, depth), key=lambda k: (k == 1, k))

    def collect(blocks, holds):
        got = [blocks[0]] + [None] * (depth - 1)
        for k in order:
            got[k] = xor_permute(after(blocks[k], *holds), "seq", k)
        return got

    first = collect(first_blocks, [])
    vec, mb, cm = vectors_call(
        own, map_weight.T, token_cotangent, first_gain, first_shift, query_value_bias, out_bias, second_gain,
        second_shift, down_bias, up_bias, map_bias)
    plus = lambda a, b: small_call(plus_kernel, (a, b), [((8, 128), f32)], "plus", 1)[0]
    step, holds = 1, list(first[1:])
    while step < dps:
        if step == 2:
            count = after(count, vec)
        if step == dps // 2:
            holds.append(count)
            count_got = xor_permute(count, "dp", step)
        else:
            count = plus(count, xor_permute(count, "dp", step))
        step *= 2
    rest = collect(rest_blocks, holds)

    saved, learns = [], []
    bases = [0] + [rows * i for i in range(own - 1)]
    acc = dwo = sm = tok = None
    for i in range(own):
        v = vec if tok is None else after(vec, tok)
        qa, key, val, caug, att, mid, x, slots = attend_call(
            first if i == 0 else rest, first, i, bases[i], rows, v, qkv_weight, out_weight)
        if i == 0:
            count = plus(after(count, caug), count_got)
        gm, doa, learn, acc, dwo, sm = feed_call(
            i, own, rows_a, mid, att, slots, vec, mb, cm, image_valid, count,
            out_weight, up_weight, down_weight, acc, dwo, sm)
        tok = sm
        saved.append((qa, key, val, doa, caug, gm, x, slots))
        learns.append(learn)

    got = xor_permute(core_call(acc, sm), "dp", 1)
    bits = depth.bit_length() - 1
    dms, sums, nrms, sent = [], [], [], []
    for i in range(own):
        qa, key, val, doa, caug, gm, x, slots = saved[i]
        started = ()
        if i == 0:
            started = start_call(slots, qa, key, val, doa, after(caug, tok))
            sends, kept, small = plane_call(acc, after(sm, started[1]), got, chips)
            gots = plane_exchange(sends)
            tok = small
        o = back_call(
            slots, (qa, key, val, doa, after(caug, tok)), rows, depth if i < own - 1 else 0, vec, qkv_weight, x, gm, started)
        dms.append(o[0])
        sums.append(o[1])
        tok = o[1]
        leaving = o[2:2 + depth]
        if i < own - 1:
            nrms.append(o[-1])
        if i == own - 2:
            riders = [s[1][0] for s in sent]
            send, kept, small = halve_call(
                kept, after(small, tok, *[x for s in sent for x, _ in s[2:]]), gots, 0, riders)
            got = xor_permute(send, "seq", 1)
            base = kept.shape[0] + 2 * small.shape[0]
            for m, s in enumerate(sent):
                s[1] = (got, base + rows * m)
            tok = small
        if i < own - 1:
            near = (xor_permute(leaving[1], "seq", 1), 0) if i == own - 2 else (leaving[1], 0)
            far = [(xor_permute(x, "seq", k), 0) for k, x in enumerate(leaving) if k > 1]
            sent.append([(leaving[0], 0), near] + far)
    for bit in range(1, bits):
        send, kept, small = halve_call(kept, after(small, tok), [got], bit)
        got = xor_permute(send, "seq", 1 << bit)
        tok = small
    o = last_call(
        rows_b, rows, depth, saved[-1][6], saved[-1][5], after(vec, tok), qkv_weight, [s[7] for s in saved], dms, sums,
        nrms, dwo)
    bigb, smb, tail = o[0], o[1], o[2:]
    early = [x for x, _ in sent[-1][1:]]
    part, small = spread_call(kept, small, got, learns)
    gotb = xor_permute(core_call(bigb, after(smb, small)), "dp", 1)
    size, riding = kept.shape[0], learned_rows(learns)
    got = xor_permute(part, "seq", depth // 2)
    sends, keptb, smallb = plane_call(bigb, smb, gotb, chips)
    gotsb = plane_exchange(sends)
    smallb = after(smallb, *early)
    steps = list(reversed(range(bits)))
    for m, bit in enumerate(steps):
        send, keptb, smallb = halve_call(keptb, smallb, gotsb, bit)
        gotsb = [xor_permute(send, "seq", 1 << bit)]
        part = join_call([after(part, smallb), got], "seq", bit, size, riding)
        size, riding = 2 * size, 2 * riding
        if bit:
            got = xor_permute(part, "seq", 1 << (bit - 1))
    rider = part
    peers = to_peers(first_rows(part, size), "dp", chips, 1)
    late = [tail[0]] + [xor_permute(after(x, smallb), "seq", k) for k, x in enumerate(tail) if k and k % 2 == 0]
    piece = keptb.shape[0]
    partb, smallb = spread_call(keptb, smallb, gotsb[0], (), [tail[1]])
    odd = [xor_permute(after(x, smallb), "seq", k) for k, x in enumerate(tail) if k % 2 and k > 1]
    for bit in range(bits):
        other = xor_permute(partb, "seq", 1 << bit)
        if bit == 0:
            nearest = (other, piece)
        partb = join_call([after(partb, *(late[1:] if bit == 0 else odd)), other], "seq", bit, piece << bit)
    sent.append([(tail[0], 0), nearest] + [
        (late[k // 2] if k % 2 == 0 else odd[k // 2 - 1], 0) for k in range(2, depth)])
    outs = place_call(sent, rows)
    part = join_call([after(peers[0], partb)] + peers[1:], "dp", 1, size)
    a0, a1 = part, xor_permute(part, "dp", 1)
    unpacked = unpack_call(hidden, tokens, images, own, size, a0, a1, small, rider, count)
    gdn, gup, gb_down, gb_out, g_gain2, g_shift2, gb_up, gmapw, gmapb, learned, penalty = unpacked
    peers = to_peers(partb, "dp", chips, 1)
    partb = join_call([after(peers[0], gmapw, outs)] + peers[1:], "dp", 1, partb.shape[0])
    b0, b1 = partb, xor_permute(partb, "dp", 1)
    gqkv, gout, g_gain1, g_shift1, gqv = finish_call(b0, b1, smallb)
    return (
        learned, penalty.reshape(()), outs, g_gain1, g_shift1, gqkv, gqv, gout, gb_out, g_gain2, g_shift2, gup,
        gb_up, gdn, gb_down, gmapw.T, gmapb,
    )


def solution(mesh):
    rep = P()
    placed = (P("dp", "seq", None),) + (rep,) * 14 + (P("dp", "seq"), P("dp"), P("dp", None, None))
    return jax.shard_map(
        per_device, mesh=mesh, in_specs=placed,
        out_specs=(P("dp", None, None), rep, P("dp", "seq", None)) + (rep,) * 14,
        check_vma=False,
    )
```

```python
import jax
import jax.numpy as jnp
from jax import lax
from jax.experimental import pallas as pl
from jax.experimental.pallas import tpu as pltpu
from jax.sharding import PartitionSpec as P

f32, bf = jnp.float32, jnp.bfloat16
EPSILON = 1e-6
MASKED = -1e30
MIB = 1 << 20


def in_hbm(x):
    return pltpu.with_memory_space_constraint(x, pltpu.HBM)


def mm(a, b):
    return lax.dot_general(a, b, (((1,), (0,)), ((), ())), preferred_element_type=f32)


def mm_nt(a, b):
    return lax.dot_general(a, b, (((1,), (1,)), ((), ())), preferred_element_type=f32)


def mm_tn(a, b):
    return lax.dot_general(a, b, (((0,), (0,)), ((), ())), preferred_element_type=f32)


def row_mean(x):
    return jnp.sum(x, axis=-1, keepdims=True) * (1.0 / x.shape[-1])


def normalise(x):
    centred = x - row_mean(x)
    r = lax.rsqrt(row_mean(centred * centred) + EPSILON)
    return centred * r, r


def normal_parts(v):
    expo = jnp.exp(v * v * (-0.5))
    t = 1.0 / (1.0 + jnp.abs(v) * (0.3275911 * 0.7071067811865476))
    series = t * (0.127414796 + t * (-0.142248368 + t * (0.7107068705 + t * (-0.7265760135 + t * 0.5307027145))))
    tail = series * expo
    return jnp.where(v >= 0, 1.0 - tail, tail), expo * 0.3989422804014327


def split2(a):
    high = a.astype(bf)
    return high, (a - high.astype(f32)).astype(bf)


def columns(j, count, base=0):
    if isinstance(j, int):
        return slice(base + j * count, base + (j + 1) * count)
    return pl.ds(pl.multiple_of(base + j * count, 128), count)


def row_at(j):
    return slice(j, j + 1) if isinstance(j, int) else pl.ds(j, 1)


def repeat(first, last, body, straight):
    if straight:
        for j in range(first, last):
            body(j, 0)
    else:
        lax.fori_loop(first, last, body, 0)


def row_counts(n):
    return [c for c in (384,) if c < n] + [n]


def for_rows(count, n, body):
    below = 0.0
    for c in row_counts(n):
        pl.when((count > below) & (count <= float(c)))(lambda c=c: body(c))
        below = float(c)


def kept_count(slots):
    return jnp.max(slots[4:5, 0:128])


def mover(slots, i, c, rows):
    at = lax.broadcasted_iota(jnp.int32, (c, rows), 0).astype(f32)
    return jnp.where(at == slots[i:i + 1, 0:rows], 1.0, 0.0).astype(bf)


def attend_kernel(parts, rows, slot, base, *refs):
    x_refs, flag_refs = refs[:parts], refs[parts:2 * parts]
    vec_ref, wqkv, wout = refs[2 * parts:2 * parts + 3]
    qa_ref, k_ref, v_ref, caug_ref, att_ref, mid_ref, x_ref, slots = refs[2 * parts + 3:2 * parts + 11]
    nrm_s, q_s = refs[2 * parts + 11:]
    n, width = nrm_s.shape
    vec = lambda i: vec_ref[i:i + 1, :]
    before = lax.broadcasted_iota(jnp.int32, (rows, rows), 0) < lax.broadcasted_iota(jnp.int32, (rows, rows), 1)
    before = jnp.where(before, 1.0, 0.0).astype(bf)
    total = jnp.zeros((1, 1), f32)
    slots[...] = jnp.full(slots.shape, -1.0, f32)
    for i in range(parts):
        keep = flag_refs[i][rows:rows + 16, 0:rows].astype(f32)[slot:slot + 1, :]
        rank = mm(jnp.broadcast_to(keep, (8, rows)).astype(bf), before)[0:1, :] + total
        slots[i:i + 1, 0:rows] = jnp.where(keep > 0.0, rank, -1.0)
        total = total + jnp.sum(keep, axis=-1, keepdims=True)
    slots[4:5, :] = jnp.broadcast_to(total, (1, slots.shape[1]))

    def body(c):
        x = None
        for i in range(parts):
            t = mm(mover(slots, i, c, rows), x_refs[i][base:base + rows, :])
            x = t if x is None else x + t
        x_ref[0:c, :] = x.astype(bf)
        xh, _ = normalise(x)
        nrm_s[0:c, :] = (xh * vec(0) + vec(1)).astype(bf)
        nrm = nrm_s[0:c, :]
        q_s[0:c, :] = (mm(nrm, wqkv[:, 0:width]) + vec(2)).astype(bf) * jnp.asarray(0.125, bf)
        k_ref[0:c, :] = mm(nrm, wqkv[:, width:2 * width]).astype(bf)
        v_ref[0:c, :] = (mm(nrm, wqkv[:, 2 * width:3 * width]) + vec(3)).astype(bf)
        lane = lax.broadcasted_iota(jnp.int32, (c, 128), 1)
        lane64 = lane & 63
        real = lax.broadcasted_iota(jnp.int32, (c, 128), 0).astype(f32) < slots[4:5, 0:128]
        caug_ref[0:c, :] = jnp.where(
            lane64 == 3, jnp.where(real, 0.0, MASKED), jnp.where(lane64 < 3, 1.0, 0.0)).astype(bf)
        ones = jnp.ones((c, 128), bf)
        def pair(j, carry):
            sl = columns(j, 128)
            outs = []
            for e in range(2):
                own = (lane < 64) if e == 0 else (lane >= 64)
                kp = jnp.where(own, k_ref[0:c, sl], caug_ref[0:c, :])
                qp = jnp.where(own, q_s[0:c, sl], jnp.where(lane64 == 3, 1.0, 0.0).astype(bf))
                s = mm_nt(qp, kp)
                m = jnp.max(s, axis=-1, keepdims=True)
                p = jnp.exp(s - m).astype(bf)
                o = mm(p, jnp.concatenate([v_ref[0:c, sl], ones], axis=1))
                whole = o[:, 128:256]
                outs.append(o[:, 0:128] / whole)
                logs = -(m + jnp.log(whole))
                hi = logs.astype(bf).astype(f32)
                lo = (logs - hi).astype(bf).astype(f32)
                aug = jnp.where(lane64 == 0, hi, jnp.where(lane64 == 1, lo, jnp.where(
                    lane64 == 2, logs - hi - lo, jnp.where(lane64 == 3, 1.0, 0.0))))
                qa_ref[0:c, columns(2 * j + e, 128)] = jnp.where(own, q_s[0:c, sl], aug.astype(bf))
            att_ref[0:c, sl] = jnp.where(lane < 64, outs[0], outs[1]).astype(bf)
            return carry

        repeat(0, width // 128, pair, c < n and slot == 0)
        mid_ref[0:c, :] = x_ref[0:c, :].astype(f32) + mm(att_ref[0:c, :], wout[...]) + vec(4)

    for_rows(kept_count(slots), n, body)


def attend_call(pieces, flags, slot, base, rows, vec, wqkv, wout):
    parts, width = len(pieces), wout.shape[0]
    n = parts * rows
    outs = [((n, 2 * width), bf), ((n, width), bf), ((n, width), bf), ((n, 128), bf), ((n, width), bf), ((n, width), f32)]
    outs += [((n, width), bf), ((8, 256), f32)]
    return small_call(
        lambda *refs: attend_kernel(parts, rows, slot, base, *refs), (*pieces, *flags, vec, wqkv, wout), outs, "attend",
        VM_A, scratch=[pltpu.VMEM((n, width), bf), pltpu.VMEM((n, width), bf)])


def feed_kernel(slot, own_count, first, *refs):
    mid_ref, att_ref, slots, vec_ref, mb_ref, cm_ref, valid_ref, count_ref, wout, wup, wdn = refs[:11]
    refs = refs[11:]
    if first:
        acc_in = dwo_in = sm_in = None
    else:
        acc_in, dwo_in, sm_in = refs[:3]
        refs = refs[3:]
    gm_ref, doa_ref, learn_ref, acc, dwo, sm = refs[:6]
    sec_s, hid_s, gp_s, g_s, total, gt_s, st_s, gpl_s = refs[6:]
    n, width = mid_ref.shape
    blocks = hid_s.shape[1] // width
    tokens = mb_ref.shape[0]
    vec = lambda i: vec_ref[i:i + 1, :]
    place = lax.axis_index("seq") * own_count + slot

    def add(ref, ref_in, rows, value):
        ref[rows, :] = value if first else ref_in[rows, :] + value

    def body(c):
        xh, _ = normalise(mid_ref[0:c, :])
        sec_s[0:c, :] = (xh * vec(5) + vec(6)).astype(bf)
        def up(j, carry):
            js = columns(j, width)
            pre = mm(sec_s[0:c, :], wup[:, js]) + vec_ref[row_at(8 + j), :]
            upper, density = normal_parts(pre)
            hid_s[0:c, js] = (pre * upper).astype(bf)
            gp_s[0:c, js] = upper + pre * density
            return carry

        repeat(0, blocks, up, c < n)
        total[0:c, :] = mid_ref[0:c, :] + vec(7) + mm(hid_s[0:c, :], wdn[...])
        ohi, olo = split2(total[0:c, :])
        cm = cm_ref[slot]
        lg = mm_nt(cm, ohi) + mm_nt(cm, olo)
        kept = slots[4:5, 0:1]
        keep = jnp.where(lax.broadcasted_iota(jnp.int32, (1, c), 1).astype(f32) < kept, 1.0, 0.0)
        maps = jax.nn.sigmoid(lg[0:tokens, :] + mb_ref[:, 0:1])
        inverse = 1.0 / kept
        tot = jnp.sum(maps, axis=0, keepdims=True)
        inter = jnp.sum(keep * (tot * tot - jnp.sum(maps * maps, axis=0, keepdims=True)), axis=-1, keepdims=True)
        valid = valid_ref[place].astype(f32)
        gmaps = keep * (lg[tokens:2 * tokens, :] * inverse + (2.0 * valid / count_ref[0:1, 0:1]) * (tot - maps))
        gl = gmaps * maps * (1.0 - maps)
        mk = maps * keep
        mkh, mkl = split2(mk)
        glh, gll = split2(gl)
        st = jnp.concatenate([mkh.astype(f32), mkl.astype(f32), glh.astype(f32), gll.astype(f32)], axis=0).astype(bf)
        r1 = mm(st, ohi) + mm(st, olo)
        learn_ref[...] = (r1[0:tokens, :] + r1[tokens:2 * tokens, :]) * inverse
        add(sm, sm_in, slice(8, 16), r1[2 * tokens:3 * tokens, :] + r1[3 * tokens:, :])
        gah, gal = split2(mk * inverse)
        lhs = jnp.concatenate([glh.astype(f32), gah.astype(f32), gll.astype(f32), gal.astype(f32)], axis=0).astype(bf)
        g = mm_tn(lhs, jnp.concatenate([cm, cm], axis=0))
        g_s[0:c, :] = g
        add(sm, sm_in, slice(0, 1), jnp.sum(g, axis=0, keepdims=True))
        glow = g.astype(bf)
        gt_s[:, 0:c] = glow.T
        st_s[:, 0:c] = sec_s[0:c, :].T
        def down(j, carry):
            js = columns(j, width)
            gpre = mm_nt(glow, wdn[js, :]).astype(bf).astype(f32) * gp_s[0:c, js]
            gpl_s[0:c, js] = gpre.astype(bf)
            add(sm, sm_in, row_at(4 + j), jnp.sum(gpre, axis=0, keepdims=True))
            add(acc, acc_in, js, mm(gt_s[:, 0:c], hid_s[0:c, js]))
            add(acc, acc_in, columns(j, width, blocks * width), mm(st_s[:, 0:c], gpl_s[0:c, js]))
            return carry

        repeat(0, blocks, down, c < n)
        total[0:c, :] = mm_nt(gpl_s[0:c, :], wup[...])
        gsec = total[0:c, :]
        xh, r = normalise(mid_ref[0:c, :])
        gg = gsec * vec(5)
        gm = g_s[0:c, :] + r * (gg - row_mean(gg) - xh * row_mean(gg * xh))
        gm_ref[0:c, :] = gm
        gml = gm.astype(bf)
        add(sm, sm_in, slice(1, 2), jnp.sum(gm, axis=0, keepdims=True))
        add(sm, sm_in, slice(2, 3), jnp.sum(gsec * xh, axis=0, keepdims=True))
        add(sm, sm_in, slice(3, 4), jnp.sum(gsec, axis=0, keepdims=True))
        glb = jnp.sum(gl, axis=-1, keepdims=True)
        lr = lax.broadcasted_iota(jnp.int32, (8, width), 1)
        rr = lax.broadcasted_iota(jnp.int32, (8, width), 0)
        line = jnp.sum(jnp.where(lr == rr, glb, 0.0), axis=0, keepdims=True)
        line = line + jnp.where(lr[0:1] == tokens, valid * inter * (1.0 / n), 0.0)
        add(sm, sm_in, slice(16, 24), jnp.where(rr == 0, line, 0.0))
        if first:
            sm[24:32, :] = jnp.zeros((8, width), f32)
            if acc.shape[0] > 2 * blocks * width:
                acc[2 * blocks * width:, :] = jnp.zeros((acc.shape[0] - 2 * blocks * width, width), f32)
        else:
            sm[24:32, :] = sm_in[24:32, :]
            if acc.shape[0] > 2 * blocks * width:
                acc[2 * blocks * width:, :] = acc_in[2 * blocks * width:, :]
        add(dwo, dwo_in, slice(0, width), mm(att_ref[0:c, :].T, gml))
        do = mm_nt(gml, wout[...]).astype(bf).astype(f32)
        lane = lax.broadcasted_iota(jnp.int32, (c, 128), 1)
        lane64 = lane & 63
        for j in range(width // 128):
            sl = slice(128 * j, 128 * j + 128)
            dj = do[:, sl]
            pd = dj * att_ref[0:c, sl].astype(f32)
            for e in range(2):
                own = (lane < 64) if e == 0 else (lane >= 64)
                dl = -jnp.sum(jnp.where(own, pd, 0.0), axis=-1, keepdims=True)
                hi = dl.astype(bf).astype(f32)
                aug = jnp.where(lane64 == 0, hi, jnp.where(lane64 == 1, dl - hi, 0.0))
                h = 2 * j + e
                doa_ref[0:c, 128 * h:128 * h + 128] = jnp.where(own, dj, aug).astype(bf)

    for_rows(kept_count(slots), n, body)


def feed_call(slot, own_count, packed_rows, mid, att, slots, vec, mb, cm, valid, count, wout, wup, wdn, acc, dwo, sm):
    n, width = mid.shape
    hidden = wup.shape[1]
    first = acc is None
    vm = pl.BlockSpec(memory_space=pltpu.VMEM)
    smem = pl.BlockSpec(memory_space=pltpu.SMEM)
    outs = [((n, width), f32), ((n, 2 * width), bf), ((8, width), f32), ((packed_rows, width), f32), ((width, width), f32), ((32, width), f32)]
    args = (mid, att, slots, vec, mb, cm, valid, count, wout, wup, wdn)
    extra = () if first else (acc, dwo, sm)
    return pl.pallas_call(
        lambda *refs: feed_kernel(slot, own_count, first, *refs),
        out_shape=[jax.ShapeDtypeStruct(s, d) for s, d in outs],
        in_specs=[vm] * 6 + [smem] + [vm] * (4 + len(extra)), out_specs=[vm] * 6,
        input_output_aliases={} if first else {11: 3, 12: 4, 13: 5},
        scratch_shapes=[pltpu.VMEM((n, width), bf), pltpu.VMEM((n, hidden), bf), pltpu.VMEM((n, hidden), f32), pltpu.VMEM((n, width), f32)]
        + [pltpu.VMEM((n, width), f32), pltpu.VMEM((width, n), bf), pltpu.VMEM((width, n), bf), pltpu.VMEM((n, hidden), bf)],
        compiler_params=pltpu.CompilerParams(vmem_limit_bytes=VM_F * MIB),
        cost_estimate=pl.CostEstimate(flops=1_000_000, bytes_accessed=1000, transcendentals=0),
        name="feed",
    )(*args, *extra)


def scores_back(js, c, qa, k_ref, v_ref, doa, caug, dm, sums):
    width = k_ref.shape[1]
    step = 192 if c % 192 == 0 else c
    lane = lax.broadcasted_iota(jnp.int32, (step, 128), 1)
    ones = jnp.ones((step, 128), bf)
    def pair(j, carry):
        sl = columns(j, 128)
        k_t = k_ref[0:c, sl].T
        dqt = [None, None]
        dvsum = None
        for start in range(0, c, step):
            cs = slice(start, start + step)
            dvs, dks = [], []
            for e in range(2):
                hs = columns(2 * j + e, 128)
                own = (lane < 64) if e == 0 else (lane >= 64)
                kp = jnp.where(own, k_ref[cs, sl], caug[cs, :])
                vp = jnp.where(own, v_ref[cs, sl], ones)
                p = jnp.exp(mm_nt(kp, qa[0:c, hs]))
                ds = (p * mm_nt(vp, doa[0:c, hs])).astype(bf)
                dvs.append(mm(p.astype(bf), doa[0:c, hs]))
                dks.append(mm(ds, qa[0:c, hs]))
                t = mm(k_t[64 * e:64 * e + 64, cs], ds)
                dqt[e] = t if dqt[e] is None else dqt[e] + t
            dm[cs, columns(j, 128, width)] = jnp.where(lane < 64, dks[0], dks[1]).astype(bf)
            dv = jnp.where(lane < 64, dvs[0], dvs[1])
            dm[cs, columns(j, 128, 2 * width)] = dv.astype(bf)
            s = jnp.sum(dv, axis=0, keepdims=True)
            dvsum = s if dvsum is None else dvsum + s
        dq = jnp.concatenate(dqt, axis=0).T * 0.125
        dm[0:c, sl] = dq.astype(bf)
        sums[0:1, sl] = jnp.sum(dq, axis=0, keepdims=True)
        sums[1:2, sl] = dvsum
        return carry

    repeat(js[0], js[-1] + 1, pair, c < k_ref.shape[0])


def norm_back(c, slots, x_ref, gm, dm, vec_ref, wqkv, g_refs, nrm_ref):
    vec = lambda i: vec_ref[i:i + 1, :]
    gf = mm_nt(dm[0:c, :], wqkv[...])
    xh, r = normalise(x_ref[0:c, :].astype(f32))
    nrm_ref[0:c, :] = (xh * vec(0) + vec(1)).astype(bf)
    gg = gf * vec(0)
    gx = (gm[0:c, :] + r * (gg - row_mean(gg) - xh * row_mean(gg * xh))).astype(bf)
    for i, ref in enumerate(g_refs):
        ref[...] = mm_tn(mover(slots, i, c, ref.shape[0]), gx).astype(bf)
    return jnp.sum(gf * xh, axis=0, keepdims=True), jnp.sum(gf, axis=0, keepdims=True)


def start_kernel(slots, qa, k_ref, v_ref, doa, caug, dm, sums):
    sums[...] = jnp.zeros_like(sums)
    for_rows(
        kept_count(slots), k_ref.shape[0], lambda c: scores_back([0], c, qa, k_ref, v_ref, doa, caug, dm, sums))


def start_call(slots, *attn):
    n, width = attn[1].shape
    return small_call(start_kernel, (slots, *attn), [((n, 3 * width), bf), ((8, width), f32)], "start", VM_B)


def back_kernel(parts, started, *refs):
    slots, attn, (vec_ref, wqkv, x_ref, gm) = refs[0], refs[1:6], refs[6:10]
    refs = refs[10:]
    if started:
        dm0, sums0 = refs[:2]
        refs = refs[2:]
    dm, sums = refs[:2]
    n, width = gm.shape

    def body(c):
        pairs = range(width // 128)
        if started:
            sums[...] = sums0[...]
            for s in range(3):
                dm[0:c, width * s:width * s + 128] = dm0[0:c, width * s:width * s + 128]
            pairs = pairs[1:]
        else:
            sums[...] = jnp.zeros_like(sums)
        scores_back(pairs, c, *attn, dm, sums)
        if parts:
            gain, shift = norm_back(c, slots, x_ref, gm, dm, vec_ref, wqkv, refs[2:2 + parts], refs[-1])
            sums[2:3, :] = gain
            sums[3:4, :] = shift

    for_rows(kept_count(slots), n, body)


def back_call(slots, attn, rows, parts, vec, wqkv, x, gm, started=()):
    n, width = attn[1].shape
    outs = [((n, 3 * width), bf), ((8, width), f32)]
    if parts:
        outs += [((rows, width), bf)] * parts + [((n, width), bf)]
    return small_call(
        lambda *refs: back_kernel(parts, len(started) > 0, *refs),
        (slots, *attn, vec, wqkv, x, gm, *started), outs, "back", VM_B)


def last_kernel(parts, own, *refs):
    x_ref, gm, vec_ref, wqkv, dwo = refs[:5]
    refs = refs[5:]
    slots, dms, sums, nrms = refs[:own], refs[own:2 * own], refs[2 * own:3 * own], list(refs[3 * own:4 * own - 1])
    packed, sm, g_refs, nrm_s = refs[4 * own - 1], refs[4 * own], refs[4 * own + 1:-1], refs[-1]
    n, width = gm.shape
    nrms.append(nrm_s)
    total = sum(ref[0:4, :] for ref in sums)
    sm[...] = jnp.zeros_like(sm)
    sm[2:4, :] = total[0:2, :]

    def finish(c):
        gain, shift = norm_back(c, slots[-1], x_ref, gm, dms[-1], vec_ref, wqkv, g_refs, nrm_s)
        sm[0:1, :] = total[2:3, :] + gain
        sm[1:2, :] = total[3:4, :] + shift

    for_rows(kept_count(slots[-1]), n, finish)
    for i in range(own):

        def add(c, i=i):
            nrm_t = nrms[i][0:c, :].T

            def block(s, carry):
                js = columns(s, width)
                value = mm(nrm_t, dms[i][0:c, js])
                packed[js, :] = value if i == 0 else packed[js, :] + value
                return carry

            repeat(0, 3, block, c < n)

        for_rows(kept_count(slots[i]), n, add)
    packed[3 * width:4 * width, :] = dwo[...]
    if packed.shape[0] > 4 * width:
        packed[4 * width:, :] = jnp.zeros((packed.shape[0] - 4 * width, width), f32)


def last_call(packed_rows, rows, parts, x, gm, vec, wqkv, slots, dms, sums, nrms, dwo):
    own = len(dms)
    n, width = gm.shape
    outs = [((packed_rows, width), f32), ((16, width), f32)] + [((rows, width), bf)] * parts
    return small_call(
        lambda *refs: last_kernel(parts, own, *refs), (x, gm, vec, wqkv, dwo, *slots, *dms, *sums, *nrms), outs, "last",
        VM_W, scratch=[pltpu.VMEM((n, width), bf)])


def aligned(start, rows):
    return pl.ds(pl.multiple_of(start, 16), rows)


def tree_sum(parts):
    while len(parts) > 1:
        parts = [parts[i] + parts[i + 1] for i in range(0, len(parts), 2)]
    return parts[0]


def store_small(ref, at, small):
    rows = small.shape[0]
    high = small.astype(bf)
    ref[at:at + rows, :] = high
    ref[at + rows:at + 2 * rows, :] = (small - high.astype(f32)).astype(bf)


def load_small(ref, at, rows):
    return ref[at:at + rows, :].astype(f32) + ref[at + rows:at + 2 * rows, :].astype(f32)


def rounded(small):
    high, low = split2(small)
    return high.astype(f32) + low.astype(f32)


def core_kernel(big, small, out):
    half = big.shape[0] // 2
    other = 1 - (lax.axis_index("dp") & 1)
    out[0:half, :] = big[aligned(other * half, half), :].astype(bf)
    store_small(out, half, small[...])


def core_call(big, small):
    rows, width = big.shape
    return small_call(core_kernel, (big, small), [((rows // 2 + 2 * small.shape[0], width), bf)], "core", 4)[0]


def plane_kernel(big, small, got, *outs):
    sends, keep, total = outs[:-2], outs[-2], outs[-1]
    half, rows = big.shape[0] // 2, keep.shape[0]
    dp = lax.axis_index("dp")
    base, mine = (dp & 1) * half, dp >> 1
    summed = rounded(small[...]) + load_small(got, half, small.shape[0])
    total[...] = summed
    for k in range(len(sends) + 1):
        at = (mine ^ k) * rows
        value = big[aligned(base + at, rows), :] + got[aligned(at, rows), :].astype(f32)
        if k == 0:
            keep[...] = value
        else:
            sends[k - 1][0:rows, :] = value.astype(bf)
            store_small(sends[k - 1], rows, summed)


def plane_call(big, small, got, count):
    width, s = big.shape[1], small.shape[0]
    rows = big.shape[0] // 2 // count
    outs = [((rows + 2 * s, width), bf)] * (count - 1) + [((rows, width), f32), ((s, width), f32)]
    o = small_call(plane_kernel, (big, small, got), outs, "plane", 4)
    return o[:count - 1], o[-2], o[-1]


def halve_kernel(shift, count, rider, *refs):
    kept, small, gots, riding = refs[0], refs[1], refs[2:2 + count], refs[2 + count:2 + count + rider]
    send, keep, total = refs[2 + count + rider:]
    whole, rows, s = kept.shape[0], keep.shape[0], small.shape[0]
    mine = (lax.axis_index("seq") >> shift) & 1
    summed = tree_sum([rounded(small[...])] + [load_small(got, whole, s) for got in gots])
    total[...] = summed
    for k in range(2):
        at = (mine ^ k) * rows
        value = tree_sum([kept[aligned(at, rows), :]] + [got[aligned(at, rows), :].astype(f32) for got in gots])
        if k == 0:
            keep[...] = value
        else:
            send[0:rows, :] = value.astype(bf)
    store_small(send, rows, summed)
    at = rows + 2 * s
    for ref in riding:
        send[at:at + ref.shape[0], :] = ref[...]
        at += ref.shape[0]


def halve_call(kept, small, gots, shift, riders=()):
    width, s = kept.shape[1], small.shape[0]
    rows = kept.shape[0] // 2
    outs = [((rows + 2 * s + sum(x.shape[0] for x in riders), width), bf), ((rows, width), f32), ((s, width), f32)]
    return small_call(
        lambda *refs: halve_kernel(shift, len(gots), len(riders), *refs),
        (kept, small, *gots, *riders), outs, "halve", 6)


def spread_kernel(learns, rider, *refs):
    kept, small, got = refs[:3]
    learnt, riding = refs[3:3 + learns], refs[3 + learns:3 + learns + rider]
    total, part = refs[3 + learns + rider:]
    rows, s = kept.shape[0], small.shape[0]
    total[...] = rounded(small[...]) + load_small(got, rows, s)
    part[0:rows, :] = (kept[...] + got[0:rows, :].astype(f32)).astype(bf)
    at = rows
    if learns:
        used = sum(ref.shape[0] for ref in learnt)
        blank = [jnp.zeros((-used % 16, kept.shape[1]), f32)] if used % 16 else []
        learnt = jnp.concatenate([ref[...] for ref in learnt] + blank, axis=0)
        part[rows:rows + learnt.shape[0], :] = learnt.astype(bf)
        at += learnt.shape[0]
    for ref in riding:
        part[at:at + ref.shape[0], :] = ref[...]
        at += ref.shape[0]


def learned_rows(learns):
    used = sum(ref.shape[0] for ref in learns)
    return used + -used % 16


def spread_call(kept, small, got, learns=(), riders=()):
    rows, width = kept.shape
    rows += learned_rows(learns) + sum(ref.shape[0] for ref in riders)
    outs = [(small.shape, f32), ((rows, width), bf)]
    total, part = small_call(
        lambda *refs: spread_kernel(len(learns), len(riders), *refs), (kept, small, got, *learns, *riders), outs, "spread", 6)
    return part, total


def join_kernel(axis, shift, rows, riding, count, extra, *refs):
    parts, extras, out = refs[:count], refs[count:count + extra], refs[count + extra]
    mine = (lax.axis_index(axis) >> shift) & (count - 1)
    for k, part in enumerate(parts):
        out[aligned((mine ^ k) * rows, rows), :] = part[0:rows, :]
        if riding:
            out[aligned(count * rows + (mine ^ k) * riding, riding), :] = part[rows:rows + riding, :]
    at = count * (rows + riding)
    for ref in extras:
        out[at:at + ref.shape[0], :] = ref[...]
        at += ref.shape[0]


def join_call(parts, axis, shift, rows, riding=0, extras=()):
    width = parts[0].shape[1]
    total = (rows + riding) * len(parts) + sum(x.shape[0] for x in extras)
    return small_call(
        lambda *refs: join_kernel(axis, shift, rows, riding, len(parts), len(extras), *refs), (*parts, *extras),
        [((total, width), bf)], "join", 6)[0]


def first_kernel(x, out):
    out[...] = x[0:out.shape[0], :]


def first_rows(x, rows):
    return small_call(first_kernel, (x,), [((rows, x.shape[1]), x.dtype)], "first", 4)[0]


def small_call(kernel, args, outs, name, mib, scratch=()):
    vm = pl.BlockSpec(memory_space=pltpu.VMEM)
    return pl.pallas_call(
        kernel,
        out_shape=[jax.ShapeDtypeStruct(s, d) for s, d in outs],
        in_specs=[vm] * len(args), out_specs=[vm] * len(outs), scratch_shapes=list(scratch),
        compiler_params=pltpu.CompilerParams(vmem_limit_bytes=mib * MIB),
        cost_estimate=pl.CostEstimate(flops=1_000_000, bytes_accessed=1000, transcendentals=0),
        name=name,
    )(*args)


def prepare_kernel(own, rows, depth, patches, keep, valid, count, *refs):
    blocks, (keep_s, sems) = refs[:2 * depth], refs[2 * depth:]
    width = patches.shape[2]
    me = lax.axis_index("seq")
    flags_copy = pltpu.make_async_copy(keep, keep_s, sems.at[depth * own])
    flags_copy.start()
    copies = []
    for k in [k for k in range(1, depth)] + [0]:
        for i in range(own):
            target = blocks[2 * k].at[0:rows, :] if i == 0 else blocks[2 * k + 1].at[rows * (i - 1):rows * i, :]
            copies.append(pltpu.make_async_copy(patches.at[(me ^ k) * own + i], target, sems.at[k * own + i]))
            copies[-1].start()
    total = valid[0]
    for i in range(1, valid.shape[0]):
        total = total + valid[i]
    count[...] = jnp.full(count.shape, total.astype(f32), f32)
    flags_copy.wait()
    line = lax.broadcasted_iota(jnp.int32, (16, rows), 0)
    for k in range(depth):
        flags = jnp.zeros((16, rows), f32)
        for i in range(own):
            flags = jnp.where(line == i, keep_s[pl.ds((me ^ k) * own + i, 1), :].astype(f32), flags)
        blocks[2 * k][rows:rows + 16, :] = jnp.zeros((16, width), bf)
        blocks[2 * k][rows:rows + 16, 0:rows] = flags.astype(bf)
    for copy in copies:
        copy.wait()


def prepare_call(depth, patches, keep, valid):
    images, rows, width = patches.shape
    own = images // depth
    vm, hbm = pl.BlockSpec(memory_space=pltpu.VMEM), pl.BlockSpec(memory_space=pltpu.HBM)
    outs = [((8, 128), f32)]
    for k in range(depth):
        outs += [((rows + 16, width), bf), ((rows * (own - 1), width), bf)]
    o = pl.pallas_call(
        lambda *refs: prepare_kernel(own, rows, depth, *refs),
        out_shape=[jax.ShapeDtypeStruct(s, d) for s, d in outs],
        in_specs=[hbm, hbm, pl.BlockSpec(memory_space=pltpu.SMEM)], out_specs=[vm] * len(outs),
        scratch_shapes=[pltpu.VMEM(keep.shape, keep.dtype), pltpu.SemaphoreType.DMA((depth * own + 1,))],
        compiler_params=pltpu.CompilerParams(vmem_limit_bytes=8 * MIB),
        cost_estimate=pl.CostEstimate(flops=1_000_000, bytes_accessed=1000, transcendentals=0),
        name="prepare",
    )(in_hbm(patches), in_hbm(keep), valid)
    return o[0], o[1::2], o[2::2]


def vectors_kernel(own, mapw, cot, *refs):
    half = (len(refs) - 4) // 2
    sources, vec, mb, cm, held, sems = refs[:half], refs[half], refs[half + 1], refs[half + 2], refs[half + 3:-1], refs[-1]
    copies = [pltpu.make_async_copy(a, b, sems.at[i]) for i, (a, b) in enumerate(zip(sources, held))]
    for copy in copies:
        copy.start()
    vec[...] = jnp.zeros_like(vec)
    me = lax.axis_index("seq")
    for i in range(own):
        cm[i] = jnp.concatenate([mapw[...].astype(f32), cot[me * own + i].astype(f32)], axis=0).astype(bf)
    for copy in copies:
        copy.wait()
    width, tokens = vec.shape[1], mb.shape[0]
    line = 0
    for ref in held[:-1]:
        for j in range(ref.shape[0] // width):
            vec[line, :] = ref[width * j:width * (j + 1)].astype(f32)
            line += 1
    bias = jnp.broadcast_to(held[-1][...].astype(f32).reshape(1, tokens), (tokens, tokens))
    diag = lax.broadcasted_iota(jnp.int32, (tokens, tokens), 0) == lax.broadcasted_iota(jnp.int32, (tokens, tokens), 1)
    mb[...] = jnp.broadcast_to(jnp.sum(jnp.where(diag, bias, 0.0), axis=1, keepdims=True), mb.shape)


def vectors_call(own, mapw, cot, *sources):
    width, tokens = sources[0].shape[0], sources[-1].shape[0]
    vm, hbm = pl.BlockSpec(memory_space=pltpu.VMEM), pl.BlockSpec(memory_space=pltpu.HBM)
    outs = [((16, width), f32), ((tokens, 128), f32), ((own, 2 * tokens, width), bf)]
    return pl.pallas_call(
        lambda *refs: vectors_kernel(own, *refs),
        out_shape=[jax.ShapeDtypeStruct(s, d) for s, d in outs],
        in_specs=[vm] * 2 + [hbm] * len(sources), out_specs=[vm] * 3,
        scratch_shapes=[pltpu.VMEM(s.shape, s.dtype) for s in sources] + [pltpu.SemaphoreType.DMA((len(sources),))],
        compiler_params=pltpu.CompilerParams(vmem_limit_bytes=4 * MIB),
        cost_estimate=pl.CostEstimate(flops=1_000_000, bytes_accessed=1000, transcendentals=0),
        name="vectors",
    )(mapw, cot, *map(in_hbm, sources))


def plus_kernel(a, b, out):
    out[...] = a[...] + b[...]


def unpack_kernel(hidden, own, base, a0, a1, sm_ref, rider, count_ref, gdn, gup, down, outb, gain, shift, upb, mapw, mapb, learned, penalty, a_s):
    side = lax.axis_index("dp") & 1
    half, width = a0.shape
    a_s[pl.ds(pl.multiple_of(side * half, 16), half), :] = a0[...]
    a_s[pl.ds(pl.multiple_of((1 - side) * half, 16), half), :] = a1[...]
    blocks = hidden // width
    for j in range(blocks):
        js = slice(width * j, width * (j + 1))
        gdn[js, :] = a_s[js, :].T.astype(f32)
        gup[:, js] = a_s[width * (blocks + j):width * (blocks + j + 1), :].astype(f32)
    for i, ref in enumerate((down, outb, gain, shift)):
        ref[...] = sm_ref[i, :]
    for j in range(blocks):
        upb[width * j:width * (j + 1)] = sm_ref[4 + j, :]
    mapw[...] = sm_ref[8:16, :]
    tokens = learned.shape[1]
    penalty[...] = sm_ref[16:17, tokens:tokens + 1] / count_ref[0:1, 0:1]
    mapb[...] = sm_ref[16, 0:tokens]
    count = own * tokens
    depth = learned.shape[0] // own
    bits = depth.bit_length() - 1
    for z in range(depth):
        place = sum(((z >> b) & 1) << (bits - 1 - b) for b in range(bits))
        span = count + -count % 16
        at = base + span * place
        both = rider[at:at + span, :].astype(f32)
        for i in range(own):
            learned[z * own + i] = both[tokens * i:tokens * (i + 1), :]


def unpack_call(hidden, tokens, images, own, base, a0, a1, sm, rider, count):
    width = a0.shape[1]
    vm = pl.BlockSpec(memory_space=pltpu.VMEM)
    outs = [(hidden, width), (width, hidden)] + [(width,)] * 4 + [(hidden,), (tokens, width), (tokens,)]
    outs += [(images, tokens, width), (1, 1)]
    return pl.pallas_call(
        lambda *refs: unpack_kernel(hidden, own, base, *refs),
        out_shape=[jax.ShapeDtypeStruct(s, f32) for s in outs],
        in_specs=[vm] * 5, out_specs=[vm] * len(outs),
        scratch_shapes=[pltpu.VMEM((2 * a0.shape[0], width), bf)],
        compiler_params=pltpu.CompilerParams(vmem_limit_bytes=16 * MIB),
        cost_estimate=pl.CostEstimate(flops=1_000_000, bytes_accessed=1000, transcendentals=0),
        name="unpack",
    )(a0, a1, sm, rider, count)


def finish_kernel(b0, b1, sm_ref, gqkv, gout, gain, shift, biases, b_s):
    side = lax.axis_index("dp") & 1
    half, width = b0.shape
    b_s[pl.ds(pl.multiple_of(side * half, 16), half), :] = b0[...]
    b_s[pl.ds(pl.multiple_of((1 - side) * half, 16), half), :] = b1[...]
    for j in range(3):
        js = slice(width * j, width * (j + 1))
        gqkv[:, js] = b_s[js, :].astype(f32)
    gout[...] = b_s[3 * width:4 * width, :].astype(f32)
    gain[...] = sm_ref[0, :]
    shift[...] = sm_ref[1, :]
    for j in range(2):
        biases[width * j:width * (j + 1)] = sm_ref[2 + j, :]


def finish_call(b0, b1, sm):
    width = b0.shape[1]
    vm = pl.BlockSpec(memory_space=pltpu.VMEM)
    outs = [(width, 3 * width), (width, width), (width,), (width,), (2 * width,)]
    return pl.pallas_call(
        finish_kernel,
        out_shape=[jax.ShapeDtypeStruct(s, f32) for s in outs],
        in_specs=[vm] * 3, out_specs=[vm] * len(outs),
        scratch_shapes=[pltpu.VMEM((2 * b0.shape[0], width), bf)],
        compiler_params=pltpu.CompilerParams(vmem_limit_bytes=8 * MIB),
        cost_estimate=pl.CostEstimate(flops=1_000_000, bytes_accessed=1000, transcendentals=0),
        name="finish",
    )(b0, b1, sm)


def place_kernel(parts, bases, *refs):
    out = refs[-1]
    own, rows = len(bases) // parts, out.shape[1]
    me = lax.axis_index("seq")
    for i in range(own):
        for k in range(parts):
            base = bases[i * parts + k]
            out[(me ^ k) * own + i] = refs[i * parts + k][base:base + rows, :].astype(f32)


def place_call(sent, rows):
    own, parts = len(sent), len(sent[0])
    width = sent[0][0][0].shape[1]
    bases = [base for image in sent for _, base in image]
    return small_call(
        lambda *refs: place_kernel(parts, bases, *refs), [x for image in sent for x, _ in image],
        [((parts * own, rows, width), f32)], "place", 8)[0]


VM_A, VM_F, VM_B, VM_W = 12, 26, 14, 14


def xor_permute(x, axis, k):
    return lax.ppermute(x, axis, [(i, i ^ k) for i in range(lax.axis_size(axis))])


def after(x, *others):
    if not others:
        return x
    return lax.optimization_barrier((x,) + others)[0]


def plane_exchange(sends):
    return [xor_permute(x, "dp", (k + 1) << 1) for k, x in enumerate(sends)]


def to_peers(part, axis, count, shift):
    return [part] + [xor_permute(part, axis, k << shift) for k in range(1, count)]


def padded(rows, unit):
    return rows + -rows % unit


def per_device(
    patches, first_gain, first_shift, qkv_weight, query_value_bias, out_weight, out_bias,
    second_gain, second_shift, up_weight, up_bias, down_weight, down_bias, map_weight, map_bias,
    keep_mask, image_valid, token_cotangent,
):
    images, rows, width = patches.shape
    depth, dps = lax.axis_size("seq"), lax.axis_size("dp")
    chips = dps // 2
    own = images // depth
    hidden, tokens = up_weight.shape[1], map_weight.shape[1]
    pairs = width // 128
    unit = 16 * dps * depth
    rows_a, rows_b = padded(2 * hidden, unit), padded(4 * width, unit)

    count, first_blocks, rest_blocks = prepare_call(depth, patches, keep_mask, image_valid)
    order = sorted(range(1, depth), key=lambda k: (k == 1, k))

    def collect(blocks, holds):
        got = [blocks[0]] + [None] * (depth - 1)
        for k in order:
            got[k] = xor_permute(after(blocks[k], *holds), "seq", k)
        return got

    first = collect(first_blocks, [])
    vec, mb, cm = vectors_call(
        own, map_weight.T, token_cotangent, first_gain, first_shift, query_value_bias, out_bias, second_gain,
        second_shift, down_bias, up_bias, map_bias)
    plus = lambda a, b: small_call(plus_kernel, (a, b), [((8, 128), f32)], "plus", 1)[0]
    step, holds = 1, list(first[1:])
    while step < dps:
        if step == 2:
            count = after(count, vec)
        if step == dps // 2:
            holds.append(count)
            count_got = xor_permute(count, "dp", step)
        else:
            count = plus(count, xor_permute(count, "dp", step))
        step *= 2
    rest = collect(rest_blocks, holds)

    saved, learns = [], []
    bases = [0] + [rows * i for i in range(own - 1)]
    acc = dwo = sm = tok = None
    for i in range(own):
        v = vec if tok is None else after(vec, tok)
        qa, key, val, caug, att, mid, x, slots = attend_call(
            first if i == 0 else rest, first, i, bases[i], rows, v, qkv_weight, out_weight)
        if i == 0:
            count = plus(after(count, caug), count_got)
        gm, doa, learn, acc, dwo, sm = feed_call(
            i, own, rows_a, mid, att, slots, vec, mb, cm, image_valid, count,
            out_weight, up_weight, down_weight, acc, dwo, sm)
        tok = sm
        saved.append((qa, key, val, doa, caug, gm, x, slots))
        learns.append(learn)

    got = xor_permute(core_call(acc, sm), "dp", 1)
    bits = depth.bit_length() - 1
    dms, sums, nrms, sent = [], [], [], []
    for i in range(own):
        qa, key, val, doa, caug, gm, x, slots = saved[i]
        started = ()
        if i == 0:
            started = start_call(slots, qa, key, val, doa, after(caug, tok))
            sends, kept, small = plane_call(acc, after(sm, started[1]), got, chips)
            gots = plane_exchange(sends)
            tok = small
        o = back_call(
            slots, (qa, key, val, doa, after(caug, tok)), rows, depth if i < own - 1 else 0, vec, qkv_weight, x, gm, started)
        dms.append(o[0])
        sums.append(o[1])
        tok = o[1]
        leaving = o[2:2 + depth]
        if i < own - 1:
            nrms.append(o[-1])
        if i == own - 2:
            riders = [s[1][0] for s in sent]
            send, kept, small = halve_call(
                kept, after(small, tok, *[x for s in sent for x, _ in s[2:]]), gots, 0, riders)
            got = xor_permute(send, "seq", 1)
            base = kept.shape[0] + 2 * small.shape[0]
            for m, s in enumerate(sent):
                s[1] = (got, base + rows * m)
            tok = small
        if i < own - 1:
            far = [(xor_permute(x, "seq", k), 0) for k, x in enumerate(leaving) if k > 1]
            sent.append([(leaving[0], 0), (leaving[1], 0)] + far)
    for bit in range(1, bits):
        send, kept, small = halve_call(kept, after(small, tok), [got], bit)
        got = xor_permute(send, "seq", 1 << bit)
        tok = small
    o = last_call(
        rows_b, rows, depth, saved[-1][6], saved[-1][5], after(vec, tok), qkv_weight, [s[7] for s in saved], dms, sums,
        nrms, dwo)
    bigb, smb, tail = o[0], o[1], o[2:]
    early = [x for x, _ in sent[-1][2:]]
    part, small = spread_call(kept, small, got, learns)
    gotb = xor_permute(core_call(bigb, after(smb, small)), "dp", 1)
    size, riding = kept.shape[0], learned_rows(learns)
    got = xor_permute(part, "seq", depth // 2)
    sends, keptb, smallb = plane_call(bigb, smb, gotb, chips)
    gotsb = plane_exchange(sends)
    smallb = after(smallb, *early)
    steps = list(reversed(range(bits)))
    for m, bit in enumerate(steps):
        send, keptb, smallb = halve_call(keptb, smallb, gotsb, bit, [] if bit else [sent[-1][1][0]])
        gotsb = [xor_permute(send, "seq", 1 << bit)]
        if bit == 0:
            sent[-1][1] = (gotsb[0], keptb.shape[0] + 2 * smallb.shape[0])
        part = join_call([after(part, smallb), got], "seq", bit, size, riding)
        size, riding = 2 * size, 2 * riding
        if bit:
            got = xor_permute(part, "seq", 1 << (bit - 1))
    rider = part
    peers = to_peers(first_rows(part, size), "dp", chips, 1)
    late = [tail[0]] + [xor_permute(after(x, smallb), "seq", k) for k, x in enumerate(tail) if k and k % 2 == 0]
    piece = keptb.shape[0]
    partb, smallb = spread_call(keptb, smallb, gotsb[0], (), [tail[1]])
    odd = [xor_permute(after(x, smallb), "seq", k) for k, x in enumerate(tail) if k % 2 and k > 1]
    for bit in range(bits):
        other = xor_permute(partb, "seq", 1 << bit)
        if bit == 0:
            nearest = (other, piece)
        partb = join_call([after(partb, *(late[1:] if bit == 0 else odd)), other], "seq", bit, piece << bit)
    sent.append([(tail[0], 0), nearest] + [
        (late[k // 2] if k % 2 == 0 else odd[k // 2 - 1], 0) for k in range(2, depth)])
    outs = place_call(sent, rows)
    part = join_call([after(peers[0], partb)] + peers[1:], "dp", 1, size)
    a0, a1 = part, xor_permute(part, "dp", 1)
    unpacked = unpack_call(hidden, tokens, images, own, size, a0, a1, small, rider, count)
    gdn, gup, gb_down, gb_out, g_gain2, g_shift2, gb_up, gmapw, gmapb, learned, penalty = unpacked
    peers = to_peers(partb, "dp", chips, 1)
    partb = join_call([after(peers[0], gmapw, outs)] + peers[1:], "dp", 1, partb.shape[0])
    b0, b1 = partb, xor_permute(partb, "dp", 1)
    gqkv, gout, g_gain1, g_shift1, gqv = finish_call(b0, b1, smallb)
    return (
        learned, penalty.reshape(()), outs, g_gain1, g_shift1, gqkv, gqv, gout, gb_out, g_gain2, g_shift2, gup,
        gb_up, gdn, gb_down, gmapw.T, gmapb,
    )


def solution(mesh):
    rep = P()
    placed = (P("dp", "seq", None),) + (rep,) * 14 + (P("dp", "seq"), P("dp"), P("dp", None, None))
    return jax.shard_map(
        per_device, mesh=mesh, in_specs=placed,
        out_specs=(P("dp", None, None), rep, P("dp", "seq", None)) + (rep,) * 14,
        check_vma=False,
    )
```
